128 devices in a mesh: pat: 8 (over y, core), tile: 16 (over z, x).
Axes of the slice: x: 4, y: 4, z: 4, core: 2. Of those that a mesh axis runs over, the one named last changes fastest.
Arguments:
- intensity: float32 [128, 256, 256], P(('pat', 'tile')), may hold values from 0.25 to 36, as said below
- positions: int32 [128, 2], P(('pat', 'tile')), may hold values from 0 to 3840, as said below
- object_init: float32 [2, 4096, 1024], P(None, 'tile'), may hold values from -4 to 4
- probe_init: float32 [4, 2, 256, 256], replicated, may hold values from -3 to 3
Outputs:
- object_out: float32 [2, 4096, 1024], P(None, 'tile')
- probe_out: float32 [4, 2, 256, 256], replicated
The draws below stay inside these ranges and needn't reach their ends.
Inputs may be any that keep to these rules, and one draw needn't show every extreme that they name: positions[i, 0] is pattern i's first object row and positions[i, 1] its first object column; every patch of 256 x 256 pixels lies inside the object, and pattern i's first row lies within 128 rows of ((i) % 16) * 256. `intensity`: positive measured intensities.
All inputs are finite; a program needn't handle non-finite values.
Results may differ from the reference program's by a relative error of at most 0.0001.
Values sent between devices are 32-bit elements; how exact they have to be, the bound alone decides.
No kernel may reach another device: no remote copies, remote signals or barrier semaphores. Data moves between devices by JAX's collectives and lax.ppermute only.
A program may use at most 128 MiB of HBM per device.

```python
import math
import jax
import jax.numpy as jnp
from jax import lax

PATCH = 256
MODES = 4
HALO = 128
TILE_ROWS = 256
OBJ_W = 1024
PAT_DEV = 1
ITERS = 2
TILES = 16
OBJ_H = 4096
PATTERNS = 128


def draw_positions(key, part):
    key = jax.random.fold_in(key, 11)
    row_key, col_key = jax.random.split(key)
    indices = jnp.arange(PATTERNS, dtype=jnp.int32)
    owners = indices // PAT_DEV % TILES
    jitter = jax.random.randint(row_key, (PATTERNS,), -HALO, HALO + 1, dtype=jnp.int32)
    row_offsets = jnp.clip(owners * TILE_ROWS + jitter, 0, OBJ_H - PATCH)
    column_offsets = jax.random.randint(col_key, (PATTERNS,), 0, OBJ_W - PATCH + 1, dtype=jnp.int32)
    row_offsets = row_offsets.at[0].set(0).at[PATTERNS - 1].set(OBJ_H - PATCH)
    column_offsets = column_offsets.at[0].set(0).at[PATTERNS - 1].set(OBJ_W - PATCH)
    return jnp.stack([row_offsets, column_offsets], axis=1).astype(jnp.int32)


def draw_intensity(key, part):
    key = jax.random.fold_in(key, 23)
    indices = jnp.arange(PATTERNS, dtype=jnp.float32) / max(PATTERNS - 1, 1)
    base_draw = jnp.exp(jax.random.uniform(key, (PATTERNS, PATCH, PATCH), jnp.float32, math.log(0.25), math.log(4.0)))
    ramp_factor = 1.0 + 8.0 * indices
    return (base_draw * ramp_factor[:, None, None]).astype(jnp.float32)


def steps_of(stream_key, shape, shards, least, largest):
    def one(axis_at, blocks):
        heights = jax.random.uniform(jax.random.fold_in(jax.random.fold_in(stream_key, 6), axis_at), (blocks,), jnp.float32, least / len(shards), largest / len(shards))
        return jnp.repeat(jnp.exp(heights), shape[axis_at] // blocks).reshape((-1,) + (1,) * (len(shape) - axis_at - 1))

    loudness = one(*shards[0])
    for cut in shards[1:]:
        loudness = loudness * one(*cut)
    return loudness


def normal_values(key, extent, scale, reach, pieces=(), held_as=jnp.bfloat16):
    values = jax.random.normal(key, extent, jnp.float32) * scale
    if len(pieces) > 0:
        values = steps_of(key, extent, pieces, -0.22, 0.18) * values
    return jnp.clip(values, min=-reach, max=reach).astype(held_as)


def setup_inputs(seed: int = 0) -> dict:
    keys = jax.random.split(jax.random.key(seed), 5)
    return {
        "intensity": draw_intensity(jax.random.fold_in(keys[4], 71), 0),
        "positions": draw_positions(jax.random.fold_in(keys[4], 71), 0),
        "object_init": normal_values(keys[2], (2, OBJ_H, OBJ_W), 0.7, 4.0, ((1, 16),), jnp.float32),
        "probe_init": normal_values(keys[3], (MODES, 2, PATCH, PATCH), 0.5, 3.0, (), jnp.float32),
    }


FLOOR = 0.5
RIDGE = 1.0

def patch_from(field, row, column):
    return lax.dynamic_slice(field, (row, column), (PATCH, PATCH))

def place_into(field, addend, row, column):
    current = lax.dynamic_slice(field, (row, column), (PATCH, PATCH))
    return lax.dynamic_update_slice(field, current + addend, (row, column))

def correction(object_now, probe_now, measured, position):
    patch_now = patch_from(object_now, position[0], position[1])
    far_field = jnp.fft.fft2(probe_now * patch_now, norm='ortho')
    modelled = lax.optimization_barrier(jnp.sum(far_field.real ** 2 + far_field.imag ** 2, axis=0))
    rescale = jnp.sqrt(measured / jnp.maximum(modelled, FLOOR))
    difference = jnp.fft.ifft2((rescale - 1.0) * far_field, norm='ortho')
    return (patch_now, difference)

def iterate(object_now, probe_now, intensity, positions):
    power = lax.optimization_barrier(jnp.sum(probe_now.real ** 2 + probe_now.imag ** 2, axis=0))

    def gather_terms(totals, element):
        grad_object, illum_object, grad_probe, illum_probe = totals
        measured, position = element
        patch_now, difference = correction(object_now, probe_now, measured, position)
        object_term = lax.optimization_barrier(jnp.sum(jnp.conj(probe_now) * difference, axis=0))
        grad_object = place_into(grad_object, object_term, position[0], position[1])
        illum_object = place_into(illum_object, power, position[0], position[1])
        grad_probe = grad_probe + jnp.conj(patch_now) * difference
        illum_probe = illum_probe + patch_now.real ** 2 + patch_now.imag ** 2
        return ((grad_object, illum_object, grad_probe, illum_probe), None)
    start = (jnp.zeros_like(object_now), jnp.zeros(object_now.shape, power.dtype), jnp.zeros_like(probe_now), jnp.zeros(power.shape, power.dtype))
    totals, ignored = lax.scan(gather_terms, start, (intensity, positions))
    grad_object, illum_object, grad_probe, illum_probe = totals
    dir_object = grad_object / (illum_object + RIDGE)
    dir_probe = grad_probe / (illum_probe + RIDGE)

    def step_terms(sums, element):
        measured, position = element
        patch_now, difference = correction(object_now, probe_now, measured, position)
        along_object = probe_now * patch_from(dir_object, position[0], position[1])
        along_probe = patch_now * dir_probe
        terms = jnp.stack([jnp.sum(along_object.real ** 2 + along_object.imag ** 2), jnp.sum(along_object.real * along_probe.real + along_object.imag * along_probe.imag), jnp.sum(along_probe.real ** 2 + along_probe.imag ** 2), jnp.sum(along_object.real * difference.real + along_object.imag * difference.imag), jnp.sum(along_probe.real * difference.real + along_probe.imag * difference.imag)])
        return (sums + terms, None)
    sums, ignored = lax.scan(step_terms, jnp.zeros((5,), power.dtype), (intensity, positions))
    object_power, cross_term, probe_power, object_pull, probe_pull = (sums[0], sums[1], sums[2], sums[3], sums[4])
    ridge_term = 0.1 * (object_power + probe_power) + 1e-06
    determinant = (object_power + ridge_term) * (probe_power + ridge_term) - cross_term ** 2
    object_step = ((probe_power + ridge_term) * object_pull - cross_term * probe_pull) / determinant
    probe_step = ((object_power + ridge_term) * probe_pull - cross_term * object_pull) / determinant
    return (object_now + object_step * dir_object, probe_now + probe_step * dir_probe)

def reference(intensity, positions, object_init, probe_init):
    object_now = object_init[0] + 1j * object_init[1]
    probe_now = probe_init[:, 0] + 1j * probe_init[:, 1]
    for iteration in range(ITERS):
        object_now, probe_now = iterate(object_now, probe_now, intensity, positions)
    object_out = jnp.stack([object_now.real, object_now.imag]).astype(jnp.float32)
    probe_out = jnp.stack([probe_now.real, probe_now.imag], axis=1).astype(jnp.float32)
    return (object_out, probe_out)
```

```python
import math

import jax
import jax.numpy as jnp
import ml_dtypes
import numpy as np
from jax import lax
from jax.experimental import pallas as pl
from jax.experimental.pallas import tpu as pltpu
from jax.sharding import PartitionSpec as P

ITERS = 2
FLOOR = 0.5
RIDGE = 1.0
N = 256
H = 128
F32 = jnp.float32
BF16 = jnp.bfloat16
BOTH = ("pat", "tile")
VMEM = pl.BlockSpec(memory_space=pltpu.VMEM)
SMEM = pl.BlockSpec(memory_space=pltpu.SMEM)


def real_tables():
    near = np.arange(H)[:, None]
    far = np.arange(H)[None, :]
    found = []
    for parity in range(2):
        angle = -2.0 * math.pi * ((near * (2 * far + parity)) % N) / N
        real, imag = np.cos(angle) / 16.0, np.sin(angle) / 16.0
        found.append(np.block([[real, imag], [-imag, real]]))
    even, odd = found
    out = []
    for table in (even, odd, even.T, odd.T):
        high = table.astype(np.float32).astype(ml_dtypes.bfloat16)
        low = (table - high.astype(np.float64)).astype(np.float32).astype(ml_dtypes.bfloat16)
        out.append(np.stack([high, low]))
    return np.stack(out)


def halves(value):
    high = value.astype(BF16)
    return high, (value - high.astype(F32)).astype(BF16)


def dot(left, right):
    return jnp.dot(left, right, preferred_element_type=F32)


def times_table(value, table):
    high, low = halves(value)
    return dot(high, table[0]) + (dot(low, table[0]) + dot(high, table[1]))


def table_times(table, value):
    high, low = halves(value)
    return dot(table[0], high) + (dot(table[0], low) + dot(table[1], high))


def patterns_kernel(first, *refs):
    if first:
        geo, patch, probe, measured, tab = refs[:5]
        keep, send, mine, other, psi, model, obj = refs[5:]
        patch_now, probe_now = patch, probe
    else:
        geo, steps, patch, probe, measured, tab, dirp, dprobe = refs[:8]
        patch_now, probe_now, keep, send, mine, other, psi, model, obj = refs[8:]
        for part in range(2):
            patch_now[part] = patch[part] + steps[0] * dirp[part]
    e0, y, c = geo[0], geo[1], geo[2]
    first_core = c == 0

    model[...] = jnp.zeros_like(model)
    obj[...] = jnp.zeros_like(obj)

    def gather(plane, value):
        obj[plane, 0] += value[:, :H]
        obj[plane, 1] += value[:, H:]

    def forward(k, carry):
        if not first:
            for part in range(2):
                probe_now[k, part] = probe[k, part] + steps[1] * dprobe[k, part]
        pr, pi = probe_now[k, 0], probe_now[k, 1]
        orr, oi = patch_now[0], patch_now[1]
        gather(2, pr * pr + pi * pi)
        xr = pr * orr - pi * oi
        xi = pr * oi + pi * orr
        even = times_table(
            jnp.concatenate([xr[:, :H] + xr[:, H:], xi[:, :H] + xi[:, H:]], axis=1), tab.at[0]
        )
        odd = times_table(
            jnp.concatenate([xr[:, :H] - xr[:, H:], xi[:, :H] - xi[:, H:]], axis=1), tab.at[1]
        )
        re = jnp.concatenate([even[:, :H], odd[:, :H]], axis=1)
        im = jnp.concatenate([even[:, H:], odd[:, H:]], axis=1)
        for row, sign in ((0, 1.0), (1, -1.0)):
            folded = jnp.concatenate(
                [re[:H] + sign * re[H:], im[:H] + sign * im[H:]], axis=0
            )
            far = table_times(tab.at[2 + row], folded)
            psi[k, row] = far
            model[row] += far[:H] * far[:H] + far[H:] * far[H:]
        return carry

    lax.fori_loop(0, 4, forward, 0)
    for row in range(2):
        model[row] = jnp.sqrt(measured[row] / jnp.maximum(model[row], FLOOR)) - 1.0

    def put(plane, value):
        low = value[:H].reshape(16, 8, N)
        high = value[H:].reshape(16, 8, N)
        keep[:, plane] = jnp.where(first_core, low, high)
        send[:, plane] = jnp.where(first_core, high, low)

    def backward(k, carry):
        parts = []
        for row in range(2):
            scale = model[row]
            weighted = psi[k, row] * jnp.concatenate([scale, scale], axis=0)
            parts.append(table_times(tab.at[row], weighted))
        ee, oo = parts
        re = jnp.concatenate([ee[:H] + oo[:H], ee[:H] - oo[:H]], axis=0)
        im = jnp.concatenate([ee[H:] + oo[H:], ee[H:] - oo[H:]], axis=0)
        even = times_table(jnp.concatenate([re[:, :H], im[:, :H]], axis=1), tab.at[2])
        odd = times_table(jnp.concatenate([re[:, H:], im[:, H:]], axis=1), tab.at[3])
        dr = jnp.concatenate([even[:, :H] + odd[:, :H], even[:, :H] - odd[:, :H]], axis=1)
        di = jnp.concatenate([even[:, H:] + odd[:, H:], even[:, H:] - odd[:, H:]], axis=1)
        pr, pi = probe_now[k, 0], probe_now[k, 1]
        orr, oi = patch_now[0], patch_now[1]
        gather(0, pr * dr + pi * di)
        gather(1, pr * di - pi * dr)
        put(2 * k, orr * dr + oi * di)
        put(2 * k + 1, orr * di - oi * dr)
        return carry

    lax.fori_loop(0, 4, backward, 0)
    orr, oi = patch_now[0], patch_now[1]
    put(8, orr * orr + oi * oi)
    for s in range(4):
        for which, dest in ((c, mine), (1 - c, other)):
            owner = 2 * lax.rem(y + s, 4) + which
            start = lax.rem(owner - e0 + 1024, 8)
            for plane in range(3):
                for half in range(2):
                    rows = obj[plane, half, pl.ds(start, 32, stride=8), :]
                    dest[s, plane, :, half * H : half * H + H] = rows


def place_of(geo, owner, pattern):
    e0 = geo[pattern]
    col = geo[8 + pattern]
    start = lax.rem(owner - e0 + 1024, 8)
    row = lax.shift_right_logical(e0 + start - owner, 3)
    block = lax.shift_right_logical(col, 7)
    base = pl.multiple_of(lax.shift_right_logical(row, 3) * 8, 8)
    return base, lax.rem(row, 8), pl.multiple_of(block * 128, 128), lax.rem(col, 128)


def place_kernel(geo, mine, part, b1, b2, b3, low, high, acc):
    y, c = geo[16], geo[17]
    owner = 2 * y + c
    acc[...] = jnp.zeros_like(acc)
    blank = jnp.zeros((32, 128), F32)
    under = jnp.zeros((8, 384), F32)
    for s in range(4):
        for which in range(2):
            pattern = 2 * lax.rem(y - s + 4, 4) + (c if which == 0 else 1 - c)
            row, turn, block, shift = place_of(geo, owner, pattern)
            for plane in range(3):
                if s == 0:
                    piece = (mine, part)[which][0, plane]
                else:
                    piece = (b1, b2, b3)[s - 1][which, plane]
                wide = pltpu.roll(jnp.concatenate([piece, blank], axis=1), shift, axis=1)
                wide = pltpu.roll(jnp.concatenate([wide, under], axis=0), turn, axis=0)
                acc[plane, pl.ds(row, 40), pl.ds(block, 384)] += wide
    low[...] = acc[:, :32, :1024]
    high[...] = acc[:, 32:64, :1024]


def direction_kernel(geo, low, high, above, below, band, sums, r0, r1, r2, r3, wide):
    y, c = geo[16], geo[17]
    owner = 2 * y + c
    wide[...] = jnp.zeros_like(wide)
    total_a = jnp.zeros((16, 1024), F32)
    total_n = jnp.zeros((16, 1024), F32)
    for at, (own, came) in enumerate(((low, above), (high, below))):
        illum = own[2] + came[2]
        scale = 1.0 / (illum + RIDGE)
        real = (own[0] + came[0]) * scale
        imag = (own[1] + came[1]) * scale
        rows = slice(32 * at, 32 * at + 32)
        wide[0, rows, :1024] = real
        wide[1, rows, :1024] = imag
        inner = slice(16, 32) if at == 0 else slice(0, 16)
        real, imag, illum = real[inner], imag[inner], illum[inner]
        band[0, 16 * at : 16 * at + 16] = real
        band[1, 16 * at : 16 * at + 16] = imag
        size = real * real + imag * imag
        total_n += size
        total_a += illum * size
    sums[0, 0] = jnp.sum(total_a)
    sums[0, 1] = jnp.sum(total_n)
    for s, dest in enumerate((r0, r1, r2, r3)):
        for which in range(2):
            pattern = 2 * lax.rem(y + s, 4) + (c if which == 0 else 1 - c)
            row, turn, block, shift = place_of(geo, owner, pattern)
            for part in range(2):
                piece = wide[part, pl.ds(row, 40), pl.ds(block, 384)]
                piece = pltpu.roll(piece, lax.rem(40 - turn, 40), axis=0)[:32]
                dest[which, part] = pltpu.roll(piece, lax.rem(384 - shift, 384), axis=1)[:, :N]


def cross_kernel(geo, r0, r1, r2, r3, oth, dmine, doth, patch, probe, dirp, dprobe, sums, rows):
    y, c = geo[16], geo[17]
    e0 = geo[2 * y + c]
    for s in range(4):
        for which in range(2):
            owner = 2 * lax.rem(y - s + 4, 4) + (c if which == 0 else 1 - c)
            start = lax.rem(owner - e0 + 1024, 8)
            for part in range(2):
                if which == 0:
                    piece = (r0, r1, r2, r3)[s][0, part]
                else:
                    piece = oth[s, part]
                for half in range(2):
                    at = pl.ds(start, 32, stride=8)
                    rows[part, half, at, :] = piece[:, half * H : half * H + H]
    for part in range(2):
        for half in range(2):
            dirp[part, :, half * H : half * H + H] = rows[part, half]
    first_core = c == 0
    s_real = jnp.zeros((N, N), F32)
    s_imag = jnp.zeros((N, N), F32)
    for k in range(4):
        pair = []
        for part in range(2):
            own = dmine[:, 2 * k + part].reshape(H, N)
            far = doth[:, 2 * k + part].reshape(H, N)
            value = jnp.concatenate(
                [jnp.where(first_core, own, far), jnp.where(first_core, far, own)], axis=0
            )
            dprobe[k, part] = value
            pair.append(value)
        pr, pi = probe[k, 0], probe[k, 1]
        s_real += pr * pair[0] + pi * pair[1]
        s_imag += pr * pair[1] - pi * pair[0]
    t_real = dirp[0] * patch[0] + dirp[1] * patch[1]
    t_imag = dirp[0] * patch[1] - dirp[1] * patch[0]
    sums[0, 0] = jnp.sum(t_real * s_real - t_imag * s_imag)


def finish_kernel(geo, steps1, steps2, field, probe, dprobe, *refs):
    bands, (field_out, probe_out, lanes) = refs[:10], refs[10:]
    y, c = geo[16], geo[17]
    for s in range(4):
        for which in range(2):
            owner = 2 * lax.rem(y - s + 4, 4) + (c if which == 0 else 1 - c)
            rows = pl.ds(owner, 32, stride=8)
            for part in range(2):
                pair = [
                    bands[at + s][part] if which == 0 else bands[at + 4][s, part]
                    for at in (0, 5)
                ]
                moved = steps1[0] * pair[0] + steps2[0] * pair[1]
                for at in range(8):
                    lanes[part, at, rows, :] = moved[:, at * H : at * H + H]
    for part in range(2):
        for at in range(8):
            here = slice(at * H, at * H + H)
            field_out[part, :, here] = field[part, :, here] + lanes[part, at]
    for k in range(4):
        for part in range(2):
            probe_out[k, part] = probe[k, part] + steps2[1] * dprobe[k, part]


def call(kernel, outs, args, smem_in, scratch=(), smem_out=(), flops=0):
    shapes = [jax.ShapeDtypeStruct(shape, F32) for shape in outs]
    moved = 4 * (sum(math.prod(s) for s in outs) + sum(a.size for a in args))
    return pl.pallas_call(
        kernel,
        out_shape=shapes,
        in_specs=[SMEM if i in smem_in else VMEM for i in range(len(args))],
        out_specs=[SMEM if i in smem_out else VMEM for i in range(len(outs))],
        scratch_shapes=[pltpu.VMEM(shape, F32) for shape in scratch],
        compiler_params=pltpu.CompilerParams(vmem_limit_bytes=48 * 2**20),
        cost_estimate=pl.CostEstimate(flops=flops, bytes_accessed=moved, transcendentals=0),
    )(*args)


def along_y(value, s):
    return lax.ppermute(value, "pat", [(i, (i + 2 * s) % 8) for i in range(8)])


def partner(value):
    return lax.ppermute(value, "pat", [(i, i ^ 1) for i in range(8)])


def up(value):
    return lax.ppermute(value, "tile", [(i, i + 1) for i in range(15)])


def down(value):
    return lax.ppermute(value, "tile", [(i + 1, i) for i in range(15)])


def spread(value, axes, count):
    return lax.all_to_all(jnp.broadcast_to(value[None], (count,) + value.shape), axes, 0, 0)


def first_patch(field, e0, col, c):
    edge = (2, H, 512)
    from_above = up(lax.dynamic_slice(field, (0, H, 512 * c), edge))
    from_below = down(lax.dynamic_slice(field, (0, 0, 512 * c), edge))
    both = jnp.stack([from_above, from_below])
    far = partner(both)
    left = jnp.where(c == 0, both, far)
    right = jnp.where(c == 0, far, both)
    rims = jnp.concatenate([left, right], axis=-1)
    extended = jnp.concatenate([rims[0], field, rims[1]], axis=1)
    return lax.dynamic_slice(extended, (0, e0, col), (2, N, N))


def body(intensity, positions, object_init, probe_init):
    tile = lax.axis_index("tile")
    pat = lax.axis_index("pat")
    y, c = pat // 2, pat % 2
    top = tile * N - H
    e0 = positions[0, 0] - top
    col = positions[0, 1]
    own = jnp.stack([e0, y, c]).astype(jnp.int32)
    table = jnp.asarray(real_tables())
    measured = intensity[0].reshape(H, 2, H, 2).transpose(1, 0, 3, 2).reshape(2, H, N)
    patch = first_patch(object_init, e0, col, c)
    places = spread(jnp.broadcast_to(positions, (8, 2)), "pat", 8)[:, 0]
    geo = jnp.concatenate(
        [places[:, 0] - top, places[:, 1], jnp.stack([y, c, tile, pat])]
    ).astype(jnp.int32)
    probe = probe_init
    steps = dirp = dprobe = None
    bands = []
    sent = (16, 9, 8, N)
    pieces = (4, 3, 32, N)
    scratch = ((4, 2, N, N), (2, H, N), (3, 2, N, H))
    for iteration in range(ITERS):
        if iteration == 0:
            keep, send, mine, other = call(
                lambda *refs: patterns_kernel(True, *refs),
                (sent, sent, pieces, pieces),
                (own, patch, probe, measured, table),
                (0,),
                scratch,
                flops=6 * 10**9,
            )
        else:
            patch, probe, keep, send, mine, other = call(
                lambda *refs: patterns_kernel(False, *refs),
                ((2, N, N), (4, 2, N, N), sent, sent, pieces, pieces),
                (own, steps, patch, probe, measured, table, dirp, dprobe),
                (0, 1),
                scratch,
                flops=6 * 10**9,
            )
        part = partner(other)
        chip = keep + partner(send)
        came = [
            along_y(jnp.stack([mine[s], part[s]]), s) for s in range(1, 4)
        ]
        shares = lax.all_to_all(chip, "tile", 0, 0)
        share = jnp.sum(shares, axis=0)
        low, high = call(
            place_kernel,
            ((3, 32, 1024), (3, 32, 1024)),
            (geo, mine, part, *came),
            (0,),
            ((3, 72, 1152),),
        )
        above = up(high)
        below = down(low)
        total = share + along_y(share, 1) + along_y(share, 2) + along_y(share, 3)
        illum = total[8:]
        d_share = total[:8] / (illum + RIDGE)
        d_size = d_share * d_share
        d_sum = 0.25 * jnp.sum(illum * d_size)
        f_sum = d_sum + 0.25 * jnp.sum(d_size)
        band, ae, r0, r1, r2, r3 = call(
            direction_kernel,
            ((2, 32, 1024), (1, 2)) + ((2, 2, 32, N),) * 4,
            (geo, low, high, above, below),
            (0,),
            ((2, 72, 1152),),
            smem_out=(1,),
        )
        back = [r0] + [along_y(r, s) for s, r in ((1, r1), (2, r2), (3, r3))]
        dmine = spread(d_share, "tile", 16)
        oth = partner(jnp.stack([r[1] for r in back]))
        doth = partner(dmine)
        dirp, dprobe, cross = call(
            cross_kernel,
            ((2, N, N), (4, 2, N, N), (1, 1)),
            (geo, *back, oth, dmine, doth, patch, probe),
            (0,),
            ((2, 2, N, H),),
            smem_out=(2,),
        )
        mixed = jnp.stack([ae[0, 0], cross[0, 0], d_sum, ae[0, 0] + ae[0, 1], f_sum])
        everyone = spread(jnp.broadcast_to(mixed[:, None], (5, 128)), BOTH, 128)
        sums = jnp.sum(everyone[:, :, 0], axis=0)
        object_power, cross_term, probe_power, object_pull, probe_pull = (
            sums[0],
            sums[1],
            sums[2],
            sums[3],
            sums[4],
        )
        ridge_term = 0.1 * (object_power + probe_power) + 1e-06
        determinant = (object_power + ridge_term) * (
            probe_power + ridge_term
        ) - cross_term * cross_term
        object_step = (
            (probe_power + ridge_term) * object_pull - cross_term * probe_pull
        ) / determinant
        probe_step = (
            (object_power + ridge_term) * probe_pull - cross_term * object_pull
        ) / determinant
        old_steps, steps = steps, jnp.stack([object_step, probe_step])
        bands.append(band)
        bands.extend(along_y(band, s) for s in range(1, 4))
        bands.append(partner(jnp.stack(bands[-4:])))
    return call(
        finish_kernel,
        (object_init.shape, probe_init.shape),
        (geo, old_steps, steps, object_init, probe, dprobe, *bands),
        (0, 1, 2),
        ((2, 8, N, H),),
    )


def solution(mesh):
    placed = (P(("pat", "tile"), None, None), P(("pat", "tile"), None), P(None, "tile", None), P())
    return jax.shard_map(
        body, mesh=mesh, in_specs=placed, out_specs=(P(None, "tile", None), P()), check_vma=False
    )
```

```python
import math

import jax
import jax.numpy as jnp
import ml_dtypes
import numpy as np
from jax import lax
from jax.experimental import pallas as pl
from jax.experimental.pallas import tpu as pltpu
from jax.sharding import PartitionSpec as P

ITERS = 2
FLOOR = 0.5
RIDGE = 1.0
N = 256
H = 128
F32 = jnp.float32
BF16 = jnp.bfloat16
BOTH = ("pat", "tile")
VMEM = pl.BlockSpec(memory_space=pltpu.VMEM)
SMEM = pl.BlockSpec(memory_space=pltpu.SMEM)
ANY = pl.BlockSpec(memory_space=pl.ANY)


def real_tables():
    near = np.arange(H)[:, None]
    far = np.arange(H)[None, :]
    found = []
    for parity in range(2):
        angle = -2.0 * math.pi * ((near * (2 * far + parity)) % N) / N
        real, imag = np.cos(angle) / 16.0, np.sin(angle) / 16.0
        found.append(np.block([[real, imag], [-imag, real]]))
    even, odd = found
    out = []
    for table in (even, odd, even.T, odd.T):
        high = table.astype(np.float32).astype(ml_dtypes.bfloat16)
        low = (table - high.astype(np.float64)).astype(np.float32).astype(ml_dtypes.bfloat16)
        out.append(np.stack([high, low]))
    return np.stack(out)


def halves(value):
    high = value.astype(BF16)
    return high, (value - high.astype(F32)).astype(BF16)


def dot(left, right):
    return jnp.dot(left, right, preferred_element_type=F32)


def times_table(value, table):
    high, low = halves(value)
    return dot(high, table[0]) + (dot(low, table[0]) + dot(high, table[1]))


def table_times(table, value):
    high, low = halves(value)
    return dot(table[0], high) + (dot(table[0], low) + dot(table[1], high))


def thirds(value):
    high, mid = halves(value)
    return high, mid, (value - high.astype(F32) - mid.astype(F32)).astype(BF16)


def step_sizes(everyone):
    total = jnp.sum(everyone[...], axis=0, keepdims=True)
    lane = lax.broadcasted_iota(jnp.int32, (1, 128), 1)
    object_power, cross_term, probe_power, object_pull, probe_pull = (
        jnp.broadcast_to(
            jnp.sum(jnp.where(lane == at, total, 0.0), axis=1, keepdims=True), (1, 128)
        )
        for at in range(5)
    )
    ridge = 0.1 * (object_power + probe_power) + 1e-06
    determinant = (object_power + ridge) * (probe_power + ridge) - cross_term * cross_term
    object_step = ((probe_power + ridge) * object_pull - cross_term * probe_pull) / determinant
    probe_step = ((object_power + ridge) * probe_pull - cross_term * object_pull) / determinant
    return object_step, probe_step


def twice(value):
    return jnp.concatenate([value, value], axis=1)


def joined(first_core, mine, other, plane):
    own, far = mine[plane], other[plane]
    return jnp.concatenate(
        [jnp.where(first_core, own, far), jnp.where(first_core, far, own)], axis=0
    )


def window_of(here):
    col = here[0, 1]
    block = pl.multiple_of(lax.min(lax.shift_right_logical(col, 7), 5) * H, H)
    return block, col - block


def cut(rows, e0, shift):
    rows = pltpu.roll(rows, lax.rem(2 * N - e0, N), axis=0)
    return pltpu.roll(rows, lax.rem(384 - shift, 384), axis=1)[:, :N]


def prepare_kernel(where, here, near, measured, swap, field, out, base, token):
    high, mid, low = thirds(measured[...])
    across, down_rows = swap[0], swap[1]
    high, mid, low = thirds(dot(high, across) + dot(mid, across) + dot(low, across))
    value = dot(down_rows, high) + dot(down_rows, mid) + dot(down_rows, low)
    out[0] = value[:H]
    out[1] = value[H:]
    e0 = here[0, 0] - where[3]
    block, shift = window_of(here)
    row = lax.broadcasted_iota(jnp.int32, (N, N), 0) + e0
    inside = (row >= H) & (row < H + N)
    for part in range(2):
        rows = field[part, :, pl.ds(block, 384)]
        rows = jnp.concatenate([rows[H:], rows[:H]], axis=0)
        base[part] = jnp.where(inside, cut(rows, e0, shift), 0.0)
    token[0, 0] = 0.0


def edge_kernel(where, field, top_rows, low_rows, sems):
    c = where[1]
    copies = [
        pltpu.make_async_copy(field.at[c, pl.ds(0, H), :], top_rows, sems.at[0]),
        pltpu.make_async_copy(field.at[c, pl.ds(H, H), :], low_rows, sems.at[1]),
    ]
    for copy in copies:
        copy.start()
    for copy in copies:
        copy.wait()


def edges(where, field):
    rows = pltpu.HBM((H, field.shape[2]), F32)
    hbm = pl.BlockSpec(memory_space=pltpu.HBM)
    return pl.pallas_call(
        edge_kernel,
        out_shape=[rows, rows],
        in_specs=[SMEM, ANY],
        out_specs=[hbm, hbm],
        scratch_shapes=[pltpu.SemaphoreType.DMA((2,))],
        compiler_params=pltpu.CompilerParams(vmem_limit_bytes=2**20),
    )(where, field)


def announce_kernel(here, above, below, out):
    lane = lax.broadcasted_iota(jnp.int32, (8, 128), 1)
    value = jnp.zeros((8, 128), jnp.int32)
    for at, place in enumerate((here, above, below)):
        value = jnp.where(lane == 2 * at, place[0, 0], value)
        value = jnp.where(lane == 2 * at + 1, place[0, 1], value)
    out[...] = value


def side_kernel(where, near, token, above, below, own, far):
    y, c, top = where[0], where[1], where[3]
    own_row = near[2 * y + c, 0] - top
    far_row = near[2 * y + 1 - c, 0] - top
    own[...] = jnp.where(own_row < H, above[...], below[...])
    far[...] = jnp.where(far_row < H, above[...], below[...])


def add_side(where, here, base, own_side, far_side, patch):
    e0, first_core = here[0, 0] - where[3], where[1] == 0
    block, shift = window_of(here)
    row = lax.broadcasted_iota(jnp.int32, (N, N), 0) + e0
    outside = (row < H) | (row >= H + N)
    own, far = own_side[:, pl.ds(block, 384)], far_side[:, pl.ds(block, 384)]
    for part in range(2):
        rows = jnp.where(first_core == (part == 0), own, far)
        rows = cut(jnp.concatenate([rows, rows], axis=0), e0, shift)
        patch[part] = jnp.where(outside, rows, base[part])


def patterns_kernel(first, ready, *refs):
    if first:
        where, here, base, own_side, far_side, probe_now, measured, tab = refs[:8]
        patch_now, keep, send, mine, other, power, token, psi, model, obj = refs[8:]
        token[0, 0] = 0.0
        add_side(where, here, base, own_side, far_side, patch_now)
    else:
        where, here, everyone, patch, probe, measured, tab, dirp, dmine, doth = refs[:10]
        patch_now, probe_now = refs[10:12]
        keep, send, mine, other, power, psi, model, obj = refs[12:]
        object_step, probe_step = map(twice, step_sizes(everyone))
        ready(3)
        ready(7)
        for part in range(2):
            patch_now[part] = patch[part] + object_step * dirp[part]
    y, c = where[0], where[1]
    e0 = here[0, 0] - where[3]
    first_core = c == 0
    model[...] = jnp.zeros_like(model)
    obj[...] = jnp.zeros_like(obj)
    power[...] = jnp.zeros_like(power)

    def gather(plane, value):
        obj[plane, 0] += value[:, :H]
        obj[plane, 1] += value[:, H:]

    def forward(k):
        if first:
            ready(5, k)
        else:
            ready(4, k)
            for part in range(2):
                ready(8, 2 * k + part)
                ready(9, 2 * k + part)
                moved = probe_step * joined(first_core, dmine, doth, 2 * k + part)
                probe_now[k, part] = probe[k, part] + moved
        pr, pi = probe_now[k, 0], probe_now[k, 1]
        orr, oi = patch_now[0], patch_now[1]
        power[...] += pr * pr + pi * pi
        xr = pr * orr - pi * oi
        xi = pr * oi + pi * orr
        even = times_table(
            jnp.concatenate([xr[:, :H] + xr[:, H:], xi[:, :H] + xi[:, H:]], axis=1), tab.at[0]
        )
        odd = times_table(
            jnp.concatenate([xr[:, :H] - xr[:, H:], xi[:, :H] - xi[:, H:]], axis=1), tab.at[1]
        )
        re = jnp.concatenate([even[:, :H], odd[:, :H]], axis=1)
        im = jnp.concatenate([even[:, H:], odd[:, H:]], axis=1)
        for row, sign in ((0, 1.0), (1, -1.0)):
            folded = jnp.concatenate(
                [re[:H] + sign * re[H:], im[:H] + sign * im[H:]], axis=0
            )
            far = table_times(tab.at[2 + row], folded)
            psi[k, row] = far
            model[row] += far[:H] * far[:H] + far[H:] * far[H:]

    ready(7 if first else 6)
    for k in range(4):
        forward(k)
    ready(6 if first else 5)
    for row in range(2):
        model[row] = jnp.sqrt(measured[row] / jnp.maximum(model[row], FLOOR)) - 1.0

    def put(plane, value):
        low = value[:H].reshape(16, 8, N)
        high = value[H:].reshape(16, 8, N)
        keep[:, plane] = jnp.where(first_core, low, high)
        send[:, plane] = jnp.where(first_core, high, low)

    def backward(k):
        parts = []
        for row in range(2):
            scale = model[row]
            weighted = psi[k, row] * jnp.concatenate([scale, scale], axis=0)
            parts.append(table_times(tab.at[row], weighted))
        ee, oo = parts
        re = jnp.concatenate([ee[:H] + oo[:H], ee[:H] - oo[:H]], axis=0)
        im = jnp.concatenate([ee[H:] + oo[H:], ee[H:] - oo[H:]], axis=0)
        even = times_table(jnp.concatenate([re[:, :H], im[:, :H]], axis=1), tab.at[2])
        odd = times_table(jnp.concatenate([re[:, H:], im[:, H:]], axis=1), tab.at[3])
        dr = jnp.concatenate([even[:, :H] + odd[:, :H], even[:, :H] - odd[:, :H]], axis=1)
        di = jnp.concatenate([even[:, H:] + odd[:, H:], even[:, H:] - odd[:, H:]], axis=1)
        pr, pi = probe_now[k, 0], probe_now[k, 1]
        orr, oi = patch_now[0], patch_now[1]
        gather(0, pr * dr + pi * di)
        gather(1, pr * di - pi * dr)
        put(2 * k, orr * dr + oi * di)
        put(2 * k + 1, orr * di - oi * dr)

    for k in range(4):
        backward(k)
    orr, oi = patch_now[0], patch_now[1]
    put(8, orr * orr + oi * oi)
    for s in range(4):
        for which, dest in ((c, mine), (1 - c, other)):
            owner = 2 * lax.rem(y + s, 4) + which
            start = lax.rem(owner - e0 + 1024, 8)
            for plane in range(2):
                for half in range(2):
                    rows = obj[plane, half, pl.ds(start, 32, stride=8), :]
                    dest[s, plane, :, half * H : half * H + H] = rows


def place_of(where, places, owner, pattern, band=0):
    e0 = places[pattern, 2 * band] - where[3]
    col = places[pattern, 2 * band + 1]
    start = lax.rem(owner - e0 + 1024, 8)
    row = lax.shift_right_logical(e0 + 256 + start - owner, 3)
    base = pl.multiple_of(lax.shift_right_logical(row, 3) * 8, 8)
    block = pl.multiple_of(lax.shift_right_logical(col, 7) * 128, 128)
    return start, base, lax.rem(row, 8), block, lax.rem(col, 128)


def place(acc, piece, base, turn, block, shift):
    wide = pltpu.roll(jnp.concatenate([piece, jnp.zeros((32, 128), F32)], axis=1), shift, axis=1)
    wide = pltpu.roll(jnp.concatenate([wide, jnp.zeros((8, 384), F32)], axis=0), turn, axis=0)
    acc[pl.ds(base, 40), pl.ds(block, 384)] += wide


def illum_kernel(where, near, token, total, out, power, acc):
    owner = 2 * where[0] + where[1]
    acc[...] = jnp.zeros_like(acc)
    power[0] = total[:, :H]
    power[1] = total[:, H:]

    def from_band(band):
        def one(pattern, carry):
            start, base, turn, block, shift = place_of(where, near, owner, pattern, band)
            rows = pl.ds(start, 32, stride=8)
            piece = jnp.concatenate([power[0, rows, :], power[1, rows, :]], axis=1)
            place(acc, piece, base, turn, block, shift)
            return carry

        return one

    tile = where[2]
    lax.fori_loop(0, 8, from_band(0), 0)
    lax.fori_loop(0, jnp.where(tile == 0, 0, 8), from_band(1), 0)
    lax.fori_loop(0, jnp.where(tile == 15, 0, 8), from_band(2), 0)
    out[...] = acc[32:96, :1024]


def place_kernel(where, near, b0, b1, b2, b3, low, high, token, acc):
    token[0, 0] = 0.0
    y, c = where[0], where[1]
    owner = 2 * y + c
    acc[...] = jnp.zeros_like(acc)
    for s in range(4):
        for which in range(2):
            pattern = 2 * lax.rem(y - s + 4, 4) + (c if which == 0 else 1 - c)
            start, base, turn, block, shift = place_of(where, near, owner, pattern)
            for plane in range(2):
                piece = (b0, b1, b2, b3)[s][which, plane]
                place(acc.at[plane], piece, base - 32, turn, block, shift)
    low[...] = acc[:, :32, :1024]
    high[...] = acc[:, 32:64, :1024]


def direction_kernel(
    where, near, token, illum, low, high, above, below, band, sums, r0, r1, r2, r3, wide
):
    y, c = where[0], where[1]
    owner = 2 * y + c
    wide[...] = jnp.zeros_like(wide)
    total_a = jnp.zeros((16, 1024), F32)
    total_n = jnp.zeros((16, 1024), F32)
    for at, (own, came) in enumerate(((low, above), (high, below))):
        rows = slice(32 * at, 32 * at + 32)
        light = illum[rows]
        scale = 1.0 / (light + RIDGE)
        real = (own[0] + came[0]) * scale
        imag = (own[1] + came[1]) * scale
        wide[0, rows, :1024] = real
        wide[1, rows, :1024] = imag
        inner = slice(16, 32) if at == 0 else slice(0, 16)
        real, imag, light = real[inner], imag[inner], light[inner]
        band[0, 16 * at : 16 * at + 16] = real
        band[1, 16 * at : 16 * at + 16] = imag
        size = real * real + imag * imag
        total_n += size
        total_a += light * size
    sums[0, 0] = jnp.sum(total_a)
    sums[0, 1] = jnp.sum(total_n)
    for s, dest in enumerate((r0, r1, r2, r3)):
        for which in range(2):
            pattern = 2 * lax.rem(y + s, 4) + (c if which == 0 else 1 - c)
            start, base, turn, block, shift = place_of(where, near, owner, pattern)
            for part in range(2):
                piece = wide[part, pl.ds(base - 32, 40), pl.ds(block, 384)]
                piece = pltpu.roll(piece, lax.rem(40 - turn, 40), axis=0)[:32]
                dest[which, part] = pltpu.roll(piece, lax.rem(384 - shift, 384), axis=1)[:, :N]


def stack_kernel(r0, r1, r2, r3, out):
    for s, came in enumerate((r0, r1, r2, r3)):
        out[s] = came[1]


def patch_kernel(where, near, r0, r1, r2, r3, oth, patch, dirp, kept, sent, lanes):
    y, c = where[0], where[1]
    e0 = near[2 * y + c, 0] - where[3]
    for s, came in enumerate((r0, r1, r2, r3)):
        for which in range(2):
            owner = 2 * lax.rem(y - s + 4, 4) + (c if which == 0 else 1 - c)
            rows = pl.ds(lax.rem(owner - e0 + 1024, 8), 32, stride=8)
            for part in range(2):
                piece = came[0, part] if which == 0 else oth[s, part]
                for half in range(2):
                    lanes[part, half, rows, :] = piece[:, half * H : half * H + H]
    for part in range(2):
        for half in range(2):
            dirp[part, :, half * H : half * H + H] = lanes[part, half]
    for which, dest in ((c, kept), (1 - c, sent)):
        rows = pl.ds(pl.multiple_of(which * H, H), H)
        dr, di = dirp[0, rows, :], dirp[1, rows, :]
        orr, oi = patch[0, rows, :], patch[1, rows, :]
        dest[0] = dr * orr + di * oi
        dest[1] = dr * oi - di * orr


def pack_kernel(keep, came, mine, part, chip, b0, b1, b2, b3):
    chip[...] = keep[...] + came[...]
    for s, dest in enumerate((b0, b1, b2, b3)):
        dest[0] = mine[s]
        dest[1] = part[s]


def sum_kernel(before, shares, out, token):
    out[...] = jnp.sum(shares[...], axis=0)
    token[0, 0] = 0.0


def share_kernel(own, a, b, d, above, below, light, spread_out, sums):
    total = own[...] + a[...] + b[...] + d[...]
    illum = total[8]
    value = total[:8] * (1.0 / (illum + RIDGE))
    spread_out[...] = jnp.broadcast_to(value[None], (16, 8, 8, N))
    size = jnp.sum(value * value, axis=0)
    sums[0, 0] = jnp.sum(size * illum)
    sums[0, 1] = jnp.sum(size)


def relay_kernel(token, gathered, out):
    for plane in range(8):
        out[plane] = gathered[:, plane].reshape(H, N)


def message_kernel(where, gathered, probe, kept, came, ae, df, out, token, half, sem):
    token[0, 0] = 0.0
    rows = pl.ds(pl.multiple_of(where[1] * H, H), H)
    copy = pltpu.make_async_copy(probe.at[:, :, rows, :], half, sem)
    copy.start()
    total = jnp.zeros((H, N), F32)
    mixed_real = kept[0] + came[0]
    mixed_imag = kept[1] + came[1]
    copy.wait()
    for k in range(4):
        dr = gathered[:, 2 * k].reshape(H, N)
        di = gathered[:, 2 * k + 1].reshape(H, N)
        pr, pi = half[k, 0], half[k, 1]
        total += mixed_real * (pr * dr + pi * di) - mixed_imag * (pr * di - pi * dr)
    cross = jnp.sum(total)
    d_sum = 0.25 * df[0, 0]
    values = (ae[0, 0], cross, d_sum, ae[0, 0] + ae[0, 1], d_sum + 0.25 * df[0, 1])
    lane = lax.broadcasted_iota(jnp.int32, (128, 128), 1)
    message = jnp.zeros((128, 128), F32)
    for at, value in enumerate(values):
        message = jnp.where(lane == at, value, message)
    out[...] = message


def finish_kernel(
    where, one, two, field, band1, band2, probe, dmine, doth, field_out, probe_out, steps, lanes
):
    at = pl.program_id(0)

    @pl.when(at == 0)
    def _():
        steps[0:1] = step_sizes(one)[0]
        object_step, probe_step = step_sizes(two)
        steps[1:2] = object_step
        steps[2:3] = probe_step

    first = jnp.concatenate([steps[0:1]] * 8, axis=1)
    second = jnp.concatenate([steps[1:2]] * 8, axis=1)
    probe_step = twice(steps[2:3])
    for part in range(2):
        for owner in range(8):
            rows = pl.ds(owner, 8, stride=8)
            moved = first * band1[owner, part] + second * band2[owner, part]
            for column in range(8):
                lanes[part, column, rows, :] = moved[:, column * H : column * H + H]
        for column in range(8):
            here = slice(column * H, column * H + H)
            field_out[part, :, here] = field[part, :, here] + lanes[part, column]
    local = lax.shift_right_logical(at, 1) == where[1]
    for k in range(4):
        for part in range(2):
            plane = 2 * k + part
            value = jnp.where(local, dmine[plane], doth[plane])
            probe_out[k, part] = probe[k, part] + probe_step * value


def finish(where, one, two, field, band1, band2, probe, dmine, doth):
    rows = pl.BlockSpec((2, 64, 1024), lambda i: (0, i, 0))
    classes = pl.BlockSpec((8, 2, 8, 1024), lambda i: (0, 0, i, 0))
    modes = pl.BlockSpec((4, 2, 64, N), lambda i: (0, 0, i, 0))
    gathered = pl.BlockSpec((8, 64, N), lambda i: (0, lax.rem(i, 2), 0))
    whole = pl.BlockSpec((128, 128), lambda i: (0, 0))
    return pl.pallas_call(
        finish_kernel,
        grid=(4,),
        out_shape=[
            jax.ShapeDtypeStruct(field.shape, F32),
            jax.ShapeDtypeStruct(probe.shape, F32),
        ],
        in_specs=[SMEM, whole, whole, rows, classes, classes, modes, gathered, gathered],
        out_specs=[rows, modes],
        scratch_shapes=[pltpu.VMEM((8, 128), F32), pltpu.VMEM((2, 8, 64, H), F32)],
        compiler_params=pltpu.CompilerParams(vmem_limit_bytes=14 * 2**20),
    )(
        where,
        one,
        two,
        *[
            pltpu.with_memory_space_constraint(a, pltpu.HBM)
            for a in (field, band1, band2, probe, dmine, doth)
        ],
    )


def call(
    kernel,
    outs,
    args,
    smem_in,
    scratch=(),
    smem_out=(),
    hbm_out=(),
    vmem_out=(),
    hbm_in=(),
    any_in=(),
    lazy=False,
    flops=0,
    room=12,
    name=None,
):
    outs = [out if isinstance(out[0], tuple) else (out, F32) for out in outs]
    shapes = [
        pltpu.HBM(*out)
        if i in hbm_out
        else pltpu.VMEM(*out)
        if i in vmem_out
        else jax.ShapeDtypeStruct(*out)
        for i, out in enumerate(outs)
    ]
    hbm_in = hbm_in if isinstance(hbm_in, dict) else {index: 1 for index in hbm_in}
    moved = 4 * (sum(math.prod(out[0]) for out in outs) + sum(a.size for a in args))
    stage_in = [pltpu.VMEM(args[i].shape, args[i].dtype) for i in hbm_in]
    stage_out = [pltpu.VMEM(*outs[i]) for i in hbm_out]
    args = [
        pltpu.with_memory_space_constraint(a, pltpu.HBM) if i in hbm_in else a
        for i, a in enumerate(args)
    ]
    first, last = len(args), len(args) + len(outs)
    pieces = sum(hbm_in.values())

    def run(*refs):
        given, results = list(refs[:first]), list(refs[first:last])
        rest = refs[last:]
        staged = rest[len(scratch) : len(scratch) + len(stage_in) + len(stage_out)]
        sems = rest[-1] if staged else None
        arrivals, at = {}, 0
        for slot, (index, count) in enumerate(hbm_in.items()):
            stage, source = staged[slot], given[index]
            for piece in range(count):
                pair = (source, stage) if count == 1 else (source.at[piece], stage.at[piece])
                copy = pltpu.make_async_copy(*pair, sems.at[at])
                copy.start()
                arrivals[index, piece] = copy
                at += 1
            given[index] = stage
        departures = []
        for slot, index in enumerate(hbm_out):
            stage = staged[len(stage_in) + slot]
            departures.append(pltpu.make_async_copy(stage, results[index], sems.at[at + slot]))
            results[index] = stage

        def ready(index, piece=0):
            arrivals[index, piece].wait()

        if lazy:
            kernel(ready, *given, *results, *rest[: len(scratch)])
        else:
            for copy in arrivals.values():
                copy.wait()
            kernel(*given, *results, *rest[: len(scratch)])
        for copy in departures:
            copy.start()
        for copy in departures:
            copy.wait()

    def space(index, smem, hbm):
        return SMEM if index in smem else ANY if index in hbm or index in any_in else VMEM

    extra = stage_in + stage_out
    if extra:
        extra.append(pltpu.SemaphoreType.DMA((pieces + len(stage_out),)))
    hbm = pl.BlockSpec(memory_space=pltpu.HBM)
    return pl.pallas_call(
        run,
        out_shape=shapes,
        in_specs=[space(i, smem_in, hbm_in) for i in range(len(args))],
        out_specs=[
            hbm if i in hbm_out else SMEM if i in smem_out else VMEM for i in range(len(outs))
        ],
        scratch_shapes=[
            pltpu.VMEM(shape, F32) if shape else pltpu.SemaphoreType.DMA for shape in scratch
        ]
        + extra,
        name=name or kernel.__name__,
        compiler_params=pltpu.CompilerParams(vmem_limit_bytes=room * 2**20),
        cost_estimate=pl.CostEstimate(flops=flops, bytes_accessed=moved, transcendentals=0),
    )(*args)


def along_y(value, s):
    return lax.ppermute(value, "pat", [(i, (i + 2 * s) % 8) for i in range(8)])


def partner(value):
    return lax.ppermute(value, "pat", [(i, i ^ 1) for i in range(8)])


def up(value):
    return lax.ppermute(value, "tile", [(i, i + 1) for i in range(15)])


def down(value):
    return lax.ppermute(value, "tile", [(i + 1, i) for i in range(15)])


def spread(value, axes, count):
    return lax.all_to_all(jnp.broadcast_to(value[None], (count,) + value.shape), axes, 0, 0)


def one_hot():
    order = np.concatenate([np.arange(0, N, 2), np.arange(1, N, 2)])
    across = np.zeros((N, N), np.float32)
    across[order, np.arange(N)] = 1.0
    return np.stack([across, across.T]).astype(ml_dtypes.bfloat16)


def body(intensity, positions, object_init, probe_init):
    tile = lax.axis_index("tile")
    pat = lax.axis_index("pat")
    y, c = pat // 2, pat % 2
    top = tile * N - H
    where = jnp.stack([y, c, tile, top]).astype(jnp.int32)
    neighbours = up(positions), down(positions)
    top_rows, low_rows = edges(where, object_init)
    from_above, from_below = up(low_rows), down(top_rows)
    (news,) = call(
        announce_kernel, (((8, 128), jnp.int32),), (positions, *neighbours), (0, 1, 2), room=1
    )
    near = lax.all_to_all(news, "pat", 0, 0)
    table = jnp.asarray(real_tables())
    measured, base, token = call(
        prepare_kernel,
        ((2, H, N), (2, N, N), (1, 1)),
        (
            where,
            positions,
            near,
            intensity[0],
            jnp.asarray(one_hot()),
            object_init,
        ),
        (0, 1, 2),
        hbm_in=(3, 4, 5),
        smem_out=(2,),
        hbm_out=(0,),
        room=16,
    )
    own_side, far_side = call(
        side_kernel,
        ((H, 1024), (H, 1024)),
        (where, near, token, from_above, from_below),
        (0, 1, 2),
        room=4,
    )
    far_side = partner(far_side)

    probe = probe_init
    sent = (16, 9, 8, N)
    pieces = (4, 2, 32, N)
    scratch = ((4, 2, N, N), (2, H, N), (2, 2, N, H))
    outs = (sent, sent, pieces, pieces, (N, N))
    messages, bands = [], []

    for iteration in range(ITERS):
        if iteration == 0:
            patch, keep, send, mine, other, power, token = call(
                lambda *refs: patterns_kernel(True, *refs),
                ((2, N, N),) + outs + ((1, 1),),
                (where, positions, base, own_side, far_side, probe, measured, table),
                (0, 1),
                scratch,
                hbm_in={5: 4, 6: 1, 7: 1},
                lazy=True,
                smem_out=(6,),
                flops=6 * 10**9,
                room=28,
                name="patterns",
            )
        else:
            patch, probe, keep, send, mine, other, power = call(
                lambda *refs: patterns_kernel(False, *refs),
                ((2, N, N), (4, 2, N, N)) + outs,
                (where, positions, messages[-1], patch, probe, measured, table, dirp, dmine, doth),
                (0, 1),
                scratch,
                hbm_in={3: 1, 4: 4, 5: 1, 6: 1, 7: 1, 8: 8, 9: 8},
                lazy=True,
                hbm_out=(0, 1),
                flops=6 * 10**9,
                room=30,
                name="patterns",
            )
        chip, b0, b1, b2, b3 = call(
            pack_kernel,
            (sent,) + ((2, 2, 32, N),) * 4,
            (keep, partner(send), mine, partner(other)),
            (),
            hbm_out=(0, 2, 3, 4),
        )
        came = [b0, along_y(b1, 1), along_y(b2, 2), along_y(b3, 3)]
        low, high, token = call(
            place_kernel,
            ((2, 32, 1024), (2, 32, 1024), (1, 1)),
            (where, near, *came),
            (0, 1),
            ((2, 72, 1152),),
            smem_out=(2,),
            hbm_out=(0, 1),
        )
        above, below = up(high), down(low)
        shares = lax.all_to_all(chip, "tile", 0, 0)
        share, token = call(
            sum_kernel, ((9, 8, N), (1, 1)), (token, shares), (0,), smem_out=(1,)
        )
        (illum,) = call(
            illum_kernel,
            ((64, 1024),),
            (where, near, token, power),
            (0, 1, 2),
            ((2, N, H), (136, 1152)),
        )
        probe_dir, df = call(
            share_kernel,
            ((16, 8, 8, N), (1, 2)),
            (share, *[along_y(share, s) for s in range(1, 4)], above, below, illum),
            (),
            smem_out=(1,),
            hbm_out=(0,),
            any_in=(4, 5, 6),
        )
        gathered = lax.all_to_all(probe_dir, "tile", 0, 0)
        band, ae, r0, r1, r2, r3 = call(
            direction_kernel,
            ((2, 32, 1024), (1, 2)) + ((2, 2, 32, N),) * 4,
            (where, near, df, illum, low, high, above, below),
            (0, 1, 2),
            ((2, 72, 1152),),
            smem_out=(1,),
            hbm_out=(0, 3, 4, 5),
            hbm_in=(4, 5, 6, 7),
        )
        bands.append(lax.all_gather(band, "pat"))
        back = [r0] + [along_y(r, s) for s, r in ((1, r1), (2, r2), (3, r3))]
        (oth,) = call(stack_kernel, ((4, 2, 32, N),), back, (), room=4)
        dirp, kept, sent_mixed = call(
            patch_kernel,
            ((2, N, N), (2, H, N), (2, H, N)),
            (where, near, *back, partner(oth), patch),
            (0, 1),
            ((2, 2, N, H),),
        )
        message, token = call(
            message_kernel,
            ((128, 128), (1, 1)),
            (
                where,
                gathered,
                pltpu.with_memory_space_constraint(probe, pltpu.HBM),
                kept,
                partner(sent_mixed),
                ae,
                df,
            ),
            (0, 5, 6),
            ((4, 2, H, N), None),
            any_in=(2,),
            smem_out=(1,),
            hbm_out=(0,),
        )
        (dmine,) = call(relay_kernel, ((8, H, N),), (token, gathered), (0,))
        doth = partner(dmine)
        messages.append(lax.all_to_all(message, BOTH, 0, 0))
    return finish(where, *messages, object_init, *bands, probe, dmine, doth)


def solution(mesh):
    placed = (P(("pat", "tile"), None, None), P(("pat", "tile"), None), P(None, "tile", None), P())
    return jax.shard_map(
        body, mesh=mesh, in_specs=placed, out_specs=(P(None, "tile", None), P()), check_vma=False
    )
```

```python
import math

import jax
import jax.numpy as jnp
import ml_dtypes
import numpy as np
from jax import lax
from jax.experimental import pallas as pl
from jax.experimental.pallas import tpu as pltpu
from jax.sharding import PartitionSpec as P

ITERS = 2
FLOOR = 0.5
RIDGE = 1.0
N = 256
H = 128
F32 = jnp.float32
BF16 = jnp.bfloat16
BOTH = ("pat", "tile")
VMEM = pl.BlockSpec(memory_space=pltpu.VMEM)
SMEM = pl.BlockSpec(memory_space=pltpu.SMEM)
ANY = pl.BlockSpec(memory_space=pl.ANY)


def real_tables():
    near = np.arange(H)[:, None]
    far = np.arange(H)[None, :]
    found = []
    for parity in range(2):
        angle = -2.0 * math.pi * ((near * (2 * far + parity)) % N) / N
        real, imag = np.cos(angle) / 16.0, np.sin(angle) / 16.0
        found.append(np.block([[real, imag], [-imag, real]]))
    even, odd = found
    out = []
    for table in (even, odd, even.T, odd.T):
        high = table.astype(np.float32).astype(ml_dtypes.bfloat16)
        low = (table - high.astype(np.float64)).astype(np.float32).astype(ml_dtypes.bfloat16)
        out.append(np.stack([high, low]))
    return np.stack(out)


def halves(value):
    high = value.astype(BF16)
    return high, (value - high.astype(F32)).astype(BF16)


def dot(left, right):
    return jnp.dot(left, right, preferred_element_type=F32)


def times_table(value, table):
    high, low = halves(value)
    return dot(high, table[0]) + (dot(low, table[0]) + dot(high, table[1]))


def table_times(table, value):
    high, low = halves(value)
    return dot(table[0], high) + (dot(table[0], low) + dot(table[1], high))


def thirds(value):
    high, mid = halves(value)
    return high, mid, (value - high.astype(F32) - mid.astype(F32)).astype(BF16)


def step_sizes(everyone):
    total = jnp.sum(everyone[...], axis=0, keepdims=True)
    lane = lax.broadcasted_iota(jnp.int32, (1, 128), 1)
    object_power, cross_term, probe_power, object_pull, probe_pull = (
        jnp.broadcast_to(
            jnp.sum(jnp.where(lane == at, total, 0.0), axis=1, keepdims=True), (1, 128)
        )
        for at in range(5)
    )
    ridge = 0.1 * (object_power + probe_power) + 1e-06
    determinant = (object_power + ridge) * (probe_power + ridge) - cross_term * cross_term
    object_step = ((probe_power + ridge) * object_pull - cross_term * probe_pull) / determinant
    probe_step = ((object_power + ridge) * probe_pull - cross_term * object_pull) / determinant
    return object_step, probe_step


def twice(value):
    return jnp.concatenate([value, value], axis=1)


def joined(first_core, mine, other, plane):
    own, far = mine[plane], other[plane]
    return jnp.concatenate(
        [jnp.where(first_core, own, far), jnp.where(first_core, far, own)], axis=0
    )


def window_of(here):
    col = here[0, 1]
    block = pl.multiple_of(lax.min(lax.shift_right_logical(col, 7), 5) * H, H)
    return block, col - block


def cut(rows, e0, shift):
    rows = pltpu.roll(rows, lax.rem(2 * N - e0, N), axis=0)
    return pltpu.roll(rows, lax.rem(384 - shift, 384), axis=1)[:, :N]


def prepare_kernel(where, here, measured, swap, field, out, base, window, sem):
    e0 = here[0, 0] - where[3]
    block, shift = window_of(here)
    copy = pltpu.make_async_copy(field.at[:, :, pl.ds(block, 384)], window, sem)
    copy.start()
    high, mid, low = thirds(measured[...])
    across, down_rows = swap[0], swap[1]
    high, mid, low = thirds(dot(high, across) + dot(mid, across) + dot(low, across))
    value = dot(down_rows, high) + dot(down_rows, mid) + dot(down_rows, low)
    out[0] = value[:H]
    out[1] = value[H:]
    row = lax.broadcasted_iota(jnp.int32, (N, N), 0) + e0
    inside = (row >= H) & (row < H + N)
    copy.wait()
    for part in range(2):
        rows = jnp.concatenate([window[part, H:], window[part, :H]], axis=0)
        base[part] = jnp.where(inside, cut(rows, e0, shift), 0.0)


def edge_kernel(where, field, top_rows, low_rows, sems):
    c = where[1]
    copies = [
        pltpu.make_async_copy(field.at[c, pl.ds(0, H), :], top_rows, sems.at[0]),
        pltpu.make_async_copy(field.at[c, pl.ds(H, H), :], low_rows, sems.at[1]),
    ]
    for copy in copies:
        copy.start()
    for copy in copies:
        copy.wait()


def edges(where, field):
    rows = pltpu.VMEM((H, field.shape[2]), F32)
    return pl.pallas_call(
        edge_kernel,
        out_shape=[rows, rows],
        in_specs=[SMEM, ANY],
        out_specs=[VMEM, VMEM],
        scratch_shapes=[pltpu.SemaphoreType.DMA((2,))],
        compiler_params=pltpu.CompilerParams(vmem_limit_bytes=2 * 2**20),
    )(where, field)


def announce_kernel(here, out):
    lane = lax.broadcasted_iota(jnp.int32, (8, 128), 1)
    out[...] = jnp.where(lane == 0, here[0, 0], here[0, 1])


def side_kernel(where, near, base, above, below, own, far):
    y, c, top = where[0], where[1], where[3]
    own_row = near[2 * y + c, 0] - top
    far_row = near[2 * y + 1 - c, 0] - top
    own[...] = jnp.where(own_row < H, above[...], below[...])
    far[...] = jnp.where(far_row < H, above[...], below[...])


def add_side(where, here, base, own_side, far_side, patch):
    e0, first_core = here[0, 0] - where[3], where[1] == 0
    block, shift = window_of(here)
    row = lax.broadcasted_iota(jnp.int32, (N, N), 0) + e0
    outside = (row < H) | (row >= H + N)
    own, far = own_side[:, pl.ds(block, 384)], far_side[:, pl.ds(block, 384)]
    for part in range(2):
        rows = jnp.where(first_core == (part == 0), own, far)
        rows = cut(jnp.concatenate([rows, rows], axis=0), e0, shift)
        patch[part] = jnp.where(outside, rows, base[part])


def patterns_kernel(first, ready, leave, *refs):
    if first:
        where, here, base, own_side, far_side, probe_now, measured, tab = refs[:8]
        patch_now, keep, send, mine, other, power, psi, model, obj = refs[8:]
        add_side(where, here, base, own_side, far_side, patch_now)
    else:
        where, here, everyone, patch, probe, measured, tab, dirp, dmine, doth = refs[:10]
        patch_now, probe_now = refs[13:15]
        keep, send, mine, other, power, psi, model, obj = refs[15:]
        object_step, probe_step = map(twice, step_sizes(everyone))
        ready(3)
        ready(7)
        for part in range(2):
            patch_now[part] = patch[part] + object_step * dirp[part]
        leave(0)
    y, c = where[0], where[1]
    e0 = here[0, 0] - where[3]
    first_core = c == 0
    model[...] = jnp.zeros_like(model)
    obj[...] = jnp.zeros_like(obj)
    power[...] = jnp.zeros_like(power)

    def gather(plane, value):
        obj[plane, 0] += value[:, :H]
        obj[plane, 1] += value[:, H:]

    def forward(k):
        if not first:
            for index in (4, 8, 9):
                ready(index, k)
            for part in range(2):
                moved = probe_step * joined(first_core, dmine, doth, 2 * k + part)
                probe_now[k, part] = probe[k, part] + moved
            leave(1, k)
        pr, pi = probe_now[k, 0], probe_now[k, 1]
        orr, oi = patch_now[0], patch_now[1]
        power[...] += pr * pr + pi * pi
        xr = pr * orr - pi * oi
        xi = pr * oi + pi * orr
        even = times_table(
            jnp.concatenate([xr[:, :H] + xr[:, H:], xi[:, :H] + xi[:, H:]], axis=1), tab.at[0]
        )
        odd = times_table(
            jnp.concatenate([xr[:, :H] - xr[:, H:], xi[:, :H] - xi[:, H:]], axis=1), tab.at[1]
        )
        re = jnp.concatenate([even[:, :H], odd[:, :H]], axis=1)
        im = jnp.concatenate([even[:, H:], odd[:, H:]], axis=1)
        for row, sign in ((0, 1.0), (1, -1.0)):
            folded = jnp.concatenate(
                [re[:H] + sign * re[H:], im[:H] + sign * im[H:]], axis=0
            )
            far = table_times(tab.at[2 + row], folded)
            psi[k, row] = far
            model[row] += far[:H] * far[:H] + far[H:] * far[H:]

    if not first:
        ready(6)
    for k in range(4):
        forward(k)
    if not first:
        ready(5)
    for row in range(2):
        model[row] = jnp.sqrt(measured[row] / jnp.maximum(model[row], FLOOR)) - 1.0

    def put(plane, value):
        low = value[:H].reshape(16, 8, N)
        high = value[H:].reshape(16, 8, N)
        keep[:, plane] = jnp.where(first_core, low, high)
        send[:, plane] = jnp.where(first_core, high, low)

    def backward(k):
        parts = []
        for row in range(2):
            scale = model[row]
            weighted = psi[k, row] * jnp.concatenate([scale, scale], axis=0)
            parts.append(table_times(tab.at[row], weighted))
        ee, oo = parts
        re = jnp.concatenate([ee[:H] + oo[:H], ee[:H] - oo[:H]], axis=0)
        im = jnp.concatenate([ee[H:] + oo[H:], ee[H:] - oo[H:]], axis=0)
        even = times_table(jnp.concatenate([re[:, :H], im[:, :H]], axis=1), tab.at[2])
        odd = times_table(jnp.concatenate([re[:, H:], im[:, H:]], axis=1), tab.at[3])
        dr = jnp.concatenate([even[:, :H] + odd[:, :H], even[:, :H] - odd[:, :H]], axis=1)
        di = jnp.concatenate([even[:, H:] + odd[:, H:], even[:, H:] - odd[:, H:]], axis=1)
        pr, pi = probe_now[k, 0], probe_now[k, 1]
        orr, oi = patch_now[0], patch_now[1]
        gather(0, pr * dr + pi * di)
        gather(1, pr * di - pi * dr)
        put(2 * k, orr * dr + oi * di)
        put(2 * k + 1, orr * di - oi * dr)

    for k in range(4):
        backward(k)
    orr, oi = patch_now[0], patch_now[1]
    put(8, orr * orr + oi * oi)
    for s in range(4):
        for which, dest in ((c, mine), (1 - c, other)):
            owner = 2 * lax.rem(y + s, 4) + which
            start = lax.rem(owner - e0 + 1024, 8)
            for plane in range(2):
                for half in range(2):
                    rows = obj[plane, half, pl.ds(start, 32, stride=8), :]
                    dest[s, plane, :, half * H : half * H + H] = rows


def place_of(where, places, owner, pattern):
    e0 = places[pattern, 0] - where[3]
    col = places[pattern, 1]
    start = lax.rem(owner - e0 + 1024, 8)
    row = lax.shift_right_logical(e0 + 256 + start - owner, 3)
    base = pl.multiple_of(lax.shift_right_logical(row, 3) * 8, 8)
    block = pl.multiple_of(lax.shift_right_logical(col, 7) * 128, 128)
    return start, base, lax.rem(row, 8), block, lax.rem(col, 128)


def place(acc, piece, base, turn, block, shift):
    wide = pltpu.roll(jnp.concatenate([piece, jnp.zeros((32, 128), F32)], axis=1), shift, axis=1)
    wide = pltpu.roll(jnp.concatenate([wide, jnp.zeros((8, 384), F32)], axis=0), turn, axis=0)
    acc[pl.ds(base, 40), pl.ds(block, 384)] += wide


def illum_kernel(where, near, total, out, power, acc):
    owner = 2 * where[0] + where[1]
    acc[...] = jnp.zeros_like(acc)
    power[0] = total[:, :H]
    power[1] = total[:, H:]
    for pattern in range(8):
        start, base, turn, block, shift = place_of(where, near, owner, pattern)
        rows = pl.ds(start, 32, stride=8)
        piece = jnp.concatenate([power[0, rows, :], power[1, rows, :]], axis=1)
        place(acc, piece, base - 32, turn, block, shift)
    out[...] = acc[:64, :1024]


def place_kernel(where, near, light, b0, b1, b2, b3, low, high, token, acc):
    token[0, 0] = 0.0
    y, c = where[0], where[1]
    owner = 2 * y + c
    acc[...] = jnp.zeros_like(acc)
    for s in range(4):
        for which in range(2):
            pattern = 2 * lax.rem(y - s + 4, 4) + (c if which == 0 else 1 - c)
            start, base, turn, block, shift = place_of(where, near, owner, pattern)
            for plane in range(2):
                piece = (b0, b1, b2, b3)[s][which, plane]
                place(acc.at[plane], piece, base - 32, turn, block, shift)
    low[:2] = acc[:, :32, :1024]
    high[:2] = acc[:, 32:64, :1024]
    low[2] = light[:32]
    high[2] = light[32:]


def direction_kernel(
    where, near, token, low, high, above, below, band, sums, r0, r1, r2, r3, wide
):
    y, c = where[0], where[1]
    owner = 2 * y + c
    wide[...] = jnp.zeros_like(wide)
    total_a = jnp.zeros((16, 1024), F32)
    total_n = jnp.zeros((16, 1024), F32)
    for at, (own, came) in enumerate(((low, above), (high, below))):
        rows = slice(32 * at, 32 * at + 32)
        light = own[2] + came[2]
        scale = 1.0 / (light + RIDGE)
        real = (own[0] + came[0]) * scale
        imag = (own[1] + came[1]) * scale
        wide[0, rows, :1024] = real
        wide[1, rows, :1024] = imag
        inner = slice(16, 32) if at == 0 else slice(0, 16)
        real, imag, light = real[inner], imag[inner], light[inner]
        band[0, 16 * at : 16 * at + 16] = real
        band[1, 16 * at : 16 * at + 16] = imag
        size = real * real + imag * imag
        total_n += size
        total_a += light * size
    sums[0, 0] = jnp.sum(total_a)
    sums[0, 1] = jnp.sum(total_n)
    for s, dest in enumerate((r0, r1, r2, r3)):
        for which in range(2):
            pattern = 2 * lax.rem(y + s, 4) + (c if which == 0 else 1 - c)
            start, base, turn, block, shift = place_of(where, near, owner, pattern)
            for part in range(2):
                piece = wide[part, pl.ds(base - 32, 40), pl.ds(block, 384)]
                piece = pltpu.roll(piece, lax.rem(40 - turn, 40), axis=0)[:32]
                dest[which, part] = pltpu.roll(piece, lax.rem(384 - shift, 384), axis=1)[:, :N]


def stack_kernel(r0, r1, r2, r3, out):
    for s, came in enumerate((r0, r1, r2, r3)):
        out[s] = came[1]


def patch_kernel(where, near, r0, r1, r2, r3, oth, patch, dirp, kept, sent, lanes):
    y, c = where[0], where[1]
    e0 = near[2 * y + c, 0] - where[3]
    for s, came in enumerate((r0, r1, r2, r3)):
        for which in range(2):
            owner = 2 * lax.rem(y - s + 4, 4) + (c if which == 0 else 1 - c)
            rows = pl.ds(lax.rem(owner - e0 + 1024, 8), 32, stride=8)
            for part in range(2):
                piece = came[0, part] if which == 0 else oth[s, part]
                for half in range(2):
                    lanes[part, half, rows, :] = piece[:, half * H : half * H + H]
    for part in range(2):
        for half in range(2):
            dirp[part, :, half * H : half * H + H] = lanes[part, half]
    for which, dest in ((c, kept), (1 - c, sent)):
        rows = pl.ds(pl.multiple_of(which * H, H), H)
        dr, di = dirp[0, rows, :], dirp[1, rows, :]
        orr, oi = patch[0, rows, :], patch[1, rows, :]
        dest[0] = dr * orr + di * oi
        dest[1] = dr * oi - di * orr


def pack_kernel(keep, came, mine, part, chip, b0, b1, b2, b3):
    chip[...] = keep[...] + came[...]
    for s, dest in enumerate((b0, b1, b2, b3)):
        dest[0] = mine[s]
        dest[1] = part[s]


def sum_kernel(before, shares, out, token):
    out[...] = jnp.sum(shares[...], axis=0)
    token[0, 0] = 0.0


def share_kernel(own, a, b, d, above, below, spread_out, sums):
    total = own[...] + a[...] + b[...] + d[...]
    illum = total[8]
    value = total[:8] * (1.0 / (illum + RIDGE))
    spread_out[...] = jnp.broadcast_to(value[None], (16, 8, 8, N))
    size = jnp.sum(value * value, axis=0)
    sums[0, 0] = jnp.sum(size * illum)
    sums[0, 1] = jnp.sum(size)


def relay_kernel(token, gathered, out):
    for plane in range(8):
        out[plane] = gathered[:, plane].reshape(H, N)


def message_kernel(where, gathered, probe, kept, came, ae, df, out, token, half, sem):
    token[0, 0] = 0.0
    rows = pl.ds(pl.multiple_of(where[1] * H, H), H)
    copy = pltpu.make_async_copy(probe.at[:, :, rows, :], half, sem)
    copy.start()
    total = jnp.zeros((H, N), F32)
    mixed_real = kept[0] + came[0]
    mixed_imag = kept[1] + came[1]
    copy.wait()
    for k in range(4):
        dr = gathered[:, 2 * k].reshape(H, N)
        di = gathered[:, 2 * k + 1].reshape(H, N)
        pr, pi = half[k, 0], half[k, 1]
        total += mixed_real * (pr * dr + pi * di) - mixed_imag * (pr * di - pi * dr)
    cross = jnp.sum(total)
    d_sum = 0.25 * df[0, 0]
    values = (ae[0, 0], cross, d_sum, ae[0, 0] + ae[0, 1], d_sum + 0.25 * df[0, 1])
    lane = lax.broadcasted_iota(jnp.int32, (128, 128), 1)
    message = jnp.zeros((128, 128), F32)
    for at, value in enumerate(values):
        message = jnp.where(lane == at, value, message)
    out[...] = message


def combine_kernel(ready, leave, one, two, *refs):
    bands, out = refs[:8], refs[8]
    first = jnp.concatenate([step_sizes(one)[0]] * 8, axis=1)
    second = jnp.concatenate([step_sizes(two)[0]] * 8, axis=1)
    for s in range(4):
        ready(2 + s)
        ready(6 + s)
        for part in range(2):
            out[s, part] = first * bands[s][part] + second * bands[4 + s][part]
        leave(0, s)


def probe_kernel(ready, leave, where, two, probe, dmine, doth, probe_out):
    probe_step = twice(step_sizes(two)[1])
    first_core = where[1] == 0
    for k in range(4):
        for index in (2, 3, 4):
            ready(index, k)
        for part in range(2):
            moved = probe_step * joined(first_core, dmine, doth, 2 * k + part)
            probe_out[k, part] = probe[k, part] + moved
        leave(0, k)


def object_kernel(ready, leave, where, field, mine, other, out, lanes):
    y, c = where[0], where[1]
    for block in range(4):
        for index in (1, 2, 3):
            ready(index, block)
        own = slice(8 * block, 8 * block + 8)
        for s in range(4):
            for which, change in ((c, mine), (1 - c, other)):
                owner = 2 * lax.rem(y - s + 4, 4) + which
                rows = pl.ds(64 * block + owner, 8, stride=8)
                for part in range(2):
                    moved = change[s, part, own]
                    for column in range(8):
                        lanes[part, column, rows, :] = moved[:, column * H : column * H + H]
        for part in range(2):
            rows = slice(64 * block, 64 * block + 64)
            for column in range(8):
                here = slice(column * H, column * H + H)
                out[part, rows, here] = field[part, rows, here] + lanes[part, column, rows]
        leave(0, block)


def call(
    kernel,
    outs,
    args,
    smem_in,
    scratch=(),
    smem_out=(),
    hbm_out=(),
    vmem_out=(),
    hbm_in=(),
    any_in=(),
    lazy=False,
    cheap=False,
    flops=0,
    room=12,
    name=None,
):
    outs = [out if isinstance(out[0], tuple) else (out, F32) for out in outs]
    shapes = [
        pltpu.HBM(*out)
        if i in hbm_out
        else pltpu.VMEM(*out)
        if i in vmem_out
        else jax.ShapeDtypeStruct(*out)
        for i, out in enumerate(outs)
    ]
    hbm_in = hbm_in if isinstance(hbm_in, dict) else {index: 1 for index in hbm_in}
    hbm_out = hbm_out if isinstance(hbm_out, dict) else {index: 1 for index in hbm_out}
    moved = 4 * (sum(math.prod(out[0]) for out in outs) + sum(a.size for a in args))
    stage_in = [pltpu.VMEM(args[i].shape, args[i].dtype) for i in hbm_in]
    stage_out = [pltpu.VMEM(*outs[i]) for i in hbm_out]
    args = [
        pltpu.with_memory_space_constraint(a, pltpu.HBM) if i in hbm_in else a
        for i, a in enumerate(args)
    ]
    first, last = len(args), len(args) + len(outs)

    def cuts(ref, count):
        if count == 1:
            return [ref]
        count, axis = count if isinstance(count, tuple) else (count, 0)
        size = ref.shape[axis] // count
        return [
            ref.at[(slice(None),) * axis + (pl.ds(size * piece, size),)] for piece in range(count)
        ]

    def number(count):
        return count[0] if isinstance(count, tuple) else count

    def run(*refs):
        given, results = list(refs[:first]), list(refs[first:last])
        rest = refs[last:]
        staged = rest[len(scratch) : len(scratch) + len(stage_in) + len(stage_out)]
        sems = rest[-1] if staged else None
        arrivals, departures, at = {}, {}, 0
        for slot, (index, count) in enumerate(hbm_in.items()):
            stage, source = staged[slot], given[index]
            for piece, pair in enumerate(zip(cuts(source, count), cuts(stage, count))):
                copy = pltpu.make_async_copy(*pair, sems.at[at])
                copy.start()
                arrivals[index, piece] = copy
                at += 1
            given[index] = stage
        for slot, (index, count) in enumerate(hbm_out.items()):
            stage = staged[len(stage_in) + slot]
            for piece, pair in enumerate(zip(cuts(stage, count), cuts(results[index], count))):
                departures[index, piece] = pltpu.make_async_copy(*pair, sems.at[at])
                at += 1
            results[index] = stage

        def ready(index, piece=0):
            arrivals[index, piece].wait()

        def leave(index, piece=0):
            departures[index, piece].start()

        if lazy:
            kernel(ready, leave, *given, *results, *rest[: len(scratch)])
        else:
            for copy in arrivals.values():
                copy.wait()
            kernel(*given, *results, *rest[: len(scratch)])
            for copy in departures.values():
                copy.start()
        for copy in departures.values():
            copy.wait()

    def space(index, smem, hbm):
        return SMEM if index in smem else ANY if index in hbm or index in any_in else VMEM

    extra = stage_in + stage_out
    if extra:
        count = sum(number(n) for n in (*hbm_in.values(), *hbm_out.values()))
        extra.append(pltpu.SemaphoreType.DMA((count,)))
    hbm = pl.BlockSpec(memory_space=pltpu.HBM)
    return pl.pallas_call(
        run,
        out_shape=shapes,
        in_specs=[space(i, smem_in, hbm_in) for i in range(len(args))],
        out_specs=[
            hbm if i in hbm_out else SMEM if i in smem_out else VMEM for i in range(len(outs))
        ],
        scratch_shapes=[
            pltpu.VMEM(shape, F32) if shape else pltpu.SemaphoreType.DMA for shape in scratch
        ]
        + extra,
        name=name or kernel.__name__,
        compiler_params=pltpu.CompilerParams(vmem_limit_bytes=room * 2**20),
        cost_estimate=pl.CostEstimate(
            flops=flops, bytes_accessed=0 if cheap else moved, transcendentals=0
        ),
    )(*args)


def along_y(value, s):
    return lax.ppermute(value, "pat", [(i, (i + 2 * s) % 8) for i in range(8)])


def partner(value):
    return lax.ppermute(value, "pat", [(i, i ^ 1) for i in range(8)])


def up(value):
    return lax.ppermute(value, "tile", [(i, i + 1) for i in range(15)])


def down(value):
    return lax.ppermute(value, "tile", [(i + 1, i) for i in range(15)])


def spread(value, axes, count):
    return lax.all_to_all(jnp.broadcast_to(value[None], (count,) + value.shape), axes, 0, 0)


def one_hot():
    order = np.concatenate([np.arange(0, N, 2), np.arange(1, N, 2)])
    across = np.zeros((N, N), np.float32)
    across[order, np.arange(N)] = 1.0
    return np.stack([across, across.T]).astype(ml_dtypes.bfloat16)


def body(intensity, positions, object_init, probe_init):
    tile = lax.axis_index("tile")
    pat = lax.axis_index("pat")
    y, c = pat // 2, pat % 2
    top = tile * N - H
    where = jnp.stack([y, c, tile, top]).astype(jnp.int32)
    top_rows, low_rows = edges(where, pltpu.with_memory_space_constraint(object_init, pltpu.HBM))
    from_above, from_below = up(low_rows), down(top_rows)
    (news,) = call(announce_kernel, (((8, 128), jnp.int32),), (positions,), (0,), room=1)
    near = lax.all_to_all(news, "pat", 0, 0)
    table = jnp.asarray(real_tables())
    field = pltpu.with_memory_space_constraint(object_init, pltpu.HBM)
    measured, base = call(
        prepare_kernel,
        ((2, H, N), (2, N, N)),
        (where, positions, intensity[0], jnp.asarray(one_hot()), field),
        (0, 1),
        ((2, N, 384), None),
        any_in=(4,),
        room=8,
    )
    own_side, far_side = call(
        side_kernel,
        ((H, 1024), (H, 1024)),
        (where, near, base, from_above, from_below),
        (0, 1),
        any_in=(2,),
        room=4,
    )
    far_side = partner(far_side)

    probe = probe_init
    sent = (16, 9, 8, N)
    pieces = (4, 2, 32, N)
    scratch = ((4, 2, N, N), (2, H, N), (2, 2, N, H))
    outs = (sent, sent, pieces, pieces, (N, N))
    messages, bands = [], []

    for iteration in range(ITERS):
        if iteration == 0:
            patch, keep, send, mine, other, power = call(
                lambda *refs: patterns_kernel(True, *refs),
                ((2, N, N),) + outs,
                (
                    where,
                    positions,
                    base,
                    own_side,
                    far_side,
                    probe,
                    measured,
                    table,
                ),
                (0, 1),
                scratch,
                lazy=True,
                flops=6 * 10**9,
                room=28,
                name="patterns",
            )
        else:
            patch, probe, keep, send, mine, other, power = call(
                lambda *refs: patterns_kernel(False, *refs),
                ((2, N, N), (4, 2, N, N)) + outs,
                (
                    where,
                    positions,
                    messages[-1],
                    patch,
                    probe,
                    measured,
                    table,
                    dirp,
                    dmine,
                    doth,
                    *bands[0][1:],
                ),
                (0, 1),
                scratch,
                hbm_in={3: 1, 7: 1, 6: 1, 4: 4, 8: 4, 9: 4, 5: 1},
                lazy=True,
                hbm_out={0: 1, 1: 4},
                any_in=(10, 11, 12),
                flops=6 * 10**9,
                room=30,
                name="patterns",
            )
        chip, b0, b1, b2, b3 = call(
            pack_kernel,
            (sent,) + ((2, 2, 32, N),) * 4,
            (keep, partner(send), mine, partner(other)),
            (),
            hbm_out=(0, 2, 3, 4),
        )
        came = [b0, along_y(b1, 1), along_y(b2, 2), along_y(b3, 3)]
        (illum,) = call(
            illum_kernel,
            ((64, 1024),),
            (where, near, power),
            (0, 1),
            ((2, N, H), (72, 1152)),
        )
        low, high, token = call(
            place_kernel,
            ((3, 32, 1024), (3, 32, 1024), (1, 1)),
            (where, near, illum, *came),
            (0, 1),
            ((2, 72, 1152),),
            smem_out=(2,),
            hbm_out=(0, 1),
        )
        above, below = up(high), down(low)
        shares = lax.all_to_all(chip, "tile", 0, 0)
        share, token = call(
            sum_kernel, ((9, 8, N), (1, 1)), (token, shares), (0,), smem_out=(1,)
        )
        probe_dir, df = call(
            share_kernel,
            ((16, 8, 8, N), (1, 2)),
            (share, *[along_y(share, s) for s in range(1, 4)], above, below),
            (),
            smem_out=(1,),
            hbm_out=(0,),
            any_in=(4, 5),
        )
        gathered = lax.all_to_all(probe_dir, "tile", 0, 0)
        band, ae, r0, r1, r2, r3 = call(
            direction_kernel,
            ((2, 32, 1024), (1, 2)) + ((2, 2, 32, N),) * 4,
            (where, near, df, low, high, above, below),
            (0, 1, 2),
            ((2, 72, 1152),),
            smem_out=(1,),
            hbm_out=(0,),
            hbm_in=(3, 4, 5, 6),
            cheap=True,
        )
        bands.append([band] + [along_y(band, s) for s in range(1, 4)])
        back = [r0] + [along_y(r, s) for s, r in ((1, r1), (2, r2), (3, r3))]
        (oth,) = call(stack_kernel, ((4, 2, 32, N),), back, (), room=4, cheap=True)
        dirp, kept, sent_mixed = call(
            patch_kernel,
            ((2, N, N), (2, H, N), (2, H, N)),
            (where, near, *back, partner(oth), patch),
            (0, 1),
            ((2, 2, N, H),),
            cheap=True,
        )
        message, token = call(
            message_kernel,
            ((128, 128), (1, 1)),
            (
                where,
                gathered,
                pltpu.with_memory_space_constraint(probe, pltpu.HBM),
                kept,
                partner(sent_mixed),
                ae,
                df,
            ),
            (0, 5, 6),
            ((4, 2, H, N), None),
            any_in=(2,),
            smem_out=(1,),
            hbm_out=(0,),
        )
        (dmine,) = call(relay_kernel, ((8, H, N),), (token, gathered), (0,))
        doth = partner(dmine)
        messages.append(lax.all_to_all(message, BOTH, 0, 0))
    (change,) = call(
        combine_kernel,
        ((4, 2, 32, 1024),),
        (*messages, *bands[0], *bands[1]),
        (),
        hbm_in={index: 1 for index in range(2, 10)},
        hbm_out={0: 4},
        lazy=True,
    )
    change_far = partner(change)
    (probe_out,) = call(
        probe_kernel,
        (probe_init.shape,),
        (where, messages[1], probe, dmine, doth),
        (0,),
        hbm_in={2: 4, 3: 4, 4: 4},
        hbm_out={0: 4},
        lazy=True,
        flops=10**9,
    )
    (object_out,) = call(
        object_kernel,
        (object_init.shape,),
        (where, object_init, change, change_far),
        (0,),
        ((2, 8, N, H),),
        hbm_in={1: (4, 1), 2: (4, 2), 3: (4, 2)},
        hbm_out={0: (4, 1)},
        lazy=True,
        room=16,
    )
    return object_out, probe_out


def solution(mesh):
    placed = (P(("pat", "tile"), None, None), P(("pat", "tile"), None), P(None, "tile", None), P())
    return jax.shard_map(
        body, mesh=mesh, in_specs=placed, out_specs=(P(None, "tile", None), P()), check_vma=False
    )
```

```python
import math

import jax
import jax.numpy as jnp
import ml_dtypes
import numpy as np
from jax import lax
from jax.experimental import pallas as pl
from jax.experimental.pallas import tpu as pltpu
from jax.sharding import PartitionSpec as P

ITERS = 2
FLOOR = 0.5
RIDGE = 1.0
N = 256
H = 128
F32 = jnp.float32
BF16 = jnp.bfloat16
BOTH = ("pat", "tile")
VMEM = pl.BlockSpec(memory_space=pltpu.VMEM)
SMEM = pl.BlockSpec(memory_space=pltpu.SMEM)
ANY = pl.BlockSpec(memory_space=pl.ANY)


def real_tables():
    near = np.arange(H)[:, None]
    far = np.arange(H)[None, :]
    found = []
    for parity in range(2):
        angle = -2.0 * math.pi * ((near * (2 * far + parity)) % N) / N
        real, imag = np.cos(angle) / 16.0, np.sin(angle) / 16.0
        found.append(np.block([[real, imag], [-imag, real]]))
    even, odd = found
    out = []
    for table in (even, odd, even.T, odd.T):
        high = table.astype(np.float32).astype(ml_dtypes.bfloat16)
        low = (table - high.astype(np.float64)).astype(np.float32).astype(ml_dtypes.bfloat16)
        out.append(np.stack([high, low]))
    return np.stack(out)


def halves(value):
    high = value.astype(BF16)
    return high, (value - high.astype(F32)).astype(BF16)


def dot(left, right):
    return jnp.dot(left, right, preferred_element_type=F32)


def times_table(value, table):
    high, low = halves(value)
    both = dot(jnp.concatenate([high, low], axis=0), table[0])
    return both[:N] + (both[N:] + dot(high, table[1]))


def table_times(table, value):
    high, low = halves(value)
    both = dot(jnp.concatenate([table[0], table[1]], axis=0), high)
    return both[:N] + (both[N:] + dot(table[0], low))


def thirds(value):
    high, mid = halves(value)
    return high, mid, (value - high.astype(F32) - mid.astype(F32)).astype(BF16)


def step_sizes(everyone):
    total = jnp.sum(everyone[...], axis=0, keepdims=True)
    lane = lax.broadcasted_iota(jnp.int32, (1, 128), 1)
    object_power, cross_term, probe_power, object_pull, probe_pull = (
        jnp.broadcast_to(
            jnp.sum(jnp.where(lane == at, total, 0.0), axis=1, keepdims=True), (1, 128)
        )
        for at in range(5)
    )
    ridge = 0.1 * (object_power + probe_power) + 1e-06
    determinant = (object_power + ridge) * (probe_power + ridge) - cross_term * cross_term
    object_step = ((probe_power + ridge) * object_pull - cross_term * probe_pull) / determinant
    probe_step = ((object_power + ridge) * probe_pull - cross_term * object_pull) / determinant
    return object_step, probe_step


def twice(value):
    return jnp.concatenate([value, value], axis=1)


def joined(first_core, mine, other, plane):
    own, far = mine[plane], other[plane]
    return jnp.concatenate(
        [jnp.where(first_core, own, far), jnp.where(first_core, far, own)], axis=0
    )


def window_of(here):
    col = here[0, 1]
    block = pl.multiple_of(lax.min(lax.shift_right_logical(col, 7), 5) * H, H)
    return block, col - block


def cut(rows, e0, shift):
    rows = pltpu.roll(rows, lax.rem(2 * N - e0, N), axis=0)
    return pltpu.roll(rows, lax.rem(384 - shift, 384), axis=1)[:, :N]


def prepare_kernel(where, here, measured, swap, field, out, base, window, sem):
    e0 = here[0, 0] - where[3]
    block, shift = window_of(here)
    copy = pltpu.make_async_copy(field.at[:, :, pl.ds(block, 384)], window, sem)
    copy.start()
    high, mid, low = thirds(measured[...])
    across, down_rows = swap[0], swap[1]
    high, mid, low = thirds(dot(high, across) + dot(mid, across) + dot(low, across))
    value = dot(down_rows, high) + dot(down_rows, mid) + dot(down_rows, low)
    out[0] = value[:H]
    out[1] = value[H:]
    row = lax.broadcasted_iota(jnp.int32, (N, N), 0) + e0
    inside = (row >= H) & (row < H + N)
    copy.wait()
    for part in range(2):
        rows = jnp.concatenate([window[part, H:], window[part, :H]], axis=0)
        base[part] = jnp.where(inside, cut(rows, e0, shift), 0.0)


def edge_kernel(where, field, top_rows, low_rows, sems):
    c = where[1]
    copies = [
        pltpu.make_async_copy(field.at[c, pl.ds(0, H), :], top_rows, sems.at[0]),
        pltpu.make_async_copy(field.at[c, pl.ds(H, H), :], low_rows, sems.at[1]),
    ]
    for copy in copies:
        copy.start()
    for copy in copies:
        copy.wait()


def edges(where, field):
    rows = pltpu.VMEM((H, field.shape[2]), F32)
    return pl.pallas_call(
        edge_kernel,
        out_shape=[rows, rows],
        in_specs=[SMEM, ANY],
        out_specs=[VMEM, VMEM],
        scratch_shapes=[pltpu.SemaphoreType.DMA((2,))],
        compiler_params=pltpu.CompilerParams(vmem_limit_bytes=2 * 2**20),
    )(where, field)


def announce_kernel(here, out):
    lane = lax.broadcasted_iota(jnp.int32, (8, 128), 1)
    out[...] = jnp.where(lane == 0, here[0, 0], here[0, 1])


def side_kernel(where, near, base, above, below, own, far):
    y, c, top = where[0], where[1], where[3]
    own_row = near[2 * y + c, 0] - top
    far_row = near[2 * y + 1 - c, 0] - top
    own[...] = jnp.where(own_row < H, above[...], below[...])
    far[...] = jnp.where(far_row < H, above[...], below[...])


def add_side(where, here, base, own_side, far_side, patch):
    e0, first_core = here[0, 0] - where[3], where[1] == 0
    block, shift = window_of(here)
    row = lax.broadcasted_iota(jnp.int32, (N, N), 0) + e0
    outside = (row < H) | (row >= H + N)
    own, far = own_side[:, pl.ds(block, 384)], far_side[:, pl.ds(block, 384)]
    for part in range(2):
        rows = jnp.where(first_core == (part == 0), own, far)
        rows = cut(jnp.concatenate([rows, rows], axis=0), e0, shift)
        patch[part] = jnp.where(outside, rows, base[part])


def patterns_kernel(first, ready, leave, *refs):
    if first:
        where, here, base, own_side, far_side, probe_now, measured, tab = refs[:8]
        patch_now, keep, send, mine, other, power, near_rows, psi, model, obj = refs[8:]
        add_side(where, here, base, own_side, far_side, patch_now)
    else:
        where, here, everyone, patch, probe, measured, tab, dirp, dmine, doth = refs[:10]
        patch_now, probe_now = refs[13:15]
        keep, send, mine, other, power, near_rows, psi, model, obj = refs[15:]
        object_step, probe_step = map(twice, step_sizes(everyone))
        ready(3)
        ready(7)
        ready.more()
        for part in range(2):
            patch_now[part] = patch[part] + object_step * dirp[part]
        leave(0)
    y, c = where[0], where[1]
    e0 = here[0, 0] - where[3]
    first_core = c == 0
    rows_at = pl.multiple_of(H * c + 8 * where[2], 8)
    model[...] = jnp.zeros_like(model)
    obj[...] = jnp.zeros_like(obj)
    power[...] = jnp.zeros_like(power)

    def gather(plane, value):
        obj[plane, 0] += value[:, :H]
        obj[plane, 1] += value[:, H:]

    def forward(k):
        if not first:
            for index in (4, 8, 9):
                ready(index, k)
            for part in range(2):
                moved = probe_step * joined(first_core, dmine, doth, 2 * k + part)
                probe_now[k, part] = probe[k, part] + moved
            leave(1, k)
        pr, pi = probe_now[k, 0], probe_now[k, 1]
        orr, oi = patch_now[0], patch_now[1]
        power[...] += pr * pr + pi * pi
        for part in range(2):
            near_rows[2 * k + part] = probe_now[k, part, pl.ds(rows_at, 8), :]
        xr = pr * orr - pi * oi
        xi = pr * oi + pi * orr
        even = times_table(
            jnp.concatenate([xr[:, :H] + xr[:, H:], xi[:, :H] + xi[:, H:]], axis=1), tab.at[0]
        )
        odd = times_table(
            jnp.concatenate([xr[:, :H] - xr[:, H:], xi[:, :H] - xi[:, H:]], axis=1), tab.at[1]
        )
        re = jnp.concatenate([even[:, :H], odd[:, :H]], axis=1)
        im = jnp.concatenate([even[:, H:], odd[:, H:]], axis=1)
        for row, sign in ((0, 1.0), (1, -1.0)):
            folded = jnp.concatenate(
                [re[:H] + sign * re[H:], im[:H] + sign * im[H:]], axis=0
            )
            far = table_times(tab.at[2 + row], folded)
            psi[k, row] = far
            model[row] += far[:H] * far[:H] + far[H:] * far[H:]

    if not first:
        ready(6)
    for k in range(4):
        forward(k)
    if not first:
        ready(5)
    for row in range(2):
        model[row] = jnp.sqrt(measured[row] / jnp.maximum(model[row], FLOOR)) - 1.0

    def put(plane, value):
        low = value[:H].reshape(16, 8, N)
        high = value[H:].reshape(16, 8, N)
        keep[:, plane] = jnp.where(first_core, low, high)
        send[:, plane] = jnp.where(first_core, high, low)

    def backward(k):
        parts = []
        for row in range(2):
            scale = model[row]
            weighted = psi[k, row] * jnp.concatenate([scale, scale], axis=0)
            parts.append(table_times(tab.at[row], weighted))
        ee, oo = parts
        re = jnp.concatenate([ee[:H] + oo[:H], ee[:H] - oo[:H]], axis=0)
        im = jnp.concatenate([ee[H:] + oo[H:], ee[H:] - oo[H:]], axis=0)
        even = times_table(jnp.concatenate([re[:, :H], im[:, :H]], axis=1), tab.at[2])
        odd = times_table(jnp.concatenate([re[:, H:], im[:, H:]], axis=1), tab.at[3])
        dr = jnp.concatenate([even[:, :H] + odd[:, :H], even[:, :H] - odd[:, :H]], axis=1)
        di = jnp.concatenate([even[:, H:] + odd[:, H:], even[:, H:] - odd[:, H:]], axis=1)
        pr, pi = probe_now[k, 0], probe_now[k, 1]
        orr, oi = patch_now[0], patch_now[1]
        gather(0, pr * dr + pi * di)
        gather(1, pr * di - pi * dr)
        put(2 * k, orr * dr + oi * di)
        put(2 * k + 1, orr * di - oi * dr)

    for k in range(4):
        backward(k)
    orr, oi = patch_now[0], patch_now[1]
    put(8, orr * orr + oi * oi)
    for s in range(4):
        for which, dest in ((c, mine), (1 - c, other)):
            owner = 2 * lax.rem(y + s, 4) + which
            start = lax.rem(owner - e0 + 1024, 8)
            for plane in range(2):
                for half in range(2):
                    rows = obj[plane, half, pl.ds(start, 32, stride=8), :]
                    dest[s, plane, :, half * H : half * H + H] = rows


def place_of(where, places, owner, pattern):
    e0 = places[pattern, 0] - where[3]
    col = places[pattern, 1]
    start = lax.rem(owner - e0 + 1024, 8)
    row = lax.shift_right_logical(e0 + 256 + start - owner, 3)
    base = pl.multiple_of(lax.shift_right_logical(row, 3) * 8, 8)
    block = pl.multiple_of(lax.shift_right_logical(col, 7) * 128, 128)
    return start, base, lax.rem(row, 8), block, lax.rem(col, 128)


def place(acc, piece, base, turn, block, shift):
    wide = pltpu.roll(jnp.concatenate([piece, jnp.zeros((32, 128), F32)], axis=1), shift, axis=1)
    wide = pltpu.roll(jnp.concatenate([wide, jnp.zeros((8, 384), F32)], axis=0), turn, axis=0)
    acc[pl.ds(base, 40), pl.ds(block, 384)] += wide


def illum_kernel(where, near, total, out, power, acc):
    owner = 2 * where[0] + where[1]
    acc[...] = jnp.zeros_like(acc)
    power[0] = total[:, :H]
    power[1] = total[:, H:]
    for pattern in range(8):
        start, base, turn, block, shift = place_of(where, near, owner, pattern)
        rows = pl.ds(start, 32, stride=8)
        piece = jnp.concatenate([power[0, rows, :], power[1, rows, :]], axis=1)
        place(acc, piece, base - 32, turn, block, shift)
    out[...] = acc[:64, :1024]


def place_kernel(where, near, light, b0, b1, b2, b3, low, high, token, acc):
    token[0, 0] = 0.0
    y, c = where[0], where[1]
    owner = 2 * y + c
    acc[...] = jnp.zeros_like(acc)
    for s in range(4):
        for which in range(2):
            pattern = 2 * lax.rem(y - s + 4, 4) + (c if which == 0 else 1 - c)
            start, base, turn, block, shift = place_of(where, near, owner, pattern)
            for plane in range(2):
                piece = (b0, b1, b2, b3)[s][which, plane]
                place(acc.at[plane], piece, base - 32, turn, block, shift)
    low[:2] = acc[:, :32, :1024]
    high[:2] = acc[:, 32:64, :1024]
    low[2] = light[:32]
    high[2] = light[32:]


def direction_kernel(
    where, near, token, low, high, above, below, band, sums, r0, r1, r2, r3, wide
):
    y, c = where[0], where[1]
    owner = 2 * y + c
    wide[...] = jnp.zeros_like(wide)
    total_a = jnp.zeros((16, 1024), F32)
    total_n = jnp.zeros((16, 1024), F32)
    for at, (own, came) in enumerate(((low, above), (high, below))):
        rows = slice(32 * at, 32 * at + 32)
        light = own[2] + came[2]
        scale = 1.0 / (light + RIDGE)
        real = (own[0] + came[0]) * scale
        imag = (own[1] + came[1]) * scale
        wide[0, rows, :1024] = real
        wide[1, rows, :1024] = imag
        inner = slice(16, 32) if at == 0 else slice(0, 16)
        real, imag, light = real[inner], imag[inner], light[inner]
        band[0, 16 * at : 16 * at + 16] = real
        band[1, 16 * at : 16 * at + 16] = imag
        size = real * real + imag * imag
        total_n += size
        total_a += light * size
    sums[0, 0] = jnp.sum(total_a)
    sums[0, 1] = jnp.sum(total_n)
    for s, dest in enumerate((r0, r1, r2, r3)):
        for which in range(2):
            pattern = 2 * lax.rem(y + s, 4) + (c if which == 0 else 1 - c)
            start, base, turn, block, shift = place_of(where, near, owner, pattern)
            for part in range(2):
                piece = wide[part, pl.ds(base - 32, 40), pl.ds(block, 384)]
                piece = pltpu.roll(piece, lax.rem(40 - turn, 40), axis=0)[:32]
                dest[which, part] = pltpu.roll(piece, lax.rem(384 - shift, 384), axis=1)[:, :N]


def stack_kernel(r0, r1, r2, r3, out):
    for s, came in enumerate((r0, r1, r2, r3)):
        out[s] = came[1]


def patch_kernel(where, near, r0, r1, r2, r3, oth, patch, dirp, kept, sent, lanes):
    y, c = where[0], where[1]
    e0 = near[2 * y + c, 0] - where[3]
    for s, came in enumerate((r0, r1, r2, r3)):
        for which in range(2):
            owner = 2 * lax.rem(y - s + 4, 4) + (c if which == 0 else 1 - c)
            rows = pl.ds(lax.rem(owner - e0 + 1024, 8), 32, stride=8)
            for part in range(2):
                piece = came[0, part] if which == 0 else oth[s, part]
                for half in range(2):
                    lanes[part, half, rows, :] = piece[:, half * H : half * H + H]
    for part in range(2):
        for half in range(2):
            dirp[part, :, half * H : half * H + H] = lanes[part, half]
    for which, dest in ((c, kept), (1 - c, sent)):
        rows = pl.ds(pl.multiple_of(which * H, H), H)
        dr, di = dirp[0, rows, :], dirp[1, rows, :]
        orr, oi = patch[0, rows, :], patch[1, rows, :]
        dest[0] = dr * orr + di * oi
        dest[1] = dr * oi - di * orr


def pack_kernel(keep, came, mine, part, chip, b0, b1, b2, b3):
    chip[...] = keep[...] + came[...]
    for s, dest in enumerate((b0, b1, b2, b3)):
        dest[0] = mine[s]
        dest[1] = part[s]


def sum_kernel(before, shares, out, token):
    out[...] = jnp.sum(shares[...], axis=0)
    token[0, 0] = 0.0


def share_kernel(own, a, b, d, above, below, near_rows, spread_out, sums):
    total = own[...] + a[...] + b[...] + d[...]
    illum = total[8]
    value = total[:8] * (1.0 / (illum + RIDGE))
    inner_real = jnp.zeros((8, N), F32)
    inner_imag = jnp.zeros((8, N), F32)
    for k in range(4):
        pr, pi = near_rows[2 * k], near_rows[2 * k + 1]
        inner_real += pr * value[2 * k] + pi * value[2 * k + 1]
        inner_imag += pr * value[2 * k + 1] - pi * value[2 * k]
    value_out = jnp.concatenate([value, inner_real[None], inner_imag[None]], axis=0)
    spread_out[...] = jnp.broadcast_to(value_out[None], (16, 10, 8, N))
    size = jnp.sum(value * value, axis=0)
    sums[0, 0] = jnp.sum(size * illum)
    sums[0, 1] = jnp.sum(size)


def message_kernel(where, gathered, kept, came, ae, df, out, planes):
    for plane in range(8):
        planes[plane] = gathered[:, plane].reshape(H, N)
    inner_real = gathered[:, 8].reshape(H, N)
    inner_imag = gathered[:, 9].reshape(H, N)
    cross = jnp.sum((kept[0] + came[0]) * inner_real - (kept[1] + came[1]) * inner_imag)
    d_sum = 0.25 * df[0, 0]
    values = (ae[0, 0], cross, d_sum, ae[0, 0] + ae[0, 1], d_sum + 0.25 * df[0, 1])
    lane = lax.broadcasted_iota(jnp.int32, (128, 128), 1)
    message = jnp.zeros((128, 128), F32)
    for at, value in enumerate(values):
        message = jnp.where(lane == at, value, message)
    out[...] = message


def combine_kernel(ready, leave, one, two, *refs):
    bands, out = refs[:8], refs[8]
    first = jnp.concatenate([step_sizes(one)[0]] * 8, axis=1)
    second = jnp.concatenate([step_sizes(two)[0]] * 8, axis=1)
    for s in range(4):
        ready(2 + s)
        ready(6 + s)
        for part in range(2):
            out[s, part] = first * bands[s][part] + second * bands[4 + s][part]


def probe_kernel(ready, leave, where, two, probe, dmine, doth, probe_out):
    probe_step = twice(step_sizes(two)[1])
    first_core = where[1] == 0
    for k in range(4):
        ready(2, k)
        for part in range(2):
            moved = probe_step * joined(first_core, dmine, doth, 2 * k + part)
            probe_out[k, part] = probe[k, part] + moved
        leave(0, k)


def object_kernel(ready, leave, where, field, mine, other, out, lanes):
    y, c = where[0], where[1]
    for block in range(4):
        ready(1, block)
        own = slice(8 * block, 8 * block + 8)
        for s in range(4):
            for which, change in ((c, mine), (1 - c, other)):
                owner = 2 * lax.rem(y - s + 4, 4) + which
                rows = pl.ds(64 * block + owner, 8, stride=8)
                for part in range(2):
                    moved = change[s, part, own]
                    for column in range(8):
                        lanes[part, column, rows, :] = moved[:, column * H : column * H + H]
        for part in range(2):
            rows = slice(64 * block, 64 * block + 64)
            for column in range(8):
                here = slice(column * H, column * H + H)
                out[part, rows, here] = field[part, rows, here] + lanes[part, column, rows]
        leave(0, block)


def call(
    kernel,
    outs,
    args,
    smem_in,
    scratch=(),
    smem_out=(),
    hbm_out=(),
    vmem_out=(),
    hbm_in=(),
    any_in=(),
    lazy=False,
    staged_in=False,
    cheap=False,
    flops=0,
    room=12,
    name=None,
):
    outs = [out if isinstance(out[0], tuple) else (out, F32) for out in outs]
    shapes = [
        pltpu.HBM(*out)
        if i in hbm_out
        else pltpu.VMEM(*out)
        if i in vmem_out
        else jax.ShapeDtypeStruct(*out)
        for i, out in enumerate(outs)
    ]
    hbm_in = hbm_in if isinstance(hbm_in, dict) else {index: 1 for index in hbm_in}
    hbm_out = hbm_out if isinstance(hbm_out, dict) else {index: 1 for index in hbm_out}
    moved = 4 * (sum(math.prod(out[0]) for out in outs) + sum(a.size for a in args))
    stage_in = [pltpu.VMEM(args[i].shape, args[i].dtype) for i in hbm_in]
    stage_out = [pltpu.VMEM(*outs[i]) for i in hbm_out]
    args = [
        pltpu.with_memory_space_constraint(a, pltpu.HBM) if i in hbm_in else a
        for i, a in enumerate(args)
    ]
    first, last = len(args), len(args) + len(outs)

    def cuts(ref, count):
        if count == 1:
            return [ref]
        count, axis = count if isinstance(count, tuple) else (count, 0)
        size = ref.shape[axis] // count
        return [
            ref.at[(slice(None),) * axis + (pl.ds(size * piece, size),)] for piece in range(count)
        ]

    def number(count):
        return count[0] if isinstance(count, tuple) else count

    def run(*refs):
        given, results = list(refs[:first]), list(refs[first:last])
        rest = refs[last:]
        staged = rest[len(scratch) : len(scratch) + len(stage_in) + len(stage_out)]
        sems = rest[-1] if staged else None
        arrivals, departures, at = {}, {}, 0
        for slot, (index, count) in enumerate(hbm_in.items()):
            stage, source = staged[slot], given[index]
            for piece, pair in enumerate(zip(cuts(source, count), cuts(stage, count))):
                copy = pltpu.make_async_copy(*pair, sems.at[at])
                if piece < 2 or not staged_in:
                    copy.start()
                arrivals[index, piece] = copy
                at += 1
            given[index] = stage
        for slot, (index, count) in enumerate(hbm_out.items()):
            stage = staged[len(stage_in) + slot]
            for piece, pair in enumerate(zip(cuts(stage, count), cuts(results[index], count))):
                departures[index, piece] = pltpu.make_async_copy(*pair, sems.at[at])
                at += 1
            results[index] = stage

        def ready(index, piece=0):
            arrivals[index, piece].wait()

        def more():
            for (index, piece), copy in arrivals.items():
                if piece >= 2:
                    copy.start()

        ready.more = more

        def leave(index, piece=0):
            departures[index, piece].start()

        if lazy:
            kernel(ready, leave, *given, *results, *rest[: len(scratch)])
        else:
            for copy in arrivals.values():
                copy.wait()
            kernel(*given, *results, *rest[: len(scratch)])
            for copy in departures.values():
                copy.start()
        for copy in departures.values():
            copy.wait()

    def space(index, smem, hbm):
        return SMEM if index in smem else ANY if index in hbm or index in any_in else VMEM

    extra = stage_in + stage_out
    if extra:
        count = sum(number(n) for n in (*hbm_in.values(), *hbm_out.values()))
        extra.append(pltpu.SemaphoreType.DMA((count,)))
    hbm = pl.BlockSpec(memory_space=pltpu.HBM)
    return pl.pallas_call(
        run,
        out_shape=shapes,
        in_specs=[space(i, smem_in, hbm_in) for i in range(len(args))],
        out_specs=[
            hbm if i in hbm_out else SMEM if i in smem_out else VMEM for i in range(len(outs))
        ],
        scratch_shapes=[
            pltpu.VMEM(shape, F32) if shape else pltpu.SemaphoreType.DMA for shape in scratch
        ]
        + extra,
        name=name or kernel.__name__,
        compiler_params=pltpu.CompilerParams(vmem_limit_bytes=room * 2**20),
        cost_estimate=pl.CostEstimate(
            flops=flops, bytes_accessed=0 if cheap else moved, transcendentals=0
        ),
    )(*args)


def along_y(value, s):
    return lax.ppermute(value, "pat", [(i, (i + 2 * s) % 8) for i in range(8)])


def partner(value):
    return lax.ppermute(value, "pat", [(i, i ^ 1) for i in range(8)])


def up(value):
    return lax.ppermute(value, "tile", [(i, i + 1) for i in range(15)])


def down(value):
    return lax.ppermute(value, "tile", [(i + 1, i) for i in range(15)])


def spread(value, axes, count):
    return lax.all_to_all(jnp.broadcast_to(value[None], (count,) + value.shape), axes, 0, 0)


def one_hot():
    order = np.concatenate([np.arange(0, N, 2), np.arange(1, N, 2)])
    across = np.zeros((N, N), np.float32)
    across[order, np.arange(N)] = 1.0
    return np.stack([across, across.T]).astype(ml_dtypes.bfloat16)


def body(intensity, positions, object_init, probe_init):
    tile = lax.axis_index("tile")
    pat = lax.axis_index("pat")
    y, c = pat // 2, pat % 2
    top = tile * N - H
    where = jnp.stack([y, c, tile, top]).astype(jnp.int32)
    top_rows, low_rows = edges(where, pltpu.with_memory_space_constraint(object_init, pltpu.HBM))
    from_above, from_below = up(low_rows), down(top_rows)
    (news,) = call(announce_kernel, (((8, 128), jnp.int32),), (positions,), (0,), room=1)
    near = lax.all_to_all(news, "pat", 0, 0)
    table = jnp.asarray(real_tables())
    field = pltpu.with_memory_space_constraint(object_init, pltpu.HBM)
    measured, base = call(
        prepare_kernel,
        ((2, H, N), (2, N, N)),
        (where, positions, intensity[0], jnp.asarray(one_hot()), field),
        (0, 1),
        ((2, N, 384), None),
        any_in=(4,),
        room=8,
    )
    own_side, far_side = call(
        side_kernel,
        ((H, 1024), (H, 1024)),
        (where, near, base, from_above, from_below),
        (0, 1),
        any_in=(2,),
        room=4,
    )
    far_side = partner(far_side)

    probe = probe_init
    sent = (16, 9, 8, N)
    pieces = (4, 2, 32, N)
    scratch = ((4, 2, N, N), (2, H, N), (2, 2, N, H))
    outs = (sent, sent, pieces, pieces, (N, N), (8, 8, N))
    messages, bands = [], []

    for iteration in range(ITERS):
        if iteration == 0:
            patch, keep, send, mine, other, power, near_rows = call(
                lambda *refs: patterns_kernel(True, *refs),
                ((2, N, N),) + outs,
                (
                    where,
                    positions,
                    base,
                    own_side,
                    far_side,
                    probe,
                    measured,
                    table,
                ),
                (0, 1),
                scratch,
                lazy=True,
                flops=6 * 10**9,
                room=28,
                name="patterns",
            )
        else:
            patch, probe, keep, send, mine, other, power, near_rows = call(
                lambda *refs: patterns_kernel(False, *refs),
                ((2, N, N), (4, 2, N, N)) + outs,
                (
                    where,
                    positions,
                    messages[-1],
                    patch,
                    probe,
                    measured,
                    table,
                    dirp,
                    dmine,
                    doth,
                    *bands[0][1:],
                ),
                (0, 1),
                scratch,
                hbm_in={3: 1, 7: 1, 6: 1, 4: 4, 8: 4, 9: 4, 5: 1},
                staged_in=True,
                lazy=True,
                hbm_out={0: 1, 1: 4},
                any_in=(10, 11, 12),
                flops=6 * 10**9,
                room=30,
                name="patterns",
            )
        chip, b0, b1, b2, b3 = call(
            pack_kernel,
            (sent,) + ((2, 2, 32, N),) * 4,
            (keep, partner(send), mine, partner(other)),
            (),
            hbm_out=(0,),
        )
        came = [b0, along_y(b1, 1), along_y(b2, 2), along_y(b3, 3)]
        (illum,) = call(
            illum_kernel,
            ((64, 1024),),
            (where, near, power),
            (0, 1),
            ((2, N, H), (72, 1152)),
        )
        low, high, token = call(
            place_kernel,
            ((3, 32, 1024), (3, 32, 1024), (1, 1)),
            (where, near, illum, *came),
            (0, 1),
            ((2, 72, 1152),),
            smem_out=(2,),
        )
        above, below = up(high), down(low)
        shares = lax.all_to_all(chip, "tile", 0, 0)
        share, token = call(
            sum_kernel, ((9, 8, N), (1, 1)), (token, shares), (0,), smem_out=(1,)
        )
        probe_dir, df = call(
            share_kernel,
            ((16, 10, 8, N), (1, 2)),
            (share, *[along_y(share, s) for s in range(1, 4)], above, below, near_rows),
            (),
            smem_out=(1,),
            hbm_out=(0,),
            any_in=(4, 5),
        )
        gathered = lax.all_to_all(probe_dir, "tile", 0, 0)
        band, ae, r0, r1, r2, r3 = call(
            direction_kernel,
            ((2, 32, 1024), (1, 2)) + ((2, 2, 32, N),) * 4,
            (where, near, df, low, high, above, below),
            (0, 1, 2),
            ((2, 72, 1152),),
            smem_out=(1,),
            cheap=True,
        )
        bands.append([band] + [along_y(band, s) for s in range(1, 4)])
        back = [r0] + [along_y(r, s) for s, r in ((1, r1), (2, r2), (3, r3))]
        (oth,) = call(stack_kernel, ((4, 2, 32, N),), back, (), room=4, cheap=True)
        dirp, kept, sent_mixed = call(
            patch_kernel,
            ((2, N, N), (2, H, N), (2, H, N)),
            (where, near, *back, partner(oth), patch),
            (0, 1),
            ((2, 2, N, H),),
            cheap=True,
        )
        message, dmine = call(
            message_kernel,
            ((128, 128), (8, H, N)),
            (where, gathered, kept, partner(sent_mixed), ae, df),
            (0, 4, 5),
            hbm_out=(0,),
        )
        doth = partner(dmine)
        messages.append(lax.all_to_all(message, BOTH, 0, 0))
    (change,) = call(
        combine_kernel,
        ((4, 2, 32, 1024),),
        (*messages, *bands[0], *bands[1]),
        (),
        hbm_in={index: 1 for index in range(2, 10)},
        lazy=True,
    )
    change_far = partner(change)
    (probe_out,) = call(
        probe_kernel,
        (probe_init.shape,),
        (where, messages[1], probe, dmine, doth),
        (0,),
        hbm_in={2: 4},
        hbm_out={0: 4},
        lazy=True,
        flops=10**9,
    )
    (object_out,) = call(
        object_kernel,
        (object_init.shape,),
        (where, object_init, change, change_far),
        (0,),
        ((2, 8, N, H),),
        hbm_in={1: (4, 1)},
        hbm_out={0: (4, 1)},
        lazy=True,
        room=16,
    )
    return object_out, probe_out


def solution(mesh):
    placed = (P(("pat", "tile"), None, None), P(("pat", "tile"), None), P(None, "tile", None), P())
    return jax.shard_map(
        body, mesh=mesh, in_specs=placed, out_specs=(P(None, "tile", None), P()), check_vma=False
    )
```

```python
import math

import jax
import jax.numpy as jnp
import ml_dtypes
import numpy as np
from jax import lax
from jax.experimental import pallas as pl
from jax.experimental.pallas import tpu as pltpu
from jax.sharding import PartitionSpec as P

ITERS = 2
FLOOR = 0.5
RIDGE = 1.0
N = 256
H = 128
F32 = jnp.float32
BF16 = jnp.bfloat16
BOTH = ("pat", "tile")
VMEM = pl.BlockSpec(memory_space=pltpu.VMEM)
SMEM = pl.BlockSpec(memory_space=pltpu.SMEM)
ANY = pl.BlockSpec(memory_space=pl.ANY)


def real_tables():
    near = np.arange(H)[:, None]
    far = np.arange(H)[None, :]
    found = []
    for parity in range(2):
        angle = -2.0 * math.pi * ((near * (2 * far + parity)) % N) / N
        real, imag = np.cos(angle) / 16.0, np.sin(angle) / 16.0
        found.append(np.block([[real, imag], [-imag, real]]))
    even, odd = found
    out = []
    for table in (even, odd, even.T, odd.T):
        high = table.astype(np.float32).astype(ml_dtypes.bfloat16)
        low = (table - high.astype(np.float64)).astype(np.float32).astype(ml_dtypes.bfloat16)
        out.append(np.stack([high, low]))
    return np.stack(out)


def halves(value):
    high = value.astype(BF16)
    return high, (value - high.astype(F32)).astype(BF16)


def dot(left, right):
    return jnp.dot(left, right, preferred_element_type=F32)


def times_table(value, table):
    high, low = halves(value)
    both = dot(jnp.concatenate([high, low], axis=0), table[0])
    return both[:N] + (both[N:] + dot(high, table[1]))


def table_times(table, value):
    high, low = halves(value)
    both = dot(jnp.concatenate([table[0], table[1]], axis=0), high)
    return both[:N] + (both[N:] + dot(table[0], low))


def thirds(value):
    high, mid = halves(value)
    return high, mid, (value - high.astype(F32) - mid.astype(F32)).astype(BF16)


def step_sizes(everyone):
    total = jnp.sum(everyone[...], axis=0, keepdims=True)
    lane = lax.broadcasted_iota(jnp.int32, (1, 128), 1)
    object_power, cross_term, probe_power, object_pull, probe_pull = (
        jnp.broadcast_to(
            jnp.sum(jnp.where(lane == at, total, 0.0), axis=1, keepdims=True), (1, 128)
        )
        for at in range(5)
    )
    ridge = 0.1 * (object_power + probe_power) + 1e-06
    determinant = (object_power + ridge) * (probe_power + ridge) - cross_term * cross_term
    object_step = ((probe_power + ridge) * object_pull - cross_term * probe_pull) / determinant
    probe_step = ((object_power + ridge) * probe_pull - cross_term * object_pull) / determinant
    return object_step, probe_step


def twice(value):
    return jnp.concatenate([value, value], axis=1)


def joined(first_core, mine, other, plane):
    own, far = mine[plane], other[plane]
    return jnp.concatenate(
        [jnp.where(first_core, own, far), jnp.where(first_core, far, own)], axis=0
    )


def window_of(here):
    col = here[0, 1]
    block = pl.multiple_of(lax.min(lax.shift_right_logical(col, 7), 5) * H, H)
    return block, col - block


def cut(rows, e0, shift):
    rows = pltpu.roll(rows, lax.rem(2 * N - e0, N), axis=0)
    return pltpu.roll(rows, lax.rem(384 - shift, 384), axis=1)[:, :N]


def prepare_kernel(where, here, measured, swap, field, out, base, window, sem):
    e0 = here[0, 0] - where[3]
    block, shift = window_of(here)
    copy = pltpu.make_async_copy(field.at[:, :, pl.ds(block, 384)], window, sem)
    copy.start()
    high, mid, low = thirds(measured[...])
    across, down_rows = swap[0], swap[1]
    high, mid, low = thirds(dot(high, across) + dot(mid, across) + dot(low, across))
    value = dot(down_rows, high) + dot(down_rows, mid) + dot(down_rows, low)
    out[0] = value[:H]
    out[1] = value[H:]
    row = lax.broadcasted_iota(jnp.int32, (N, N), 0) + e0
    inside = (row >= H) & (row < H + N)
    copy.wait()
    for part in range(2):
        rows = jnp.concatenate([window[part, H:], window[part, :H]], axis=0)
        base[part] = jnp.where(inside, cut(rows, e0, shift), 0.0)


def edge_kernel(where, field, top_rows, low_rows, sems):
    c = where[1]
    copies = [
        pltpu.make_async_copy(field.at[c, pl.ds(0, H), :], top_rows, sems.at[0]),
        pltpu.make_async_copy(field.at[c, pl.ds(H, H), :], low_rows, sems.at[1]),
    ]
    for copy in copies:
        copy.start()
    for copy in copies:
        copy.wait()


def edges(where, field):
    rows = pltpu.VMEM((H, field.shape[2]), F32)
    return pl.pallas_call(
        edge_kernel,
        out_shape=[rows, rows],
        in_specs=[SMEM, ANY],
        out_specs=[VMEM, VMEM],
        scratch_shapes=[pltpu.SemaphoreType.DMA((2,))],
        compiler_params=pltpu.CompilerParams(vmem_limit_bytes=2 * 2**20),
    )(where, field)


def announce_kernel(here, out):
    lane = lax.broadcasted_iota(jnp.int32, (8, 128), 1)
    out[...] = jnp.where(lane == 0, here[0, 0], here[0, 1])


def side_kernel(where, near, base, above, below, own, far):
    y, c, top = where[0], where[1], where[3]
    own_row = near[2 * y + c, 0] - top
    far_row = near[2 * y + 1 - c, 0] - top
    own[...] = jnp.where(own_row < H, above[...], below[...])
    far[...] = jnp.where(far_row < H, above[...], below[...])


def add_side(where, here, base, own_side, far_side, patch):
    e0, first_core = here[0, 0] - where[3], where[1] == 0
    block, shift = window_of(here)
    row = lax.broadcasted_iota(jnp.int32, (N, N), 0) + e0
    outside = (row < H) | (row >= H + N)
    own, far = own_side[:, pl.ds(block, 384)], far_side[:, pl.ds(block, 384)]
    for part in range(2):
        rows = jnp.where(first_core == (part == 0), own, far)
        rows = cut(jnp.concatenate([rows, rows], axis=0), e0, shift)
        patch[part] = jnp.where(outside, rows, base[part])


def patterns_kernel(first, ready, leave, *refs):
    if first:
        where, here, base, own_side, far_side, probe_now, measured, tab = refs[:8]
        patch_now, keep, send, mine, other, power, near_rows, psi, model, obj = refs[8:]
        add_side(where, here, base, own_side, far_side, patch_now)
    else:
        where, here, everyone, patch, probe, measured, tab, dirp, dmine, doth = refs[:10]
        patch_now, probe_now = refs[13:15]
        keep, send, mine, other, power, near_rows, psi, model, obj = refs[15:]
        object_step, probe_step = map(twice, step_sizes(everyone))
        ready(3)
        ready(7)
        ready.more()
        for part in range(2):
            patch_now[part] = patch[part] + object_step * dirp[part]
        leave(0)
    y, c = where[0], where[1]
    e0 = here[0, 0] - where[3]
    first_core = c == 0
    rows_at = pl.multiple_of(H * c + 8 * where[2], 8)
    model[...] = jnp.zeros_like(model)
    obj[...] = jnp.zeros_like(obj)
    power[...] = jnp.zeros_like(power)

    def gather(plane, value):
        obj[plane, 0] += value[:, :H]
        obj[plane, 1] += value[:, H:]

    def forward(k):
        if not first:
            ready(4, k)
            for part in range(2):
                moved = probe_step * joined(first_core, dmine, doth, 2 * k + part)
                probe_now[k, part] = probe[k, part] + moved
            leave(1, k)
        pr, pi = probe_now[k, 0], probe_now[k, 1]
        orr, oi = patch_now[0], patch_now[1]
        power[...] += pr * pr + pi * pi
        for part in range(2):
            near_rows[2 * k + part] = probe_now[k, part, pl.ds(rows_at, 8), :]
        xr = pr * orr - pi * oi
        xi = pr * oi + pi * orr
        even = times_table(
            jnp.concatenate([xr[:, :H] + xr[:, H:], xi[:, :H] + xi[:, H:]], axis=1), tab.at[0]
        )
        odd = times_table(
            jnp.concatenate([xr[:, :H] - xr[:, H:], xi[:, :H] - xi[:, H:]], axis=1), tab.at[1]
        )
        re = jnp.concatenate([even[:, :H], odd[:, :H]], axis=1)
        im = jnp.concatenate([even[:, H:], odd[:, H:]], axis=1)
        for row, sign in ((0, 1.0), (1, -1.0)):
            folded = jnp.concatenate(
                [re[:H] + sign * re[H:], im[:H] + sign * im[H:]], axis=0
            )
            far = table_times(tab.at[2 + row], folded)
            psi[k, row] = far
            model[row] += far[:H] * far[:H] + far[H:] * far[H:]

    if not first:
        ready(6)
    for k in range(4):
        forward(k)
    if not first:
        ready(5)
    for row in range(2):
        model[row] = jnp.sqrt(measured[row] / jnp.maximum(model[row], FLOOR)) - 1.0

    def put(plane, value):
        low = value[:H].reshape(16, 8, N)
        high = value[H:].reshape(16, 8, N)
        keep[:, plane] = jnp.where(first_core, low, high)
        send[:, plane] = jnp.where(first_core, high, low)

    def backward(k):
        parts = []
        for row in range(2):
            scale = model[row]
            weighted = psi[k, row] * jnp.concatenate([scale, scale], axis=0)
            parts.append(table_times(tab.at[row], weighted))
        ee, oo = parts
        re = jnp.concatenate([ee[:H] + oo[:H], ee[:H] - oo[:H]], axis=0)
        im = jnp.concatenate([ee[H:] + oo[H:], ee[H:] - oo[H:]], axis=0)
        even = times_table(jnp.concatenate([re[:, :H], im[:, :H]], axis=1), tab.at[2])
        odd = times_table(jnp.concatenate([re[:, H:], im[:, H:]], axis=1), tab.at[3])
        dr = jnp.concatenate([even[:, :H] + odd[:, :H], even[:, :H] - odd[:, :H]], axis=1)
        di = jnp.concatenate([even[:, H:] + odd[:, H:], even[:, H:] - odd[:, H:]], axis=1)
        pr, pi = probe_now[k, 0], probe_now[k, 1]
        orr, oi = patch_now[0], patch_now[1]
        gather(0, pr * dr + pi * di)
        gather(1, pr * di - pi * dr)
        put(2 * k, orr * dr + oi * di)
        put(2 * k + 1, orr * di - oi * dr)

    for k in range(4):
        backward(k)
    orr, oi = patch_now[0], patch_now[1]
    put(8, orr * orr + oi * oi)
    for s in range(4):
        for which, dest in ((c, mine), (1 - c, other)):
            owner = 2 * lax.rem(y + s, 4) + which
            start = lax.rem(owner - e0 + 1024, 8)
            for plane in range(2):
                for half in range(2):
                    rows = obj[plane, half, pl.ds(start, 32, stride=8), :]
                    dest[s, plane, :, half * H : half * H + H] = rows


def place_of(where, places, owner, pattern):
    e0 = places[pattern, 0] - where[3]
    col = places[pattern, 1]
    start = lax.rem(owner - e0 + 1024, 8)
    row = lax.shift_right_logical(e0 + 256 + start - owner, 3)
    base = pl.multiple_of(lax.shift_right_logical(row, 3) * 8, 8)
    block = pl.multiple_of(lax.shift_right_logical(col, 7) * 128, 128)
    return start, base, lax.rem(row, 8), block, lax.rem(col, 128)


def place(acc, piece, base, turn, block, shift):
    wide = pltpu.roll(jnp.concatenate([piece, jnp.zeros((32, 128), F32)], axis=1), shift, axis=1)
    wide = pltpu.roll(jnp.concatenate([wide, jnp.zeros((8, 384), F32)], axis=0), turn, axis=0)
    acc[pl.ds(base, 40), pl.ds(block, 384)] += wide


def illum_kernel(where, near, total, out, power, acc):
    owner = 2 * where[0] + where[1]
    acc[...] = jnp.zeros_like(acc)
    power[0] = total[:, :H]
    power[1] = total[:, H:]
    for pattern in range(8):
        start, base, turn, block, shift = place_of(where, near, owner, pattern)
        rows = pl.ds(start, 32, stride=8)
        piece = jnp.concatenate([power[0, rows, :], power[1, rows, :]], axis=1)
        place(acc, piece, base - 32, turn, block, shift)
    out[...] = acc[:64, :1024]


def place_kernel(where, near, light, b0, b1, b2, b3, low, high, token, acc):
    token[0, 0] = 0.0
    y, c = where[0], where[1]
    owner = 2 * y + c
    acc[...] = jnp.zeros_like(acc)
    for s in range(4):
        for which in range(2):
            pattern = 2 * lax.rem(y - s + 4, 4) + (c if which == 0 else 1 - c)
            start, base, turn, block, shift = place_of(where, near, owner, pattern)
            for plane in range(2):
                piece = (b0, b1, b2, b3)[s][which, plane]
                place(acc.at[plane], piece, base - 32, turn, block, shift)
    low[:2] = acc[:, :32, :1024]
    high[:2] = acc[:, 32:64, :1024]
    low[2] = light[:32]
    high[2] = light[32:]


def direction_kernel(
    where, near, token, low, high, above, below, band, sums, r0, r1, r2, r3, wide
):
    y, c = where[0], where[1]
    owner = 2 * y + c
    wide[...] = jnp.zeros_like(wide)
    total_a = jnp.zeros((16, 1024), F32)
    total_n = jnp.zeros((16, 1024), F32)
    for at, (own, came) in enumerate(((low, above), (high, below))):
        rows = slice(32 * at, 32 * at + 32)
        inside = where[2] != 15 * at
        total = own[...] + jnp.where(inside, came[...], 0.0)
        light = total[2]
        scale = 1.0 / (light + RIDGE)
        real = total[0] * scale
        imag = total[1] * scale
        wide[0, rows, :1024] = real
        wide[1, rows, :1024] = imag
        inner = slice(16, 32) if at == 0 else slice(0, 16)
        real, imag, light = real[inner], imag[inner], light[inner]
        band[0, 16 * at : 16 * at + 16] = real
        band[1, 16 * at : 16 * at + 16] = imag
        size = real * real + imag * imag
        total_n += size
        total_a += light * size
    sums[0, 0] = jnp.sum(total_a)
    sums[0, 1] = jnp.sum(total_n)
    for s, dest in enumerate((r0, r1, r2, r3)):
        for which in range(2):
            pattern = 2 * lax.rem(y + s, 4) + (c if which == 0 else 1 - c)
            start, base, turn, block, shift = place_of(where, near, owner, pattern)
            for part in range(2):
                piece = wide[part, pl.ds(base - 32, 40), pl.ds(block, 384)]
                piece = pltpu.roll(piece, lax.rem(40 - turn, 40), axis=0)[:32]
                dest[which, part] = pltpu.roll(piece, lax.rem(384 - shift, 384), axis=1)[:, :N]


def stack_kernel(r0, r1, r2, r3, out):
    for s, came in enumerate((r0, r1, r2, r3)):
        out[s] = came[1]


def patch_kernel(where, near, r0, r1, r2, r3, oth, patch, dirp, kept, sent, lanes):
    y, c = where[0], where[1]
    e0 = near[2 * y + c, 0] - where[3]
    for s, came in enumerate((r0, r1, r2, r3)):
        for which in range(2):
            owner = 2 * lax.rem(y - s + 4, 4) + (c if which == 0 else 1 - c)
            rows = pl.ds(lax.rem(owner - e0 + 1024, 8), 32, stride=8)
            for part in range(2):
                piece = came[0, part] if which == 0 else oth[s, part]
                for half in range(2):
                    lanes[part, half, rows, :] = piece[:, half * H : half * H + H]
    for part in range(2):
        for half in range(2):
            dirp[part, :, half * H : half * H + H] = lanes[part, half]
    for which, dest in ((c, kept), (1 - c, sent)):
        rows = pl.ds(pl.multiple_of(which * H, H), H)
        dr, di = dirp[0, rows, :], dirp[1, rows, :]
        orr, oi = patch[0, rows, :], patch[1, rows, :]
        dest[0] = dr * orr + di * oi
        dest[1] = dr * oi - di * orr


def pack_kernel(keep, came, mine, part, chip, b0, b1, b2, b3):
    chip[...] = keep[...] + came[...]
    for s, dest in enumerate((b0, b1, b2, b3)):
        dest[0] = mine[s]
        dest[1] = part[s]


def sum_kernel(before, shares, out, token):
    out[...] = jnp.sum(shares[...], axis=0)
    token[0, 0] = 0.0


def share_kernel(own, a, b, d, above, below, near_rows, spread_out, sums):
    total = own[...] + a[...] + b[...] + d[...]
    illum = total[8]
    value = total[:8] * (1.0 / (illum + RIDGE))
    inner_real = jnp.zeros((8, N), F32)
    inner_imag = jnp.zeros((8, N), F32)
    for k in range(4):
        pr, pi = near_rows[2 * k], near_rows[2 * k + 1]
        inner_real += pr * value[2 * k] + pi * value[2 * k + 1]
        inner_imag += pr * value[2 * k + 1] - pi * value[2 * k]
    value_out = jnp.concatenate([value, inner_real[None], inner_imag[None]], axis=0)
    spread_out[...] = jnp.broadcast_to(value_out[None], (16, 10, 8, N))
    size = jnp.sum(value * value, axis=0)
    sums[0, 0] = jnp.sum(size * illum)
    sums[0, 1] = jnp.sum(size)


def message_kernel(where, gathered, kept, came, ae, df, out, planes):
    for plane in range(8):
        planes[plane] = gathered[:, plane].reshape(H, N)
    inner_real = gathered[:, 8].reshape(H, N)
    inner_imag = gathered[:, 9].reshape(H, N)
    cross = jnp.sum((kept[0] + came[0]) * inner_real - (kept[1] + came[1]) * inner_imag)
    d_sum = 0.25 * df[0, 0]
    values = (ae[0, 0], cross, d_sum, ae[0, 0] + ae[0, 1], d_sum + 0.25 * df[0, 1])
    lane = lax.broadcasted_iota(jnp.int32, (128, 128), 1)
    message = jnp.zeros((128, 128), F32)
    for at, value in enumerate(values):
        message = jnp.where(lane == at, value, message)
    out[...] = message


def combine_kernel(ready, leave, one, two, *refs):
    bands, out = refs[:8], refs[8]
    first = jnp.concatenate([step_sizes(one)[0]] * 8, axis=1)
    second = jnp.concatenate([step_sizes(two)[0]] * 8, axis=1)
    for s in range(4):
        ready(2 + s)
        ready(6 + s)
        for part in range(2):
            out[s, part] = first * bands[s][part] + second * bands[4 + s][part]


def probe_kernel(ready, leave, where, two, probe, dmine, doth, probe_out):
    probe_step = twice(step_sizes(two)[1])
    first_core = where[1] == 0
    for k in range(4):
        ready(2, k)
        for part in range(2):
            moved = probe_step * joined(first_core, dmine, doth, 2 * k + part)
            probe_out[k, part] = probe[k, part] + moved
        leave(0, k)


def object_kernel(ready, leave, where, field, mine, other, out, lanes):
    y, c = where[0], where[1]
    for block in range(4):
        ready(1, block)
        own = slice(8 * block, 8 * block + 8)
        for s in range(4):
            for which, change in ((c, mine), (1 - c, other)):
                owner = 2 * lax.rem(y - s + 4, 4) + which
                rows = pl.ds(64 * block + owner, 8, stride=8)
                for part in range(2):
                    moved = change[s, part, own]
                    for column in range(8):
                        lanes[part, column, rows, :] = moved[:, column * H : column * H + H]
        for part in range(2):
            rows = slice(64 * block, 64 * block + 64)
            for column in range(8):
                here = slice(column * H, column * H + H)
                out[part, rows, here] = field[part, rows, here] + lanes[part, column, rows]
        leave(0, block)


def call(
    kernel,
    outs,
    args,
    smem_in,
    scratch=(),
    smem_out=(),
    hbm_out=(),
    vmem_out=(),
    hbm_in=(),
    any_in=(),
    lazy=False,
    staged_in=False,
    cheap=False,
    flops=0,
    room=12,
    name=None,
):
    outs = [out if isinstance(out[0], tuple) else (out, F32) for out in outs]
    shapes = [
        pltpu.HBM(*out)
        if i in hbm_out
        else pltpu.VMEM(*out)
        if i in vmem_out
        else jax.ShapeDtypeStruct(*out)
        for i, out in enumerate(outs)
    ]
    hbm_in = hbm_in if isinstance(hbm_in, dict) else {index: 1 for index in hbm_in}
    hbm_out = hbm_out if isinstance(hbm_out, dict) else {index: 1 for index in hbm_out}
    moved = 4 * (sum(math.prod(out[0]) for out in outs) + sum(a.size for a in args))
    stage_in = [pltpu.VMEM(args[i].shape, args[i].dtype) for i in hbm_in]
    stage_out = [pltpu.VMEM(*outs[i]) for i in hbm_out]
    args = [
        pltpu.with_memory_space_constraint(a, pltpu.HBM) if i in hbm_in else a
        for i, a in enumerate(args)
    ]
    first, last = len(args), len(args) + len(outs)

    def cuts(ref, count):
        if count == 1:
            return [ref]
        count, axis = count if isinstance(count, tuple) else (count, 0)
        size = ref.shape[axis] // count
        return [
            ref.at[(slice(None),) * axis + (pl.ds(size * piece, size),)] for piece in range(count)
        ]

    def number(count):
        return count[0] if isinstance(count, tuple) else count

    def run(*refs):
        given, results = list(refs[:first]), list(refs[first:last])
        rest = refs[last:]
        staged = rest[len(scratch) : len(scratch) + len(stage_in) + len(stage_out)]
        sems = rest[-1] if staged else None
        arrivals, departures, at = {}, {}, 0
        for slot, (index, count) in enumerate(hbm_in.items()):
            stage, source = staged[slot], given[index]
            for piece, pair in enumerate(zip(cuts(source, count), cuts(stage, count))):
                copy = pltpu.make_async_copy(*pair, sems.at[at])
                if piece < 2 or not staged_in:
                    copy.start()
                arrivals[index, piece] = copy
                at += 1
            given[index] = stage
        for slot, (index, count) in enumerate(hbm_out.items()):
            stage = staged[len(stage_in) + slot]
            for piece, pair in enumerate(zip(cuts(stage, count), cuts(results[index], count))):
                departures[index, piece] = pltpu.make_async_copy(*pair, sems.at[at])
                at += 1
            results[index] = stage

        def ready(index, piece=0):
            arrivals[index, piece].wait()

        def more():
            for (index, piece), copy in arrivals.items():
                if piece >= 2:
                    copy.start()

        ready.more = more

        def leave(index, piece=0):
            departures[index, piece].start()

        if lazy:
            kernel(ready, leave, *given, *results, *rest[: len(scratch)])
        else:
            for copy in arrivals.values():
                copy.wait()
            kernel(*given, *results, *rest[: len(scratch)])
            for copy in departures.values():
                copy.start()
        for copy in departures.values():
            copy.wait()

    def space(index, smem, hbm):
        return SMEM if index in smem else ANY if index in hbm or index in any_in else VMEM

    extra = stage_in + stage_out
    if extra:
        count = sum(number(n) for n in (*hbm_in.values(), *hbm_out.values()))
        extra.append(pltpu.SemaphoreType.DMA((count,)))
    hbm = pl.BlockSpec(memory_space=pltpu.HBM)
    return pl.pallas_call(
        run,
        out_shape=shapes,
        in_specs=[space(i, smem_in, hbm_in) for i in range(len(args))],
        out_specs=[
            hbm if i in hbm_out else SMEM if i in smem_out else VMEM for i in range(len(outs))
        ],
        scratch_shapes=[
            pltpu.VMEM(shape, F32) if shape else pltpu.SemaphoreType.DMA for shape in scratch
        ]
        + extra,
        name=name or kernel.__name__,
        compiler_params=pltpu.CompilerParams(vmem_limit_bytes=room * 2**20),
        cost_estimate=pl.CostEstimate(
            flops=flops, bytes_accessed=0 if cheap else moved, transcendentals=0
        ),
    )(*args)


def along_y(value, s):
    return lax.ppermute(value, "pat", [(i, (i + 2 * s) % 8) for i in range(8)])


def partner(value):
    return lax.ppermute(value, "pat", [(i, i ^ 1) for i in range(8)])


def up(value):
    return lax.ppermute(value, "tile", [(i, (i + 1) % 16) for i in range(16)])


def down(value):
    return lax.ppermute(value, "tile", [((i + 1) % 16, i) for i in range(16)])


def spread(value, axes, count):
    return lax.all_to_all(jnp.broadcast_to(value[None], (count,) + value.shape), axes, 0, 0)


def one_hot():
    order = np.concatenate([np.arange(0, N, 2), np.arange(1, N, 2)])
    across = np.zeros((N, N), np.float32)
    across[order, np.arange(N)] = 1.0
    return np.stack([across, across.T]).astype(ml_dtypes.bfloat16)


def body(intensity, positions, object_init, probe_init):
    tile = lax.axis_index("tile")
    pat = lax.axis_index("pat")
    y, c = pat // 2, pat % 2
    top = tile * N - H
    where = jnp.stack([y, c, tile, top]).astype(jnp.int32)
    top_rows, low_rows = edges(where, pltpu.with_memory_space_constraint(object_init, pltpu.HBM))
    from_above, from_below = up(low_rows), down(top_rows)
    (news,) = call(announce_kernel, (((8, 128), jnp.int32),), (positions,), (0,), room=1)
    near = lax.all_to_all(news, "pat", 0, 0)
    table = jnp.asarray(real_tables())
    field = pltpu.with_memory_space_constraint(object_init, pltpu.HBM)
    measured, base = call(
        prepare_kernel,
        ((2, H, N), (2, N, N)),
        (where, positions, intensity[0], jnp.asarray(one_hot()), field),
        (0, 1),
        ((2, N, 384), None),
        any_in=(4,),
        room=8,
    )
    own_side, far_side = call(
        side_kernel,
        ((H, 1024), (H, 1024)),
        (where, near, base, from_above, from_below),
        (0, 1),
        any_in=(2,),
        room=4,
    )
    far_side = partner(far_side)

    probe = probe_init
    sent = (16, 9, 8, N)
    pieces = (4, 2, 32, N)
    scratch = ((4, 2, N, N), (2, H, N), (2, 2, N, H))
    outs = (sent, sent, pieces, pieces, (N, N), (8, 8, N))
    messages, bands = [], []

    for iteration in range(ITERS):
        if iteration == 0:
            patch, keep, send, mine, other, power, near_rows = call(
                lambda *refs: patterns_kernel(True, *refs),
                ((2, N, N),) + outs,
                (
                    where,
                    positions,
                    base,
                    own_side,
                    far_side,
                    probe,
                    measured,
                    table,
                ),
                (0, 1),
                scratch,
                lazy=True,
                flops=6 * 10**9,
                room=28,
                name="patterns",
            )
        else:
            patch, probe, keep, send, mine, other, power, near_rows = call(
                lambda *refs: patterns_kernel(False, *refs),
                ((2, N, N), (4, 2, N, N)) + outs,
                (
                    where,
                    positions,
                    messages[-1],
                    patch,
                    probe,
                    measured,
                    table,
                    dirp,
                    dmine,
                    doth,
                    *bands[0][1:],
                ),
                (0, 1),
                scratch,
                hbm_in={3: 1, 7: 1, 6: 1, 4: 4, 5: 1},
                staged_in=True,
                lazy=True,
                hbm_out={0: 1, 1: 4},
                any_in=(10, 11, 12),
                flops=6 * 10**9,
                room=30,
                name="patterns",
            )
        chip, b0, b1, b2, b3 = call(
            pack_kernel,
            (sent,) + ((2, 2, 32, N),) * 4,
            (keep, partner(send), mine, partner(other)),
            (),
            hbm_out=(0,),
        )
        came = [b0, along_y(b1, 1), along_y(b2, 2), along_y(b3, 3)]
        (illum,) = call(
            illum_kernel,
            ((64, 1024),),
            (where, near, power),
            (0, 1),
            ((2, N, H), (72, 1152)),
        )
        low, high, token = call(
            place_kernel,
            ((3, 32, 1024), (3, 32, 1024), (1, 1)),
            (where, near, illum, *came),
            (0, 1),
            ((2, 72, 1152),),
            smem_out=(2,),
        )
        above, below = up(high), down(low)
        shares = lax.all_to_all(chip, "tile", 0, 0)
        share, token = call(
            sum_kernel, ((9, 8, N), (1, 1)), (token, shares), (0,), smem_out=(1,)
        )
        probe_dir, df = call(
            share_kernel,
            ((16, 10, 8, N), (1, 2)),
            (share, *[along_y(share, s) for s in range(1, 4)], above, below, near_rows),
            (),
            smem_out=(1,),
            hbm_out=(0,),
            any_in=(4, 5),
        )
        gathered = lax.all_to_all(probe_dir, "tile", 0, 0)
        band, ae, r0, r1, r2, r3 = call(
            direction_kernel,
            ((2, 32, 1024), (1, 2)) + ((2, 2, 32, N),) * 4,
            (where, near, df, low, high, above, below),
            (0, 1, 2),
            ((2, 72, 1152),),
            smem_out=(1,),
            cheap=True,
        )
        bands.append([band] + [along_y(band, s) for s in range(1, 4)])
        back = [r0] + [along_y(r, s) for s, r in ((1, r1), (2, r2), (3, r3))]
        (oth,) = call(stack_kernel, ((4, 2, 32, N),), back, (), room=4, cheap=True)
        dirp, kept, sent_mixed = call(
            patch_kernel,
            ((2, N, N), (2, H, N), (2, H, N)),
            (where, near, *back, partner(oth), patch),
            (0, 1),
            ((2, 2, N, H),),
            cheap=True,
        )
        message, dmine = call(
            message_kernel,
            ((128, 128), (8, H, N)),
            (where, gathered, kept, partner(sent_mixed), ae, df),
            (0, 4, 5),
            hbm_out=(0,),
        )
        doth = partner(dmine)
        messages.append(lax.all_to_all(message, BOTH, 0, 0))
    (change,) = call(
        combine_kernel,
        ((4, 2, 32, 1024),),
        (*messages, *bands[0], *bands[1]),
        (),
        hbm_in={index: 1 for index in range(2, 10)},
        lazy=True,
    )
    change_far = partner(change)
    (probe_out,) = call(
        probe_kernel,
        (probe_init.shape,),
        (where, messages[1], probe, dmine, doth),
        (0,),
        hbm_in={2: 4},
        hbm_out={0: 4},
        lazy=True,
        flops=10**9,
    )
    (object_out,) = call(
        object_kernel,
        (object_init.shape,),
        (where, object_init, change, change_far),
        (0,),
        ((2, 8, N, H),),
        hbm_in={1: (4, 1)},
        hbm_out={0: (4, 1)},
        lazy=True,
        room=16,
    )
    return object_out, probe_out


def solution(mesh):
    placed = (P(("pat", "tile"), None, None), P(("pat", "tile"), None), P(None, "tile", None), P())
    return jax.shard_map(
        body, mesh=mesh, in_specs=placed, out_specs=(P(None, "tile", None), P()), check_vma=False
    )
```

```python
import math

import jax
import jax.numpy as jnp
import ml_dtypes
import numpy as np
from jax import lax
from jax.experimental import pallas as pl
from jax.experimental.pallas import tpu as pltpu
from jax.sharding import PartitionSpec as P

ITERS = 2
FLOOR = 0.5
RIDGE = 1.0
N = 256
H = 128
F32 = jnp.float32
BF16 = jnp.bfloat16
BOTH = ("pat", "tile")
VMEM = pl.BlockSpec(memory_space=pltpu.VMEM)
SMEM = pl.BlockSpec(memory_space=pltpu.SMEM)
ANY = pl.BlockSpec(memory_space=pl.ANY)


def real_tables():
    near = np.arange(H)[:, None]
    far = np.arange(H)[None, :]
    found = []
    for parity in range(2):
        angle = -2.0 * math.pi * ((near * (2 * far + parity)) % N) / N
        real, imag = np.cos(angle) / 16.0, np.sin(angle) / 16.0
        found.append(np.block([[real, imag], [-imag, real]]))
    even, odd = found
    out = []
    for table in (even, odd, even.T, odd.T):
        high = table.astype(np.float32).astype(ml_dtypes.bfloat16)
        low = (table - high.astype(np.float64)).astype(np.float32).astype(ml_dtypes.bfloat16)
        out.append(np.stack([high, low]))
    return np.stack(out)


def halves(value):
    high = value.astype(BF16)
    return high, (value - high.astype(F32)).astype(BF16)


def dot(left, right):
    return jnp.dot(left, right, preferred_element_type=F32)


def times_table(value, table):
    high, low = halves(value)
    both = dot(jnp.concatenate([high, low], axis=0), table[0])
    return both[:N] + (both[N:] + dot(high, table[1]))


def table_times(table, value):
    high, low = halves(value)
    both = dot(jnp.concatenate([table[0], table[1]], axis=0), high)
    return both[:N] + (both[N:] + dot(table[0], low))


def thirds(value):
    high, mid = halves(value)
    return high, mid, (value - high.astype(F32) - mid.astype(F32)).astype(BF16)


def step_sizes(everyone):
    total = jnp.sum(everyone[...], axis=0, keepdims=True)
    lane = lax.broadcasted_iota(jnp.int32, (1, 128), 1)
    object_power, cross_term, probe_power, object_pull, probe_pull = (
        jnp.broadcast_to(
            jnp.sum(jnp.where(lane == at, total, 0.0), axis=1, keepdims=True), (1, 128)
        )
        for at in range(5)
    )
    ridge = 0.1 * (object_power + probe_power) + 1e-06
    determinant = (object_power + ridge) * (probe_power + ridge) - cross_term * cross_term
    object_step = ((probe_power + ridge) * object_pull - cross_term * probe_pull) / determinant
    probe_step = ((object_power + ridge) * probe_pull - cross_term * object_pull) / determinant
    return object_step, probe_step


def twice(value):
    return jnp.concatenate([value, value], axis=1)


def joined(first_core, mine, other, plane):
    own, far = mine[plane], other[plane]
    return jnp.concatenate(
        [jnp.where(first_core, own, far), jnp.where(first_core, far, own)], axis=0
    )


def window_of(here):
    col = here[0, 1]
    block = pl.multiple_of(lax.min(lax.shift_right_logical(col, 7), 5) * H, H)
    return block, col - block


def cut(rows, e0, shift):
    rows = pltpu.roll(rows, lax.rem(2 * N - e0, N), axis=0)
    return pltpu.roll(rows, lax.rem(384 - shift, 384), axis=1)[:, :N]


def prepare_kernel(where, here, measured, swap, field, out, base, window, sem):
    e0 = here[0, 0] - where[3]
    block, shift = window_of(here)
    copy = pltpu.make_async_copy(field.at[:, :, pl.ds(block, 384)], window, sem)
    copy.start()
    high, mid, low = thirds(measured[...])
    across, down_rows = swap[0], swap[1]
    high, mid, low = thirds(dot(high, across) + dot(mid, across) + dot(low, across))
    value = dot(down_rows, high) + dot(down_rows, mid) + dot(down_rows, low)
    out[0] = value[:H]
    out[1] = value[H:]
    row = lax.broadcasted_iota(jnp.int32, (N, N), 0) + e0
    inside = (row >= H) & (row < H + N)
    copy.wait()
    for part in range(2):
        rows = jnp.concatenate([window[part, H:], window[part, :H]], axis=0)
        base[part] = jnp.where(inside, cut(rows, e0, shift), 0.0)


def edge_kernel(where, field, top_rows, low_rows, sems):
    c = where[1]
    copies = [
        pltpu.make_async_copy(field.at[c, pl.ds(0, H), :], top_rows, sems.at[0]),
        pltpu.make_async_copy(field.at[c, pl.ds(H, H), :], low_rows, sems.at[1]),
    ]
    for copy in copies:
        copy.start()
    for copy in copies:
        copy.wait()


def edges(where, field):
    rows = pltpu.VMEM((H, field.shape[2]), F32)
    return pl.pallas_call(
        edge_kernel,
        out_shape=[rows, rows],
        in_specs=[SMEM, ANY],
        out_specs=[VMEM, VMEM],
        scratch_shapes=[pltpu.SemaphoreType.DMA((2,))],
        compiler_params=pltpu.CompilerParams(vmem_limit_bytes=2 * 2**20),
    )(where, field)


def announce_kernel(here, out):
    lane = lax.broadcasted_iota(jnp.int32, (8, 128), 1)
    out[...] = jnp.where(lane == 0, here[0, 0], here[0, 1])


def side_kernel(where, near, base, above, below, own, far):
    y, c, top = where[0], where[1], where[3]
    own_row = near[2 * y + c, 0] - top
    far_row = near[2 * y + 1 - c, 0] - top
    own[...] = jnp.where(own_row < H, above[...], below[...])
    far[...] = jnp.where(far_row < H, above[...], below[...])


def add_side(where, here, base, own_side, far_side, patch):
    e0, first_core = here[0, 0] - where[3], where[1] == 0
    block, shift = window_of(here)
    row = lax.broadcasted_iota(jnp.int32, (N, N), 0) + e0
    outside = (row < H) | (row >= H + N)
    own, far = own_side[:, pl.ds(block, 384)], far_side[:, pl.ds(block, 384)]
    for part in range(2):
        rows = jnp.where(first_core == (part == 0), own, far)
        rows = cut(jnp.concatenate([rows, rows], axis=0), e0, shift)
        patch[part] = jnp.where(outside, rows, base[part])


def patterns_kernel(first, ready, leave, *refs):
    if first:
        where, here, base, own_side, far_side, probe_now, measured, tab = refs[:8]
        patch_now, keep, send, mine, other, power, near_rows, psi, model, obj = refs[8:]
        add_side(where, here, base, own_side, far_side, patch_now)
    else:
        where, here, everyone, patch, probe, measured, tab, dirp, dmine, doth = refs[:10]
        patch_now, probe_now = refs[13:15]
        keep, send, mine, other, power, near_rows, psi, model, obj = refs[15:]
        object_step, probe_step = map(twice, step_sizes(everyone))
        ready(3)
        ready(7)
        ready.more()
        for part in range(2):
            patch_now[part] = patch[part] + object_step * dirp[part]
        leave(0)
    y, c = where[0], where[1]
    e0 = here[0, 0] - where[3]
    first_core = c == 0
    rows_at = pl.multiple_of(H * c + 8 * where[2], 8)
    model[...] = jnp.zeros_like(model)
    obj[...] = jnp.zeros_like(obj)
    power[...] = jnp.zeros_like(power)

    def gather(plane, value):
        obj[plane, 0] += value[:, :H]
        obj[plane, 1] += value[:, H:]

    def forward(k):
        if first:
            ready(5, k)
        else:
            ready(4, k)
            for part in range(2):
                moved = probe_step * joined(first_core, dmine, doth, 2 * k + part)
                probe_now[k, part] = probe[k, part] + moved
            leave(1, k)
        pr, pi = probe_now[k, 0], probe_now[k, 1]
        orr, oi = patch_now[0], patch_now[1]
        power[...] += pr * pr + pi * pi
        for part in range(2):
            near_rows[2 * k + part] = probe_now[k, part, pl.ds(rows_at, 8), :]
        xr = pr * orr - pi * oi
        xi = pr * oi + pi * orr
        even = times_table(
            jnp.concatenate([xr[:, :H] + xr[:, H:], xi[:, :H] + xi[:, H:]], axis=1), tab.at[0]
        )
        odd = times_table(
            jnp.concatenate([xr[:, :H] - xr[:, H:], xi[:, :H] - xi[:, H:]], axis=1), tab.at[1]
        )
        re = jnp.concatenate([even[:, :H], odd[:, :H]], axis=1)
        im = jnp.concatenate([even[:, H:], odd[:, H:]], axis=1)
        for row, sign in ((0, 1.0), (1, -1.0)):
            folded = jnp.concatenate(
                [re[:H] + sign * re[H:], im[:H] + sign * im[H:]], axis=0
            )
            far = table_times(tab.at[2 + row], folded)
            psi[k, row] = far
            model[row] += far[:H] * far[:H] + far[H:] * far[H:]

    if not first:
        ready(6)
    for k in range(4):
        forward(k)
    if not first:
        ready(5)
    for row in range(2):
        model[row] = jnp.sqrt(measured[row] / jnp.maximum(model[row], FLOOR)) - 1.0

    def put(plane, value):
        low = value[:H].reshape(16, 8, N)
        high = value[H:].reshape(16, 8, N)
        keep[:, plane] = jnp.where(first_core, low, high)
        send[:, plane] = jnp.where(first_core, high, low)

    def backward(k):
        parts = []
        for row in range(2):
            scale = model[row]
            weighted = psi[k, row] * jnp.concatenate([scale, scale], axis=0)
            parts.append(table_times(tab.at[row], weighted))
        ee, oo = parts
        re = jnp.concatenate([ee[:H] + oo[:H], ee[:H] - oo[:H]], axis=0)
        im = jnp.concatenate([ee[H:] + oo[H:], ee[H:] - oo[H:]], axis=0)
        even = times_table(jnp.concatenate([re[:, :H], im[:, :H]], axis=1), tab.at[2])
        odd = times_table(jnp.concatenate([re[:, H:], im[:, H:]], axis=1), tab.at[3])
        dr = jnp.concatenate([even[:, :H] + odd[:, :H], even[:, :H] - odd[:, :H]], axis=1)
        di = jnp.concatenate([even[:, H:] + odd[:, H:], even[:, H:] - odd[:, H:]], axis=1)
        pr, pi = probe_now[k, 0], probe_now[k, 1]
        orr, oi = patch_now[0], patch_now[1]
        gather(0, pr * dr + pi * di)
        gather(1, pr * di - pi * dr)
        put(2 * k, orr * dr + oi * di)
        put(2 * k + 1, orr * di - oi * dr)

    for k in range(4):
        backward(k)
    orr, oi = patch_now[0], patch_now[1]
    put(8, orr * orr + oi * oi)
    for s in range(4):
        for which, dest in ((c, mine), (1 - c, other)):
            owner = 2 * lax.rem(y + s, 4) + which
            start = lax.rem(owner - e0 + 1024, 8)
            for plane in range(2):
                for half in range(2):
                    rows = obj[plane, half, pl.ds(start, 32, stride=8), :]
                    dest[s, plane, :, half * H : half * H + H] = rows


def place_of(where, places, owner, pattern):
    e0 = places[pattern, 0] - where[3]
    col = places[pattern, 1]
    start = lax.rem(owner - e0 + 1024, 8)
    row = lax.shift_right_logical(e0 + 256 + start - owner, 3)
    base = pl.multiple_of(lax.shift_right_logical(row, 3) * 8, 8)
    block = pl.multiple_of(lax.shift_right_logical(col, 7) * 128, 128)
    return start, base, lax.rem(row, 8), block, lax.rem(col, 128)


def place(acc, piece, base, turn, block, shift):
    wide = pltpu.roll(jnp.concatenate([piece, jnp.zeros((32, 128), F32)], axis=1), shift, axis=1)
    wide = pltpu.roll(jnp.concatenate([wide, jnp.zeros((8, 384), F32)], axis=0), turn, axis=0)
    acc[pl.ds(base, 40), pl.ds(block, 384)] += wide


def illum_kernel(where, near, total, out, power, acc):
    owner = 2 * where[0] + where[1]
    acc[...] = jnp.zeros_like(acc)
    power[0] = total[:, :H]
    power[1] = total[:, H:]
    for pattern in range(8):
        start, base, turn, block, shift = place_of(where, near, owner, pattern)
        rows = pl.ds(start, 32, stride=8)
        piece = jnp.concatenate([power[0, rows, :], power[1, rows, :]], axis=1)
        place(acc, piece, base - 32, turn, block, shift)
    out[...] = acc[:64, :1024]


def place_kernel(where, near, light, b0, b1, b2, b3, low, high, token, acc):
    token[0, 0] = 0.0
    y, c = where[0], where[1]
    owner = 2 * y + c
    acc[...] = jnp.zeros_like(acc)
    for s in range(4):
        for which in range(2):
            pattern = 2 * lax.rem(y - s + 4, 4) + (c if which == 0 else 1 - c)
            start, base, turn, block, shift = place_of(where, near, owner, pattern)
            for plane in range(2):
                piece = (b0, b1, b2, b3)[s][which, plane]
                place(acc.at[plane], piece, base - 32, turn, block, shift)
    low[:2] = acc[:, :32, :1024]
    high[:2] = acc[:, 32:64, :1024]
    low[2] = light[:32]
    high[2] = light[32:]


def direction_kernel(
    where, near, token, low, high, above, below, band, sums, r0, r1, r2, r3, wide
):
    y, c = where[0], where[1]
    owner = 2 * y + c
    wide[...] = jnp.zeros_like(wide)
    total_a = jnp.zeros((16, 1024), F32)
    total_n = jnp.zeros((16, 1024), F32)
    for at, (own, came) in enumerate(((low, above), (high, below))):
        rows = slice(32 * at, 32 * at + 32)
        inside = where[2] != 15 * at
        total = own[...] + jnp.where(inside, came[...], 0.0)
        light = total[2]
        scale = 1.0 / (light + RIDGE)
        real = total[0] * scale
        imag = total[1] * scale
        wide[0, rows, :1024] = real
        wide[1, rows, :1024] = imag
        inner = slice(16, 32) if at == 0 else slice(0, 16)
        real, imag, light = real[inner], imag[inner], light[inner]
        band[0, 16 * at : 16 * at + 16] = real
        band[1, 16 * at : 16 * at + 16] = imag
        size = real * real + imag * imag
        total_n += size
        total_a += light * size
    sums[0, 0] = jnp.sum(total_a)
    sums[0, 1] = jnp.sum(total_n)
    for s, dest in enumerate((r0, r1, r2, r3)):
        for which in range(2):
            pattern = 2 * lax.rem(y + s, 4) + (c if which == 0 else 1 - c)
            start, base, turn, block, shift = place_of(where, near, owner, pattern)
            for part in range(2):
                piece = wide[part, pl.ds(base - 32, 40), pl.ds(block, 384)]
                piece = pltpu.roll(piece, lax.rem(40 - turn, 40), axis=0)[:32]
                dest[which, part] = pltpu.roll(piece, lax.rem(384 - shift, 384), axis=1)[:, :N]


def stack_kernel(r0, r1, r2, r3, out):
    for s, came in enumerate((r0, r1, r2, r3)):
        out[s] = came[1]


def patch_kernel(where, near, r0, r1, r2, r3, oth, patch, dirp, kept, sent, lanes):
    y, c = where[0], where[1]
    e0 = near[2 * y + c, 0] - where[3]
    for s, came in enumerate((r0, r1, r2, r3)):
        for which in range(2):
            owner = 2 * lax.rem(y - s + 4, 4) + (c if which == 0 else 1 - c)
            rows = pl.ds(lax.rem(owner - e0 + 1024, 8), 32, stride=8)
            for part in range(2):
                piece = came[0, part] if which == 0 else oth[s, part]
                for half in range(2):
                    lanes[part, half, rows, :] = piece[:, half * H : half * H + H]
    for part in range(2):
        for half in range(2):
            dirp[part, :, half * H : half * H + H] = lanes[part, half]
    for which, dest in ((c, kept), (1 - c, sent)):
        rows = pl.ds(pl.multiple_of(which * H, H), H)
        dr, di = dirp[0, rows, :], dirp[1, rows, :]
        orr, oi = patch[0, rows, :], patch[1, rows, :]
        dest[0] = dr * orr + di * oi
        dest[1] = dr * oi - di * orr


def pack_kernel(ready, leave, keep, came, mine, part, chip, b0, b1, b2, b3):
    for piece in range(4):
        tiles = slice(4 * piece, 4 * piece + 4)
        chip[tiles] = keep[tiles] + came[tiles]
        leave(0, piece)
    for s, dest in enumerate((b0, b1, b2, b3)):
        dest[0] = mine[s]
        dest[1] = part[s]


def sum_kernel(before, shares, out, token):
    out[...] = jnp.sum(shares[...], axis=0)
    token[0, 0] = 0.0


def share_kernel(own, a, b, d, above, below, near_rows, spread_out, sums, block, sems):
    total = own[...] + a[...] + b[...] + d[...]
    illum = total[8]
    value = total[:8] * (1.0 / (illum + RIDGE))
    inner_real = jnp.zeros((8, N), F32)
    inner_imag = jnp.zeros((8, N), F32)
    for k in range(4):
        pr, pi = near_rows[2 * k], near_rows[2 * k + 1]
        inner_real += pr * value[2 * k] + pi * value[2 * k + 1]
        inner_imag += pr * value[2 * k + 1] - pi * value[2 * k]
    block[:8] = value
    block[8] = inner_real
    block[9] = inner_imag
    copies = [pltpu.make_async_copy(block, spread_out.at[i], sems.at[i]) for i in range(16)]
    for copy in copies:
        copy.start()
    size = jnp.sum(value * value, axis=0)
    sums[0, 0] = jnp.sum(size * illum)
    sums[0, 1] = jnp.sum(size)
    for copy in copies:
        copy.wait()


def message_kernel(where, gathered, kept, came, ae, df, out, planes):
    for plane in range(8):
        planes[plane] = gathered[:, plane].reshape(H, N)
    inner_real = gathered[:, 8].reshape(H, N)
    inner_imag = gathered[:, 9].reshape(H, N)
    cross = jnp.sum((kept[0] + came[0]) * inner_real - (kept[1] + came[1]) * inner_imag)
    d_sum = 0.25 * df[0, 0]
    values = (ae[0, 0], cross, d_sum, ae[0, 0] + ae[0, 1], d_sum + 0.25 * df[0, 1])
    lane = lax.broadcasted_iota(jnp.int32, (128, 128), 1)
    message = jnp.zeros((128, 128), F32)
    for at, value in enumerate(values):
        message = jnp.where(lane == at, value, message)
    out[...] = message


def combine_kernel(ready, leave, one, two, *refs):
    bands, out = refs[:8], refs[8]
    first = jnp.concatenate([step_sizes(one)[0]] * 8, axis=1)
    second = jnp.concatenate([step_sizes(two)[0]] * 8, axis=1)
    for s in range(4):
        ready(2 + s)
        ready(6 + s)
        for part in range(2):
            out[s, part] = first * bands[s][part] + second * bands[4 + s][part]


def probe_kernel(ready, leave, where, two, probe, dmine, doth, probe_out):
    probe_step = twice(step_sizes(two)[1])
    first_core = where[1] == 0
    for k in range(4):
        ready(2, k)
        for part in range(2):
            moved = probe_step * joined(first_core, dmine, doth, 2 * k + part)
            probe_out[k, part] = probe[k, part] + moved
        leave(0, k)


def object_kernel(ready, leave, where, field, mine, other, out, lanes):
    y, c = where[0], where[1]
    for block in range(4):
        ready(1, block)
        own = slice(8 * block, 8 * block + 8)
        for s in range(4):
            for which, change in ((c, mine), (1 - c, other)):
                owner = 2 * lax.rem(y - s + 4, 4) + which
                rows = pl.ds(64 * block + owner, 8, stride=8)
                for part in range(2):
                    moved = change[s, part, own]
                    for column in range(8):
                        lanes[part, column, rows, :] = moved[:, column * H : column * H + H]
        for part in range(2):
            rows = slice(64 * block, 64 * block + 64)
            for column in range(8):
                here = slice(column * H, column * H + H)
                out[part, rows, here] = field[part, rows, here] + lanes[part, column, rows]
        leave(0, block)


def call(
    kernel,
    outs,
    args,
    smem_in,
    scratch=(),
    smem_out=(),
    hbm_out=(),
    vmem_out=(),
    hbm_in=(),
    any_in=(),
    raw_out=(),
    lazy=False,
    staged_in=False,
    cheap=False,
    flops=0,
    room=12,
    name=None,
):
    outs = [out if isinstance(out[0], tuple) else (out, F32) for out in outs]
    shapes = [
        pltpu.HBM(*out)
        if i in hbm_out or i in raw_out
        else pltpu.VMEM(*out)
        if i in vmem_out
        else jax.ShapeDtypeStruct(*out)
        for i, out in enumerate(outs)
    ]
    hbm_in = hbm_in if isinstance(hbm_in, dict) else {index: 1 for index in hbm_in}
    hbm_out = hbm_out if isinstance(hbm_out, dict) else {index: 1 for index in hbm_out}
    moved = 4 * (sum(math.prod(out[0]) for out in outs) + sum(a.size for a in args))
    stage_in = [pltpu.VMEM(args[i].shape, args[i].dtype) for i in hbm_in]
    stage_out = [pltpu.VMEM(*outs[i]) for i in hbm_out]
    args = [
        pltpu.with_memory_space_constraint(a, pltpu.HBM) if i in hbm_in else a
        for i, a in enumerate(args)
    ]
    first, last = len(args), len(args) + len(outs)

    def cuts(ref, count):
        if count == 1:
            return [ref]
        count, axis = count if isinstance(count, tuple) else (count, 0)
        size = ref.shape[axis] // count
        return [
            ref.at[(slice(None),) * axis + (pl.ds(size * piece, size),)] for piece in range(count)
        ]

    def number(count):
        return count[0] if isinstance(count, tuple) else count

    def run(*refs):
        given, results = list(refs[:first]), list(refs[first:last])
        rest = refs[last:]
        staged = rest[len(scratch) : len(scratch) + len(stage_in) + len(stage_out)]
        sems = rest[-1] if staged else None
        arrivals, departures, at = {}, {}, 0
        for slot, (index, count) in enumerate(hbm_in.items()):
            stage, source = staged[slot], given[index]
            for piece, pair in enumerate(zip(cuts(source, count), cuts(stage, count))):
                copy = pltpu.make_async_copy(*pair, sems.at[at])
                if piece < 2 or not staged_in:
                    copy.start()
                arrivals[index, piece] = copy
                at += 1
            given[index] = stage
        for slot, (index, count) in enumerate(hbm_out.items()):
            stage = staged[len(stage_in) + slot]
            for piece, pair in enumerate(zip(cuts(stage, count), cuts(results[index], count))):
                departures[index, piece] = pltpu.make_async_copy(*pair, sems.at[at])
                at += 1
            results[index] = stage

        def ready(index, piece=0):
            arrivals[index, piece].wait()

        def more():
            for (index, piece), copy in arrivals.items():
                if piece >= 2:
                    copy.start()

        ready.more = more

        def leave(index, piece=0):
            departures[index, piece].start()

        if lazy:
            kernel(ready, leave, *given, *results, *rest[: len(scratch)])
        else:
            for copy in arrivals.values():
                copy.wait()
            kernel(*given, *results, *rest[: len(scratch)])
            for copy in departures.values():
                copy.start()
        for copy in departures.values():
            copy.wait()

    def space(index, smem, hbm):
        return SMEM if index in smem else ANY if index in hbm or index in any_in else VMEM

    extra = stage_in + stage_out
    if extra:
        count = sum(number(n) for n in (*hbm_in.values(), *hbm_out.values()))
        extra.append(pltpu.SemaphoreType.DMA((count,)))
    hbm = pl.BlockSpec(memory_space=pltpu.HBM)
    return pl.pallas_call(
        run,
        out_shape=shapes,
        in_specs=[space(i, smem_in, hbm_in) for i in range(len(args))],
        out_specs=[
            hbm if i in hbm_out or i in raw_out else SMEM if i in smem_out else VMEM for i in range(len(outs))
        ],
        scratch_shapes=[
            pltpu.VMEM(shape, F32)
            if isinstance(shape, tuple)
            else pltpu.SemaphoreType.DMA((shape,) if shape else ())
            for shape in scratch
        ]
        + extra,
        name=name or kernel.__name__,
        compiler_params=pltpu.CompilerParams(vmem_limit_bytes=room * 2**20),
        cost_estimate=pl.CostEstimate(
            flops=flops, bytes_accessed=0 if cheap else moved, transcendentals=0
        ),
    )(*args)


def along_y(value, s):
    return lax.ppermute(value, "pat", [(i, (i + 2 * s) % 8) for i in range(8)])


def partner(value):
    return lax.ppermute(value, "pat", [(i, i ^ 1) for i in range(8)])


def up(value):
    return lax.ppermute(value, "tile", [(i, (i + 1) % 16) for i in range(16)])


def down(value):
    return lax.ppermute(value, "tile", [((i + 1) % 16, i) for i in range(16)])


def spread(value, axes, count):
    return lax.all_to_all(jnp.broadcast_to(value[None], (count,) + value.shape), axes, 0, 0)


def one_hot():
    order = np.concatenate([np.arange(0, N, 2), np.arange(1, N, 2)])
    across = np.zeros((N, N), np.float32)
    across[order, np.arange(N)] = 1.0
    return np.stack([across, across.T]).astype(ml_dtypes.bfloat16)


def body(intensity, positions, object_init, probe_init):
    tile = lax.axis_index("tile")
    pat = lax.axis_index("pat")
    y, c = pat // 2, pat % 2
    top = tile * N - H
    where = jnp.stack([y, c, tile, top]).astype(jnp.int32)
    top_rows, low_rows = edges(where, pltpu.with_memory_space_constraint(object_init, pltpu.HBM))
    from_above, from_below = up(low_rows), down(top_rows)
    (news,) = call(announce_kernel, (((8, 128), jnp.int32),), (positions,), (0,), room=1)
    near = lax.all_to_all(news, "pat", 0, 0)
    table = jnp.asarray(real_tables())
    field = pltpu.with_memory_space_constraint(object_init, pltpu.HBM)
    measured, base = call(
        prepare_kernel,
        ((2, H, N), (2, N, N)),
        (where, positions, intensity[0], jnp.asarray(one_hot()), field),
        (0, 1),
        ((2, N, 384), None),
        any_in=(4,),
        room=8,
    )
    own_side, far_side = call(
        side_kernel,
        ((H, 1024), (H, 1024)),
        (where, near, base, from_above, from_below),
        (0, 1),
        any_in=(2,),
        room=4,
    )
    far_side = partner(far_side)

    probe = probe_init
    sent = (16, 9, 8, N)
    pieces = (4, 2, 32, N)
    scratch = ((4, 2, N, N), (2, H, N), (2, 2, N, H))
    outs = (sent, sent, pieces, pieces, (N, N), (8, 8, N))
    messages, bands = [], []

    for iteration in range(ITERS):
        if iteration == 0:
            patch, keep, send, mine, other, power, near_rows = call(
                lambda *refs: patterns_kernel(True, *refs),
                ((2, N, N),) + outs,
                (
                    where,
                    positions,
                    base,
                    own_side,
                    far_side,
                    probe,
                    measured,
                    table,
                ),
                (0, 1),
                scratch,
                hbm_in={5: 4},
                lazy=True,
                flops=6 * 10**9,
                room=28,
                name="patterns",
            )
        else:
            patch, probe, keep, send, mine, other, power, near_rows = call(
                lambda *refs: patterns_kernel(False, *refs),
                ((2, N, N), (4, 2, N, N)) + outs,
                (
                    where,
                    positions,
                    messages[-1],
                    patch,
                    probe,
                    measured,
                    table,
                    dirp,
                    dmine,
                    doth,
                    *bands[0][1:],
                ),
                (0, 1),
                scratch,
                hbm_in={3: 1, 7: 1, 6: 1, 4: 4, 5: 1},
                staged_in=True,
                lazy=True,
                hbm_out={0: 1, 1: 4},
                any_in=(10, 11, 12),
                flops=6 * 10**9,
                room=30,
                name="patterns",
            )
        chip, b0, b1, b2, b3 = call(
            pack_kernel,
            (sent,) + ((2, 2, 32, N),) * 4,
            (keep, partner(send), mine, partner(other)),
            (),
            hbm_out={0: 4},
            lazy=True,
        )
        came = [b0, along_y(b1, 1), along_y(b2, 2), along_y(b3, 3)]
        (illum,) = call(
            illum_kernel,
            ((64, 1024),),
            (where, near, power),
            (0, 1),
            ((2, N, H), (72, 1152)),
        )
        low, high, token = call(
            place_kernel,
            ((3, 32, 1024), (3, 32, 1024), (1, 1)),
            (where, near, illum, *came),
            (0, 1),
            ((2, 72, 1152),),
            smem_out=(2,),
        )
        above, below = up(high), down(low)
        shares = lax.all_to_all(chip, "tile", 0, 0)
        share, token = call(
            sum_kernel, ((9, 8, N), (1, 1)), (token, shares), (0,), smem_out=(1,)
        )
        probe_dir, df = call(
            share_kernel,
            ((16, 10, 8, N), (1, 2)),
            (share, *[along_y(share, s) for s in range(1, 4)], above, below, near_rows),
            (),
            ((10, 8, N), 16),
            smem_out=(1,),
            raw_out=(0,),
            any_in=(4, 5),
        )
        gathered = lax.all_to_all(probe_dir, "tile", 0, 0)
        band, ae, r0, r1, r2, r3 = call(
            direction_kernel,
            ((2, 32, 1024), (1, 2)) + ((2, 2, 32, N),) * 4,
            (where, near, df, low, high, above, below),
            (0, 1, 2),
            ((2, 72, 1152),),
            smem_out=(1,),
            cheap=True,
        )
        bands.append([band] + [along_y(band, s) for s in range(1, 4)])
        back = [r0] + [along_y(r, s) for s, r in ((1, r1), (2, r2), (3, r3))]
        (oth,) = call(stack_kernel, ((4, 2, 32, N),), back, (), room=4, cheap=True)
        dirp, kept, sent_mixed = call(
            patch_kernel,
            ((2, N, N), (2, H, N), (2, H, N)),
            (where, near, *back, partner(oth), patch),
            (0, 1),
            ((2, 2, N, H),),
            cheap=True,
        )
        message, dmine = call(
            message_kernel,
            ((128, 128), (8, H, N)),
            (where, gathered, kept, partner(sent_mixed), ae, df),
            (0, 4, 5),
            hbm_out=(0,),
        )
        doth = partner(dmine)
        messages.append(lax.all_to_all(message, BOTH, 0, 0))
    (change,) = call(
        combine_kernel,
        ((4, 2, 32, 1024),),
        (*messages, *bands[0], *bands[1]),
        (),
        hbm_in={index: 1 for index in range(2, 10)},
        lazy=True,
    )
    change_far = partner(change)
    (probe_out,) = call(
        probe_kernel,
        (probe_init.shape,),
        (where, messages[1], probe, dmine, doth),
        (0,),
        hbm_in={2: 4},
        hbm_out={0: 4},
        lazy=True,
        flops=10**9,
    )
    (object_out,) = call(
        object_kernel,
        (object_init.shape,),
        (where, object_init, change, change_far),
        (0,),
        ((2, 8, N, H),),
        hbm_in={1: (4, 1)},
        hbm_out={0: (4, 1)},
        lazy=True,
        room=16,
    )
    return object_out, probe_out


def solution(mesh):
    placed = (P(("pat", "tile"), None, None), P(("pat", "tile"), None), P(None, "tile", None), P())
    return jax.shard_map(
        body, mesh=mesh, in_specs=placed, out_specs=(P(None, "tile", None), P()), check_vma=False
    )
```

```python
import math

import jax
import jax.numpy as jnp
import ml_dtypes
import numpy as np
from jax import lax
from jax.experimental import pallas as pl
from jax.experimental.pallas import tpu as pltpu
from jax.sharding import PartitionSpec as P

ITERS = 2
FLOOR = 0.5
RIDGE = 1.0
N = 256
H = 128
F32 = jnp.float32
BF16 = jnp.bfloat16
BOTH = ("pat", "tile")
VMEM = pl.BlockSpec(memory_space=pltpu.VMEM)
SMEM = pl.BlockSpec(memory_space=pltpu.SMEM)
ANY = pl.BlockSpec(memory_space=pl.ANY)


def real_tables():
    near = np.arange(H)[:, None]
    far = np.arange(H)[None, :]
    found = []
    for parity in range(2):
        angle = -2.0 * math.pi * ((near * (2 * far + parity)) % N) / N
        real, imag = np.cos(angle) / 16.0, np.sin(angle) / 16.0
        found.append(np.block([[real, imag], [-imag, real]]))
    even, odd = found
    out = []
    for table in (even, odd, even.T, odd.T):
        high = table.astype(np.float32).astype(ml_dtypes.bfloat16)
        low = (table - high.astype(np.float64)).astype(np.float32).astype(ml_dtypes.bfloat16)
        out.append(np.stack([high, low]))
    return np.stack(out)


def halves(value):
    high = value.astype(BF16)
    return high, (value - high.astype(F32)).astype(BF16)


def dot(left, right):
    return jnp.dot(left, right, preferred_element_type=F32)


def times_table(value, table):
    high, low = halves(value)
    both = dot(jnp.concatenate([high, low], axis=0), table[0])
    return both[:N] + (both[N:] + dot(high, table[1]))


def table_times(table, value):
    high, low = halves(value)
    both = dot(jnp.concatenate([table[0], table[1]], axis=0), high)
    return both[:N] + (both[N:] + dot(table[0], low))


def thirds(value):
    high, mid = halves(value)
    return high, mid, (value - high.astype(F32) - mid.astype(F32)).astype(BF16)


def step_sizes(everyone):
    total = jnp.sum(everyone[...], axis=0, keepdims=True)
    lane = lax.broadcasted_iota(jnp.int32, (1, 128), 1)
    object_power, cross_term, probe_power, object_pull, probe_pull = (
        jnp.broadcast_to(
            jnp.sum(jnp.where(lane == at, total, 0.0), axis=1, keepdims=True), (1, 128)
        )
        for at in range(5)
    )
    ridge = 0.1 * (object_power + probe_power) + 1e-06
    determinant = (object_power + ridge) * (probe_power + ridge) - cross_term * cross_term
    object_step = ((probe_power + ridge) * object_pull - cross_term * probe_pull) / determinant
    probe_step = ((object_power + ridge) * probe_pull - cross_term * object_pull) / determinant
    return object_step, probe_step


def twice(value):
    return jnp.concatenate([value, value], axis=1)


def joined(first_core, mine, other, plane):
    own, far = mine[plane], other[plane]
    return jnp.concatenate(
        [jnp.where(first_core, own, far), jnp.where(first_core, far, own)], axis=0
    )


def window_of(here):
    col = here[0, 1]
    block = pl.multiple_of(lax.min(lax.shift_right_logical(col, 7), 5) * H, H)
    return block, col - block


def cut(rows, e0, shift):
    rows = pltpu.roll(rows, lax.rem(2 * N - e0, N), axis=0)
    return pltpu.roll(rows, lax.rem(384 - shift, 384), axis=1)[:, :N]


def prepare_kernel(where, here, measured, swap, field, out, base, window, sem):
    e0 = here[0, 0] - where[3]
    block, shift = window_of(here)
    copy = pltpu.make_async_copy(field.at[:, :, pl.ds(block, 384)], window, sem)
    copy.start()
    high, mid, low = thirds(measured[...])
    across, down_rows = swap[0], swap[1]
    high, mid, low = thirds(dot(high, across) + dot(mid, across) + dot(low, across))
    value = dot(down_rows, high) + dot(down_rows, mid) + dot(down_rows, low)
    out[0] = value[:H]
    out[1] = value[H:]
    row = lax.broadcasted_iota(jnp.int32, (N, N), 0) + e0
    inside = (row >= H) & (row < H + N)
    copy.wait()
    for part in range(2):
        rows = jnp.concatenate([window[part, H:], window[part, :H]], axis=0)
        base[part] = jnp.where(inside, cut(rows, e0, shift), 0.0)


def edge_kernel(where, field, top_rows, low_rows, sems):
    c = where[1]
    copies = [
        pltpu.make_async_copy(field.at[c, pl.ds(0, H), :], top_rows, sems.at[0]),
        pltpu.make_async_copy(field.at[c, pl.ds(H, H), :], low_rows, sems.at[1]),
    ]
    for copy in copies:
        copy.start()
    for copy in copies:
        copy.wait()


def edges(where, field):
    rows = pltpu.VMEM((H, field.shape[2]), F32)
    return pl.pallas_call(
        edge_kernel,
        out_shape=[rows, rows],
        in_specs=[SMEM, ANY],
        out_specs=[VMEM, VMEM],
        scratch_shapes=[pltpu.SemaphoreType.DMA((2,))],
        compiler_params=pltpu.CompilerParams(vmem_limit_bytes=2 * 2**20),
    )(where, field)


def announce_kernel(here, out):
    lane = lax.broadcasted_iota(jnp.int32, (8, 128), 1)
    out[...] = jnp.where(lane == 0, here[0, 0], here[0, 1])


def side_kernel(where, near, base, above, below, own, far):
    y, c, top = where[0], where[1], where[3]
    own_row = near[2 * y + c, 0] - top
    far_row = near[2 * y + 1 - c, 0] - top
    own[...] = jnp.where(own_row < H, above[...], below[...])
    far[...] = jnp.where(far_row < H, above[...], below[...])


def add_side(where, here, base, own_side, far_side, patch):
    e0, first_core = here[0, 0] - where[3], where[1] == 0
    block, shift = window_of(here)
    row = lax.broadcasted_iota(jnp.int32, (N, N), 0) + e0
    outside = (row < H) | (row >= H + N)
    own, far = own_side[:, pl.ds(block, 384)], far_side[:, pl.ds(block, 384)]
    for part in range(2):
        rows = jnp.where(first_core == (part == 0), own, far)
        rows = cut(jnp.concatenate([rows, rows], axis=0), e0, shift)
        patch[part] = jnp.where(outside, rows, base[part])


def patterns_kernel(first, ready, leave, *refs):
    if first:
        where, here, base, own_side, far_side, probe_now, measured, tab = refs[:8]
        patch_now, keep, send, mine, other, power, near_rows, psi, model, obj = refs[8:]
        add_side(where, here, base, own_side, far_side, patch_now)
    else:
        where, here, everyone, patch, probe, measured, tab, dirp, dmine, doth = refs[:10]
        patch_now, probe_now = refs[13:15]
        keep, send, mine, other, power, near_rows, psi, model, obj = refs[15:]
        object_step, probe_step = map(twice, step_sizes(everyone))
        ready(3)
        ready(7)
        ready.more()
        for part in range(2):
            patch_now[part] = patch[part] + object_step * dirp[part]
        leave(0)
    y, c = where[0], where[1]
    e0 = here[0, 0] - where[3]
    first_core = c == 0
    rows_at = pl.multiple_of(H * c + 8 * where[2], 8)
    model[...] = jnp.zeros_like(model)
    obj[...] = jnp.zeros_like(obj)
    power[...] = jnp.zeros_like(power)

    def gather(plane, value):
        obj[plane, 0, :N] += value[:, :H]
        obj[plane, 1, :N] += value[:, H:]

    def forward(k):
        if first:
            ready(5, k)
        else:
            ready(4, k)
            for part in range(2):
                moved = probe_step * joined(first_core, dmine, doth, 2 * k + part)
                probe_now[k, part] = probe[k, part] + moved
            leave(1, k)
        pr, pi = probe_now[k, 0], probe_now[k, 1]
        orr, oi = patch_now[0], patch_now[1]
        power[...] += pr * pr + pi * pi
        for part in range(2):
            near_rows[2 * k + part] = probe_now[k, part, pl.ds(rows_at, 8), :]
        xr = pr * orr - pi * oi
        xi = pr * oi + pi * orr
        even = times_table(
            jnp.concatenate([xr[:, :H] + xr[:, H:], xi[:, :H] + xi[:, H:]], axis=1), tab.at[0]
        )
        odd = times_table(
            jnp.concatenate([xr[:, :H] - xr[:, H:], xi[:, :H] - xi[:, H:]], axis=1), tab.at[1]
        )
        re = jnp.concatenate([even[:, :H], odd[:, :H]], axis=1)
        im = jnp.concatenate([even[:, H:], odd[:, H:]], axis=1)
        for row, sign in ((0, 1.0), (1, -1.0)):
            folded = jnp.concatenate(
                [re[:H] + sign * re[H:], im[:H] + sign * im[H:]], axis=0
            )
            far = table_times(tab.at[2 + row], folded)
            psi[k, row] = far
            model[row] += far[:H] * far[:H] + far[H:] * far[H:]

    if not first:
        ready(6)
    for k in range(4):
        forward(k)
    if not first:
        ready(5)
    for row in range(2):
        model[row] = jnp.sqrt(measured[row] / jnp.maximum(model[row], FLOOR)) - 1.0

    def put(plane, value):
        low = value[:H].reshape(16, 8, N)
        high = value[H:].reshape(16, 8, N)
        keep[:, plane] = jnp.where(first_core, low, high)
        send[:, plane] = jnp.where(first_core, high, low)

    def backward(k):
        parts = []
        for row in range(2):
            scale = model[row]
            weighted = psi[k, row] * jnp.concatenate([scale, scale], axis=0)
            parts.append(table_times(tab.at[row], weighted))
        ee, oo = parts
        re = jnp.concatenate([ee[:H] + oo[:H], ee[:H] - oo[:H]], axis=0)
        im = jnp.concatenate([ee[H:] + oo[H:], ee[H:] - oo[H:]], axis=0)
        even = times_table(jnp.concatenate([re[:, :H], im[:, :H]], axis=1), tab.at[2])
        odd = times_table(jnp.concatenate([re[:, H:], im[:, H:]], axis=1), tab.at[3])
        dr = jnp.concatenate([even[:, :H] + odd[:, :H], even[:, :H] - odd[:, :H]], axis=1)
        di = jnp.concatenate([even[:, H:] + odd[:, H:], even[:, H:] - odd[:, H:]], axis=1)
        pr, pi = probe_now[k, 0], probe_now[k, 1]
        orr, oi = patch_now[0], patch_now[1]
        gather(0, pr * dr + pi * di)
        gather(1, pr * di - pi * dr)
        put(2 * k, orr * dr + oi * di)
        put(2 * k + 1, orr * di - oi * dr)

    for k in range(4):
        backward(k)
    orr, oi = patch_now[0], patch_now[1]
    put(8, orr * orr + oi * oi)
    for s in range(4):
        for which, dest in ((c, mine), (1 - c, other)):
            owner = 2 * lax.rem(y + s, 4) + which
            start = lax.rem(owner - e0 + 1024, 8)
            for plane in range(2):
                for half in range(2):
                    rows = obj[plane, half, pl.ds(start, 32, stride=8), :]
                    dest[s, plane, :, half * H : half * H + H] = rows


def place_of(where, places, owner, pattern):
    e0 = places[pattern, 0] - where[3]
    col = places[pattern, 1]
    start = lax.rem(owner - e0 + 1024, 8)
    row = lax.shift_right_logical(e0 + 256 + start - owner, 3)
    base = pl.multiple_of(lax.shift_right_logical(row, 3) * 8, 8)
    block = pl.multiple_of(lax.shift_right_logical(col, 7) * 128, 128)
    return start, base, lax.rem(row, 8), block, lax.rem(col, 128)


def place(acc, piece, base, turn, block, shift):
    wide = pltpu.roll(jnp.concatenate([piece, jnp.zeros((32, 128), F32)], axis=1), shift, axis=1)
    wide = pltpu.roll(jnp.concatenate([wide, jnp.zeros((8, 384), F32)], axis=0), turn, axis=0)
    acc[pl.ds(base, 40), pl.ds(block, 384)] += wide


def illum_kernel(where, near, total, out, power, acc):
    owner = 2 * where[0] + where[1]
    acc[...] = jnp.zeros_like(acc)
    power[0, :N] = total[:, :H]
    power[1, :N] = total[:, H:]
    for pattern in range(8):
        start, base, turn, block, shift = place_of(where, near, owner, pattern)
        rows = pl.ds(start, 32, stride=8)
        piece = jnp.concatenate([power[0, rows, :], power[1, rows, :]], axis=1)
        place(acc, piece, base - 32, turn, block, shift)
    out[...] = acc[:64, :1024]


def place_kernel(where, near, light, b0, b1, b2, b3, low, high, token, acc):
    token[0, 0] = 0.0
    y, c = where[0], where[1]
    owner = 2 * y + c
    acc[...] = jnp.zeros_like(acc)
    for s in range(4):
        for which in range(2):
            pattern = 2 * lax.rem(y - s + 4, 4) + (c if which == 0 else 1 - c)
            start, base, turn, block, shift = place_of(where, near, owner, pattern)
            for plane in range(2):
                piece = (b0, b1, b2, b3)[s][which, plane]
                place(acc.at[plane], piece, base - 32, turn, block, shift)
    low[:2] = acc[:, :32, :1024]
    high[:2] = acc[:, 32:64, :1024]
    low[2] = light[:32]
    high[2] = light[32:]


def direction_kernel(
    where, near, token, low, high, above, below, band, sums, r0, r1, r2, r3, wide
):
    y, c = where[0], where[1]
    owner = 2 * y + c
    wide[...] = jnp.zeros_like(wide)
    total_a = jnp.zeros((16, 1024), F32)
    total_n = jnp.zeros((16, 1024), F32)
    for at, (own, came) in enumerate(((low, above), (high, below))):
        rows = slice(32 * at, 32 * at + 32)
        inside = where[2] != 15 * at
        total = own[...] + jnp.where(inside, came[...], 0.0)
        light = total[2]
        scale = 1.0 / (light + RIDGE)
        real = total[0] * scale
        imag = total[1] * scale
        wide[0, rows, :1024] = real
        wide[1, rows, :1024] = imag
        inner = slice(16, 32) if at == 0 else slice(0, 16)
        real, imag, light = real[inner], imag[inner], light[inner]
        band[0, 16 * at : 16 * at + 16] = real
        band[1, 16 * at : 16 * at + 16] = imag
        size = real * real + imag * imag
        total_n += size
        total_a += light * size
    sums[0, 0] = jnp.sum(total_a)
    sums[0, 1] = jnp.sum(total_n)
    for s, dest in enumerate((r0, r1, r2, r3)):
        for which in range(2):
            pattern = 2 * lax.rem(y + s, 4) + (c if which == 0 else 1 - c)
            start, base, turn, block, shift = place_of(where, near, owner, pattern)
            for part in range(2):
                piece = wide[part, pl.ds(base - 32, 40), pl.ds(block, 384)]
                piece = pltpu.roll(piece, lax.rem(40 - turn, 40), axis=0)[:32]
                dest[which, part] = pltpu.roll(piece, lax.rem(384 - shift, 384), axis=1)[:, :N]


def stack_kernel(r0, r1, r2, r3, out):
    for s, came in enumerate((r0, r1, r2, r3)):
        out[s] = came[1]


def patch_kernel(where, near, r0, r1, r2, r3, oth, patch, dirp, kept, sent, lanes):
    y, c = where[0], where[1]
    e0 = near[2 * y + c, 0] - where[3]
    for s, came in enumerate((r0, r1, r2, r3)):
        for which in range(2):
            owner = 2 * lax.rem(y - s + 4, 4) + (c if which == 0 else 1 - c)
            rows = pl.ds(lax.rem(owner - e0 + 1024, 8), 32, stride=8)
            for part in range(2):
                piece = came[0, part] if which == 0 else oth[s, part]
                for half in range(2):
                    lanes[part, half, rows, :] = piece[:, half * H : half * H + H]
    for part in range(2):
        for half in range(2):
            dirp[part, :, half * H : half * H + H] = lanes[part, half, :N]
    for which, dest in ((c, kept), (1 - c, sent)):
        rows = pl.ds(pl.multiple_of(which * H, H), H)
        dr, di = dirp[0, rows, :], dirp[1, rows, :]
        orr, oi = patch[0, rows, :], patch[1, rows, :]
        dest[0] = dr * orr + di * oi
        dest[1] = dr * oi - di * orr


def pack_kernel(ready, leave, keep, came, mine, part, chip, b0, b1, b2, b3):
    for piece in range(4):
        tiles = slice(4 * piece, 4 * piece + 4)
        chip[tiles] = keep[tiles] + came[tiles]
        leave(0, piece)
    for s, dest in enumerate((b0, b1, b2, b3)):
        dest[0] = mine[s]
        dest[1] = part[s]


def sum_kernel(before, shares, out, token):
    out[...] = jnp.sum(shares[...], axis=0)
    token[0, 0] = 0.0


def share_kernel(own, a, b, d, above, below, near_rows, spread_out, sums, block, sems):
    total = own[...] + a[...] + b[...] + d[...]
    illum = total[8]
    value = total[:8] * (1.0 / (illum + RIDGE))
    inner_real = jnp.zeros((8, N), F32)
    inner_imag = jnp.zeros((8, N), F32)
    for k in range(4):
        pr, pi = near_rows[2 * k], near_rows[2 * k + 1]
        inner_real += pr * value[2 * k] + pi * value[2 * k + 1]
        inner_imag += pr * value[2 * k + 1] - pi * value[2 * k]
    block[:8] = value
    block[8] = inner_real
    block[9] = inner_imag
    copies = [pltpu.make_async_copy(block, spread_out.at[i], sems.at[i]) for i in range(16)]
    for copy in copies:
        copy.start()
    size = jnp.sum(value * value, axis=0)
    sums[0, 0] = jnp.sum(size * illum)
    sums[0, 1] = jnp.sum(size)
    for copy in copies:
        copy.wait()


def message_kernel(where, gathered, kept, came, ae, df, out, planes):
    for plane in range(8):
        planes[plane] = gathered[:, plane].reshape(H, N)
    inner_real = gathered[:, 8].reshape(H, N)
    inner_imag = gathered[:, 9].reshape(H, N)
    cross = jnp.sum((kept[0] + came[0]) * inner_real - (kept[1] + came[1]) * inner_imag)
    d_sum = 0.25 * df[0, 0]
    values = (ae[0, 0], cross, d_sum, ae[0, 0] + ae[0, 1], d_sum + 0.25 * df[0, 1])
    lane = lax.broadcasted_iota(jnp.int32, (128, 128), 1)
    message = jnp.zeros((128, 128), F32)
    for at, value in enumerate(values):
        message = jnp.where(lane == at, value, message)
    out[...] = message


def combine_kernel(ready, leave, one, two, *refs):
    bands, out = refs[:8], refs[8]
    first = jnp.concatenate([step_sizes(one)[0]] * 8, axis=1)
    second = jnp.concatenate([step_sizes(two)[0]] * 8, axis=1)
    for s in range(4):
        ready(2 + s)
        ready(6 + s)
        for part in range(2):
            out[s, part] = first * bands[s][part] + second * bands[4 + s][part]


def probe_kernel(ready, leave, where, two, probe, dmine, doth, probe_out):
    probe_step = twice(step_sizes(two)[1])
    first_core = where[1] == 0
    for k in range(4):
        ready(2, k)
        for part in range(2):
            moved = probe_step * joined(first_core, dmine, doth, 2 * k + part)
            probe_out[k, part] = probe[k, part] + moved
        leave(0, k)


def object_kernel(ready, leave, where, field, mine, other, out, lanes):
    y, c = where[0], where[1]
    for block in range(4):
        ready(1, block)
        own = slice(8 * block, 8 * block + 8)
        for s in range(4):
            for which, change in ((c, mine), (1 - c, other)):
                owner = 2 * lax.rem(y - s + 4, 4) + which
                rows = pl.ds(64 * block + owner, 8, stride=8)
                for part in range(2):
                    moved = change[s, part, own]
                    for column in range(8):
                        lanes[part, column, rows, :] = moved[:, column * H : column * H + H]
        for part in range(2):
            rows = slice(64 * block, 64 * block + 64)
            for column in range(8):
                here = slice(column * H, column * H + H)
                out[part, rows, here] = field[part, rows, here] + lanes[part, column, rows]
        leave(0, block)


def call(
    kernel,
    outs,
    args,
    smem_in,
    scratch=(),
    smem_out=(),
    hbm_out=(),
    vmem_out=(),
    hbm_in=(),
    any_in=(),
    raw_out=(),
    lazy=False,
    staged_in=False,
    cheap=False,
    flops=0,
    room=12,
    name=None,
):
    outs = [out if isinstance(out[0], tuple) else (out, F32) for out in outs]
    shapes = [
        pltpu.HBM(*out)
        if i in hbm_out or i in raw_out
        else pltpu.VMEM(*out)
        if i in vmem_out
        else jax.ShapeDtypeStruct(*out)
        for i, out in enumerate(outs)
    ]
    hbm_in = hbm_in if isinstance(hbm_in, dict) else {index: 1 for index in hbm_in}
    hbm_out = hbm_out if isinstance(hbm_out, dict) else {index: 1 for index in hbm_out}
    moved = 4 * (sum(math.prod(out[0]) for out in outs) + sum(a.size for a in args))
    stage_in = [pltpu.VMEM(args[i].shape, args[i].dtype) for i in hbm_in]
    stage_out = [pltpu.VMEM(*outs[i]) for i in hbm_out]
    args = [
        pltpu.with_memory_space_constraint(a, pltpu.HBM) if i in hbm_in else a
        for i, a in enumerate(args)
    ]
    first, last = len(args), len(args) + len(outs)

    def cuts(ref, count):
        if count == 1:
            return [ref]
        count, axis = count if isinstance(count, tuple) else (count, 0)
        size = ref.shape[axis] // count
        return [
            ref.at[(slice(None),) * axis + (pl.ds(size * piece, size),)] for piece in range(count)
        ]

    def number(count):
        return count[0] if isinstance(count, tuple) else count

    def run(*refs):
        given, results = list(refs[:first]), list(refs[first:last])
        rest = refs[last:]
        staged = rest[len(scratch) : len(scratch) + len(stage_in) + len(stage_out)]
        sems = rest[-1] if staged else None
        arrivals, departures, at = {}, {}, 0
        for slot, (index, count) in enumerate(hbm_in.items()):
            stage, source = staged[slot], given[index]
            for piece, pair in enumerate(zip(cuts(source, count), cuts(stage, count))):
                copy = pltpu.make_async_copy(*pair, sems.at[at])
                if piece < 2 or not staged_in:
                    copy.start()
                arrivals[index, piece] = copy
                at += 1
            given[index] = stage
        for slot, (index, count) in enumerate(hbm_out.items()):
            stage = staged[len(stage_in) + slot]
            for piece, pair in enumerate(zip(cuts(stage, count), cuts(results[index], count))):
                departures[index, piece] = pltpu.make_async_copy(*pair, sems.at[at])
                at += 1
            results[index] = stage

        def ready(index, piece=0):
            arrivals[index, piece].wait()

        def more():
            for (index, piece), copy in arrivals.items():
                if piece >= 2:
                    copy.start()

        ready.more = more

        def leave(index, piece=0):
            departures[index, piece].start()

        if lazy:
            kernel(ready, leave, *given, *results, *rest[: len(scratch)])
        else:
            for copy in arrivals.values():
                copy.wait()
            kernel(*given, *results, *rest[: len(scratch)])
            for copy in departures.values():
                copy.start()
        for copy in departures.values():
            copy.wait()

    def space(index, smem, hbm):
        return SMEM if index in smem else ANY if index in hbm or index in any_in else VMEM

    extra = stage_in + stage_out
    if extra:
        count = sum(number(n) for n in (*hbm_in.values(), *hbm_out.values()))
        extra.append(pltpu.SemaphoreType.DMA((count,)))
    hbm = pl.BlockSpec(memory_space=pltpu.HBM)
    return pl.pallas_call(
        run,
        out_shape=shapes,
        in_specs=[space(i, smem_in, hbm_in) for i in range(len(args))],
        out_specs=[
            hbm if i in hbm_out or i in raw_out else SMEM if i in smem_out else VMEM for i in range(len(outs))
        ],
        scratch_shapes=[
            pltpu.VMEM(shape, F32)
            if isinstance(shape, tuple)
            else pltpu.SemaphoreType.DMA((shape,) if shape else ())
            for shape in scratch
        ]
        + extra,
        name=name or kernel.__name__,
        compiler_params=pltpu.CompilerParams(vmem_limit_bytes=room * 2**20),
        cost_estimate=pl.CostEstimate(
            flops=flops, bytes_accessed=0 if cheap else moved, transcendentals=0
        ),
    )(*args)


def along_y(value, s):
    return lax.ppermute(value, "pat", [(i, (i + 2 * s) % 8) for i in range(8)])


def partner(value):
    return lax.ppermute(value, "pat", [(i, i ^ 1) for i in range(8)])


def up(value):
    return lax.ppermute(value, "tile", [(i, (i + 1) % 16) for i in range(16)])


def down(value):
    return lax.ppermute(value, "tile", [((i + 1) % 16, i) for i in range(16)])


def spread(value, axes, count):
    return lax.all_to_all(jnp.broadcast_to(value[None], (count,) + value.shape), axes, 0, 0)


def one_hot():
    order = np.concatenate([np.arange(0, N, 2), np.arange(1, N, 2)])
    across = np.zeros((N, N), np.float32)
    across[order, np.arange(N)] = 1.0
    return np.stack([across, across.T]).astype(ml_dtypes.bfloat16)


def body(intensity, positions, object_init, probe_init):
    tile = lax.axis_index("tile")
    pat = lax.axis_index("pat")
    y, c = pat // 2, pat % 2
    top = tile * N - H
    where = jnp.stack([y, c, tile, top]).astype(jnp.int32)
    top_rows, low_rows = edges(where, pltpu.with_memory_space_constraint(object_init, pltpu.HBM))
    from_above, from_below = up(low_rows), down(top_rows)
    (news,) = call(announce_kernel, (((8, 128), jnp.int32),), (positions,), (0,), room=1)
    near = lax.all_to_all(news, "pat", 0, 0)
    table = jnp.asarray(real_tables())
    field = pltpu.with_memory_space_constraint(object_init, pltpu.HBM)
    measured, base = call(
        prepare_kernel,
        ((2, H, N), (2, N, N)),
        (where, positions, intensity[0], jnp.asarray(one_hot()), field),
        (0, 1),
        ((2, N, 384), None),
        any_in=(4,),
        room=8,
    )
    own_side, far_side = call(
        side_kernel,
        ((H, 1024), (H, 1024)),
        (where, near, base, from_above, from_below),
        (0, 1),
        any_in=(2,),
        room=4,
    )
    far_side = partner(far_side)

    probe = probe_init
    sent = (16, 9, 8, N)
    pieces = (4, 2, 32, N)
    scratch = ((4, 2, N, N), (2, H, N), (2, 2, N + 8, H))
    outs = (sent, sent, pieces, pieces, (N, N), (8, 8, N))
    messages, bands = [], []

    for iteration in range(ITERS):
        if iteration == 0:
            patch, keep, send, mine, other, power, near_rows = call(
                lambda *refs: patterns_kernel(True, *refs),
                ((2, N, N),) + outs,
                (
                    where,
                    positions,
                    base,
                    own_side,
                    far_side,
                    probe,
                    measured,
                    table,
                ),
                (0, 1),
                scratch,
                hbm_in={5: 4},
                lazy=True,
                flops=6 * 10**9,
                room=28,
                name="patterns",
            )
        else:
            patch, probe, keep, send, mine, other, power, near_rows = call(
                lambda *refs: patterns_kernel(False, *refs),
                ((2, N, N), (4, 2, N, N)) + outs,
                (
                    where,
                    positions,
                    messages[-1],
                    patch,
                    probe,
                    measured,
                    table,
                    dirp,
                    dmine,
                    doth,
                    *bands[0][1:],
                ),
                (0, 1),
                scratch,
                hbm_in={3: 1, 7: 1, 6: 1, 4: 4, 5: 1},
                staged_in=True,
                lazy=True,
                hbm_out={0: 1, 1: 4},
                any_in=(10, 11, 12),
                flops=6 * 10**9,
                room=30,
                name="patterns",
            )
        chip, b0, b1, b2, b3 = call(
            pack_kernel,
            (sent,) + ((2, 2, 32, N),) * 4,
            (keep, partner(send), mine, partner(other)),
            (),
            hbm_out={0: 4},
            lazy=True,
        )
        came = [b0, along_y(b1, 1), along_y(b2, 2), along_y(b3, 3)]
        (illum,) = call(
            illum_kernel,
            ((64, 1024),),
            (where, near, power),
            (0, 1),
            ((2, N + 8, H), (72, 1152)),
        )
        low, high, token = call(
            place_kernel,
            ((3, 32, 1024), (3, 32, 1024), (1, 1)),
            (where, near, illum, *came),
            (0, 1),
            ((2, 72, 1152),),
            smem_out=(2,),
        )
        above, below = up(high), down(low)
        shares = lax.all_to_all(chip, "tile", 0, 0)
        share, token = call(
            sum_kernel, ((9, 8, N), (1, 1)), (token, shares), (0,), smem_out=(1,)
        )
        probe_dir, df = call(
            share_kernel,
            ((16, 10, 8, N), (1, 2)),
            (share, *[along_y(share, s) for s in range(1, 4)], above, below, near_rows),
            (),
            ((10, 8, N), 16),
            smem_out=(1,),
            raw_out=(0,),
            any_in=(4, 5),
        )
        gathered = lax.all_to_all(probe_dir, "tile", 0, 0)
        band, ae, r0, r1, r2, r3 = call(
            direction_kernel,
            ((2, 32, 1024), (1, 2)) + ((2, 2, 32, N),) * 4,
            (where, near, df, low, high, above, below),
            (0, 1, 2),
            ((2, 72, 1152),),
            smem_out=(1,),
            cheap=True,
        )
        bands.append([band] + [along_y(band, s) for s in range(1, 4)])
        back = [r0] + [along_y(r, s) for s, r in ((1, r1), (2, r2), (3, r3))]
        (oth,) = call(stack_kernel, ((4, 2, 32, N),), back, (), room=4, cheap=True)
        dirp, kept, sent_mixed = call(
            patch_kernel,
            ((2, N, N), (2, H, N), (2, H, N)),
            (where, near, *back, partner(oth), patch),
            (0, 1),
            ((2, 2, N + 8, H),),
            cheap=True,
        )
        message, dmine = call(
            message_kernel,
            ((128, 128), (8, H, N)),
            (where, gathered, kept, partner(sent_mixed), ae, df),
            (0, 4, 5),
            hbm_out=(0,),
        )
        doth = partner(dmine)
        messages.append(lax.all_to_all(message, BOTH, 0, 0))
    (change,) = call(
        combine_kernel,
        ((4, 2, 32, 1024),),
        (*messages, *bands[0], *bands[1]),
        (),
        hbm_in={index: 1 for index in range(2, 10)},
        lazy=True,
    )
    change_far = partner(change)
    (probe_out,) = call(
        probe_kernel,
        (probe_init.shape,),
        (where, messages[1], probe, dmine, doth),
        (0,),
        hbm_in={2: 4},
        hbm_out={0: 4},
        lazy=True,
        flops=10**9,
    )
    (object_out,) = call(
        object_kernel,
        (object_init.shape,),
        (where, object_init, change, change_far),
        (0,),
        ((2, 8, N + 8, H),),
        hbm_in={1: (4, 1)},
        hbm_out={0: (4, 1)},
        lazy=True,
        room=16,
    )
    return object_out, probe_out


def solution(mesh):
    placed = (P(("pat", "tile"), None, None), P(("pat", "tile"), None), P(None, "tile", None), P())
    return jax.shard_map(
        body, mesh=mesh, in_specs=placed, out_specs=(P(None, "tile", None), P()), check_vma=False
    )
```

```python
import math

import jax
import jax.numpy as jnp
import ml_dtypes
import numpy as np
from jax import lax
from jax.experimental import pallas as pl
from jax.experimental.pallas import tpu as pltpu
from jax.sharding import PartitionSpec as P

ITERS = 2
FLOOR = 0.5
RIDGE = 1.0
N = 256
H = 128
F32 = jnp.float32
BF16 = jnp.bfloat16
BOTH = ("pat", "tile")
VMEM = pl.BlockSpec(memory_space=pltpu.VMEM)
SMEM = pl.BlockSpec(memory_space=pltpu.SMEM)
ANY = pl.BlockSpec(memory_space=pl.ANY)


def real_tables():
    near = np.arange(H)[:, None]
    far = np.arange(H)[None, :]
    found = []
    for parity in range(2):
        angle = -2.0 * math.pi * ((near * (2 * far + parity)) % N) / N
        real, imag = np.cos(angle) / 16.0, np.sin(angle) / 16.0
        found.append(np.block([[real, imag], [-imag, real]]))
    even, odd = found
    out = []
    for table in (even, odd, even.T, odd.T):
        high = table.astype(np.float32).astype(ml_dtypes.bfloat16)
        low = (table - high.astype(np.float64)).astype(np.float32).astype(ml_dtypes.bfloat16)
        out.append(np.stack([high, low]))
    return np.stack(out)


def halves(value):
    high = value.astype(BF16)
    return high, (value - high.astype(F32)).astype(BF16)


def dot(left, right):
    return jnp.dot(left, right, preferred_element_type=F32)


def times_table(value, table):
    high, low = halves(value)
    both = dot(jnp.concatenate([high, low], axis=0), table[0])
    return both[:N] + (both[N:] + dot(high, table[1]))


def table_times(table, value):
    high, low = halves(value)
    both = dot(jnp.concatenate([table[0], table[1]], axis=0), high)
    return both[:N] + (both[N:] + dot(table[0], low))


def thirds(value):
    high, mid = halves(value)
    return high, mid, (value - high.astype(F32) - mid.astype(F32)).astype(BF16)


def step_sizes(everyone):
    total = jnp.sum(everyone[...], axis=0, keepdims=True)
    lane = lax.broadcasted_iota(jnp.int32, (1, 128), 1)
    object_power, cross_term, probe_power, object_pull, probe_pull = (
        jnp.broadcast_to(
            jnp.sum(jnp.where(lane == at, total, 0.0), axis=1, keepdims=True), (1, 128)
        )
        for at in range(5)
    )
    ridge = 0.1 * (object_power + probe_power) + 1e-06
    determinant = (object_power + ridge) * (probe_power + ridge) - cross_term * cross_term
    object_step = ((probe_power + ridge) * object_pull - cross_term * probe_pull) / determinant
    probe_step = ((object_power + ridge) * probe_pull - cross_term * object_pull) / determinant
    return object_step, probe_step


def twice(value):
    return jnp.concatenate([value, value], axis=1)


def joined(first_core, mine, other, plane):
    own, far = mine[plane], other[plane]
    return jnp.concatenate(
        [jnp.where(first_core, own, far), jnp.where(first_core, far, own)], axis=0
    )


def window_of(here):
    col = here[0, 1]
    block = pl.multiple_of(lax.min(lax.shift_right_logical(col, 7), 5) * H, H)
    return block, col - block


def cut(rows, e0, shift):
    rows = pltpu.roll(rows, lax.rem(2 * N - e0, N), axis=0)
    return pltpu.roll(rows, lax.rem(384 - shift, 384), axis=1)[:, :N]


def prepare_kernel(where, here, measured, swap, field, out, base, window, sem):
    e0 = here[0, 0] - where[3]
    block, shift = window_of(here)
    copy = pltpu.make_async_copy(field.at[:, :, pl.ds(block, 384)], window, sem)
    copy.start()
    high, mid, low = thirds(measured[...])
    across, down_rows = swap[0], swap[1]
    high, mid, low = thirds(dot(high, across) + dot(mid, across) + dot(low, across))
    value = dot(down_rows, high) + dot(down_rows, mid) + dot(down_rows, low)
    out[0] = value[:H]
    out[1] = value[H:]
    row = lax.broadcasted_iota(jnp.int32, (N, N), 0) + e0
    inside = (row >= H) & (row < H + N)
    copy.wait()
    for part in range(2):
        rows = jnp.concatenate([window[part, H:], window[part, :H]], axis=0)
        base[part] = jnp.where(inside, cut(rows, e0, shift), 0.0)


def edge_kernel(where, field, top_rows, low_rows, sems):
    c = where[1]
    copies = [
        pltpu.make_async_copy(field.at[c, pl.ds(0, H), :], top_rows, sems.at[0]),
        pltpu.make_async_copy(field.at[c, pl.ds(H, H), :], low_rows, sems.at[1]),
    ]
    for copy in copies:
        copy.start()
    for copy in copies:
        copy.wait()


def edges(where, field):
    rows = pltpu.VMEM((H, field.shape[2]), F32)
    return pl.pallas_call(
        edge_kernel,
        out_shape=[rows, rows],
        in_specs=[SMEM, ANY],
        out_specs=[VMEM, VMEM],
        scratch_shapes=[pltpu.SemaphoreType.DMA((2,))],
        compiler_params=pltpu.CompilerParams(vmem_limit_bytes=2 * 2**20),
    )(where, field)


def announce_kernel(here, out):
    lane = lax.broadcasted_iota(jnp.int32, (8, 128), 1)
    out[...] = jnp.where(lane == 0, here[0, 0], here[0, 1])


def side_kernel(where, near, base, above, below, own, far):
    y, c, top = where[0], where[1], where[3]
    own_row = near[2 * y + c, 0] - top
    far_row = near[2 * y + 1 - c, 0] - top
    own[...] = jnp.where(own_row < H, above[...], below[...])
    far[...] = jnp.where(far_row < H, above[...], below[...])


def add_side(where, here, base, own_side, far_side, patch):
    e0, first_core = here[0, 0] - where[3], where[1] == 0
    block, shift = window_of(here)
    row = lax.broadcasted_iota(jnp.int32, (N, N), 0) + e0
    outside = (row < H) | (row >= H + N)
    own, far = own_side[:, pl.ds(block, 384)], far_side[:, pl.ds(block, 384)]
    for part in range(2):
        rows = jnp.where(first_core == (part == 0), own, far)
        rows = cut(jnp.concatenate([rows, rows], axis=0), e0, shift)
        patch[part] = jnp.where(outside, rows, base[part])


def patterns_kernel(first, ready, leave, *refs):
    if first:
        where, here, base, own_side, far_side, probe_now, measured, tab = refs[:8]
        patch_now, keep, send, mine, other, power, near_rows, psi, model, obj = refs[8:]
        add_side(where, here, base, own_side, far_side, patch_now)
    else:
        where, here, everyone, patch, probe, measured, tab, dirp, dmine, doth = refs[:10]
        patch_now, probe_now = refs[13:15]
        keep, send, mine, other, power, near_rows, psi, model, obj = refs[15:]
        object_step, probe_step = map(twice, step_sizes(everyone))
        ready(3)
        ready(7)
        ready.more()
        for part in range(2):
            patch_now[part] = patch[part] + object_step * dirp[part]
        leave(0)
    y, c = where[0], where[1]
    e0 = here[0, 0] - where[3]
    first_core = c == 0
    rows_at = pl.multiple_of(H * c + 8 * where[2], 8)

    def gather(k, plane, value):
        for half in range(2):
            part = value[:, half * H : half * H + H]
            obj[plane, half, :N] = part if k == 0 else obj[plane, half, :N] + part

    def forward(k):
        if first:
            ready(5, k)
        else:
            ready(4, k)
            for part in range(2):
                moved = probe_step * joined(first_core, dmine, doth, 2 * k + part)
                probe_now[k, part] = probe[k, part] + moved
            leave(1, k)
        pr, pi = probe_now[k, 0], probe_now[k, 1]
        orr, oi = patch_now[0], patch_now[1]
        size = pr * pr + pi * pi
        power[...] = size if k == 0 else power[...] + size
        for part in range(2):
            near_rows[2 * k + part] = probe_now[k, part, pl.ds(rows_at, 8), :]
        xr = pr * orr - pi * oi
        xi = pr * oi + pi * orr
        even = times_table(
            jnp.concatenate([xr[:, :H] + xr[:, H:], xi[:, :H] + xi[:, H:]], axis=1), tab.at[0]
        )
        odd = times_table(
            jnp.concatenate([xr[:, :H] - xr[:, H:], xi[:, :H] - xi[:, H:]], axis=1), tab.at[1]
        )
        re = jnp.concatenate([even[:, :H], odd[:, :H]], axis=1)
        im = jnp.concatenate([even[:, H:], odd[:, H:]], axis=1)
        for row, sign in ((0, 1.0), (1, -1.0)):
            folded = jnp.concatenate(
                [re[:H] + sign * re[H:], im[:H] + sign * im[H:]], axis=0
            )
            far = table_times(tab.at[2 + row], folded)
            psi[k, row] = far
            size = far[:H] * far[:H] + far[H:] * far[H:]
            model[row] = size if k == 0 else model[row] + size

    if not first:
        ready(6)
    for k in range(4):
        forward(k)
    if not first:
        ready(5)
    for row in range(2):
        model[row] = jnp.sqrt(measured[row] / jnp.maximum(model[row], FLOOR)) - 1.0

    def put(plane, value):
        low = value[:H].reshape(16, 8, N)
        high = value[H:].reshape(16, 8, N)
        keep[:, plane] = jnp.where(first_core, low, high)
        send[:, plane] = jnp.where(first_core, high, low)

    def backward(k):
        parts = []
        for row in range(2):
            scale = model[row]
            weighted = psi[k, row] * jnp.concatenate([scale, scale], axis=0)
            parts.append(table_times(tab.at[row], weighted))
        ee, oo = parts
        re = jnp.concatenate([ee[:H] + oo[:H], ee[:H] - oo[:H]], axis=0)
        im = jnp.concatenate([ee[H:] + oo[H:], ee[H:] - oo[H:]], axis=0)
        even = times_table(jnp.concatenate([re[:, :H], im[:, :H]], axis=1), tab.at[2])
        odd = times_table(jnp.concatenate([re[:, H:], im[:, H:]], axis=1), tab.at[3])
        dr = jnp.concatenate([even[:, :H] + odd[:, :H], even[:, :H] - odd[:, :H]], axis=1)
        di = jnp.concatenate([even[:, H:] + odd[:, H:], even[:, H:] - odd[:, H:]], axis=1)
        pr, pi = probe_now[k, 0], probe_now[k, 1]
        orr, oi = patch_now[0], patch_now[1]
        gather(k, 0, pr * dr + pi * di)
        gather(k, 1, pr * di - pi * dr)
        put(2 * k, orr * dr + oi * di)
        put(2 * k + 1, orr * di - oi * dr)

    for k in range(4):
        backward(k)
    orr, oi = patch_now[0], patch_now[1]
    put(8, orr * orr + oi * oi)
    for s in range(4):
        for which, dest in ((c, mine), (1 - c, other)):
            owner = 2 * lax.rem(y + s, 4) + which
            start = lax.rem(owner - e0 + 1024, 8)
            for plane in range(2):
                for half in range(2):
                    rows = obj[plane, half, pl.ds(start, 32, stride=8), :]
                    dest[s, plane, :, half * H : half * H + H] = rows


def place_of(where, places, owner, pattern):
    e0 = places[pattern, 0] - where[3]
    col = places[pattern, 1]
    start = lax.rem(owner - e0 + 1024, 8)
    row = lax.shift_right_logical(e0 + 256 + start - owner, 3)
    base = pl.multiple_of(lax.shift_right_logical(row, 3) * 8, 8)
    block = pl.multiple_of(lax.shift_right_logical(col, 7) * 128, 128)
    return start, base, lax.rem(row, 8), block, lax.rem(col, 128)


def place(acc, piece, base, turn, block, shift):
    wide = pltpu.roll(jnp.concatenate([piece, jnp.zeros((32, 128), F32)], axis=1), shift, axis=1)
    wide = pltpu.roll(jnp.concatenate([wide, jnp.zeros((8, 384), F32)], axis=0), turn, axis=0)
    acc[pl.ds(base, 40), pl.ds(block, 384)] += wide


def illum_kernel(where, near, total, out, power, acc):
    owner = 2 * where[0] + where[1]
    acc[...] = jnp.zeros_like(acc)
    power[0, :N] = total[:, :H]
    power[1, :N] = total[:, H:]
    for pattern in range(8):
        start, base, turn, block, shift = place_of(where, near, owner, pattern)
        rows = pl.ds(start, 32, stride=8)
        piece = jnp.concatenate([power[0, rows, :], power[1, rows, :]], axis=1)
        place(acc, piece, base - 32, turn, block, shift)
    out[...] = acc[:64, :1024]


def place_kernel(where, near, light, b0, b1, b2, b3, low, high, token, acc):
    token[0, 0] = 0.0
    y, c = where[0], where[1]
    owner = 2 * y + c
    acc[...] = jnp.zeros_like(acc)
    for s in range(4):
        for which in range(2):
            pattern = 2 * lax.rem(y - s + 4, 4) + (c if which == 0 else 1 - c)
            start, base, turn, block, shift = place_of(where, near, owner, pattern)
            for plane in range(2):
                piece = (b0, b1, b2, b3)[s][which, plane]
                place(acc.at[plane], piece, base - 32, turn, block, shift)
    low[:2] = acc[:, :32, :1024]
    high[:2] = acc[:, 32:64, :1024]
    low[2] = light[:32]
    high[2] = light[32:]


def direction_kernel(
    where, near, token, low, high, above, below, band, sums, r0, r1, r2, r3, wide
):
    y, c = where[0], where[1]
    owner = 2 * y + c
    wide[...] = jnp.zeros_like(wide)
    total_a = jnp.zeros((16, 1024), F32)
    total_n = jnp.zeros((16, 1024), F32)
    for at, (own, came) in enumerate(((low, above), (high, below))):
        rows = slice(32 * at, 32 * at + 32)
        inside = where[2] != 15 * at
        total = own[...] + jnp.where(inside, came[...], 0.0)
        light = total[2]
        scale = 1.0 / (light + RIDGE)
        real = total[0] * scale
        imag = total[1] * scale
        wide[0, rows, :1024] = real
        wide[1, rows, :1024] = imag
        inner = slice(16, 32) if at == 0 else slice(0, 16)
        real, imag, light = real[inner], imag[inner], light[inner]
        band[0, 16 * at : 16 * at + 16] = real
        band[1, 16 * at : 16 * at + 16] = imag
        size = real * real + imag * imag
        total_n += size
        total_a += light * size
    sums[0, 0] = jnp.sum(total_a)
    sums[0, 1] = jnp.sum(total_n)
    for s, dest in enumerate((r0, r1, r2, r3)):
        for which in range(2):
            pattern = 2 * lax.rem(y + s, 4) + (c if which == 0 else 1 - c)
            start, base, turn, block, shift = place_of(where, near, owner, pattern)
            for part in range(2):
                piece = wide[part, pl.ds(base - 32, 40), pl.ds(block, 384)]
                piece = pltpu.roll(piece, lax.rem(40 - turn, 40), axis=0)[:32]
                dest[which, part] = pltpu.roll(piece, lax.rem(384 - shift, 384), axis=1)[:, :N]


def stack_kernel(r0, r1, r2, r3, out):
    for s, came in enumerate((r0, r1, r2, r3)):
        out[s] = came[1]


def patch_kernel(where, near, r0, r1, r2, r3, oth, patch, dirp, kept, sent, lanes):
    y, c = where[0], where[1]
    e0 = near[2 * y + c, 0] - where[3]
    for s, came in enumerate((r0, r1, r2, r3)):
        for which in range(2):
            owner = 2 * lax.rem(y - s + 4, 4) + (c if which == 0 else 1 - c)
            rows = pl.ds(lax.rem(owner - e0 + 1024, 8), 32, stride=8)
            for part in range(2):
                piece = came[0, part] if which == 0 else oth[s, part]
                for half in range(2):
                    lanes[part, half, rows, :] = piece[:, half * H : half * H + H]
    for part in range(2):
        for half in range(2):
            dirp[part, :, half * H : half * H + H] = lanes[part, half, :N]
    for which, dest in ((c, kept), (1 - c, sent)):
        rows = pl.ds(pl.multiple_of(which * H, H), H)
        dr, di = dirp[0, rows, :], dirp[1, rows, :]
        orr, oi = patch[0, rows, :], patch[1, rows, :]
        dest[0] = dr * orr + di * oi
        dest[1] = dr * oi - di * orr


def pack_kernel(ready, leave, keep, came, mine, part, chip, b0, b1, b2, b3):
    for piece in range(4):
        tiles = slice(4 * piece, 4 * piece + 4)
        chip[tiles] = keep[tiles] + came[tiles]
        leave(0, piece)
    for s, dest in enumerate((b0, b1, b2, b3)):
        dest[0] = mine[s]
        dest[1] = part[s]


def last_patch_kernel(*refs):
    given, (kept, sent, lanes, dirp) = refs[:-4], refs[-4:]
    patch_kernel(*given, dirp, kept, sent, lanes)


def sum_kernel(before, shares, out, token):
    out[...] = jnp.sum(shares[...], axis=0)
    token[0, 0] = 0.0


def share_kernel(own, a, b, d, above, below, near_rows, spread_out, sums, block, sems):
    total = own[...] + a[...] + b[...] + d[...]
    illum = total[8]
    value = total[:8] * (1.0 / (illum + RIDGE))
    inner_real = jnp.zeros((8, N), F32)
    inner_imag = jnp.zeros((8, N), F32)
    for k in range(4):
        pr, pi = near_rows[2 * k], near_rows[2 * k + 1]
        inner_real += pr * value[2 * k] + pi * value[2 * k + 1]
        inner_imag += pr * value[2 * k + 1] - pi * value[2 * k]
    block[:8] = value
    block[8] = inner_real
    block[9] = inner_imag
    copies = [pltpu.make_async_copy(block, spread_out.at[i], sems.at[i]) for i in range(16)]
    for copy in copies:
        copy.start()
    size = jnp.sum(value * value, axis=0)
    sums[0, 0] = jnp.sum(size * illum)
    sums[0, 1] = jnp.sum(size)
    for copy in copies:
        copy.wait()


def message_kernel(where, gathered, kept, came, ae, df, out, planes):
    for plane in range(8):
        planes[plane] = gathered[:, plane].reshape(H, N)
    inner_real = gathered[:, 8].reshape(H, N)
    inner_imag = gathered[:, 9].reshape(H, N)
    cross = jnp.sum((kept[0] + came[0]) * inner_real - (kept[1] + came[1]) * inner_imag)
    d_sum = 0.25 * df[0, 0]
    values = (ae[0, 0], cross, d_sum, ae[0, 0] + ae[0, 1], d_sum + 0.25 * df[0, 1])
    lane = lax.broadcasted_iota(jnp.int32, (128, 128), 1)
    message = jnp.zeros((128, 128), F32)
    for at, value in enumerate(values):
        message = jnp.where(lane == at, value, message)
    out[...] = message


def combine_kernel(ready, leave, one, two, *refs):
    bands, out = refs[:8], refs[8]
    first = jnp.concatenate([step_sizes(one)[0]] * 8, axis=1)
    second = jnp.concatenate([step_sizes(two)[0]] * 8, axis=1)
    for s in range(4):
        ready(2 + s)
        ready(6 + s)
        for part in range(2):
            out[s, part] = first * bands[s][part] + second * bands[4 + s][part]


def probe_kernel(ready, leave, where, two, probe, dmine, doth, probe_out):
    probe_step = twice(step_sizes(two)[1])
    first_core = where[1] == 0
    for k in range(4):
        ready(2, k)
        for part in range(2):
            moved = probe_step * joined(first_core, dmine, doth, 2 * k + part)
            probe_out[k, part] = probe[k, part] + moved
        leave(0, k)


def object_kernel(ready, leave, where, field, mine, other, out, lanes):
    y, c = where[0], where[1]
    for block in range(4):
        ready(1, block)
        own = slice(8 * block, 8 * block + 8)
        for s in range(4):
            for which, change in ((c, mine), (1 - c, other)):
                owner = 2 * lax.rem(y - s + 4, 4) + which
                rows = pl.ds(64 * block + owner, 8, stride=8)
                for part in range(2):
                    moved = change[s, part, own]
                    for column in range(8):
                        lanes[part, column, rows, :] = moved[:, column * H : column * H + H]
        for part in range(2):
            rows = slice(64 * block, 64 * block + 64)
            for column in range(8):
                here = slice(column * H, column * H + H)
                out[part, rows, here] = field[part, rows, here] + lanes[part, column, rows]
        leave(0, block)


def call(
    kernel,
    outs,
    args,
    smem_in,
    scratch=(),
    smem_out=(),
    hbm_out=(),
    vmem_out=(),
    hbm_in=(),
    any_in=(),
    raw_out=(),
    lazy=False,
    staged_in=False,
    cheap=False,
    flops=0,
    room=12,
    name=None,
):
    outs = [out if isinstance(out[0], tuple) else (out, F32) for out in outs]
    shapes = [
        pltpu.HBM(*out)
        if i in hbm_out or i in raw_out
        else pltpu.VMEM(*out)
        if i in vmem_out
        else jax.ShapeDtypeStruct(*out)
        for i, out in enumerate(outs)
    ]
    hbm_in = hbm_in if isinstance(hbm_in, dict) else {index: 1 for index in hbm_in}
    hbm_out = hbm_out if isinstance(hbm_out, dict) else {index: 1 for index in hbm_out}
    moved = 4 * (sum(math.prod(out[0]) for out in outs) + sum(a.size for a in args))
    stage_in = [pltpu.VMEM(args[i].shape, args[i].dtype) for i in hbm_in]
    stage_out = [pltpu.VMEM(*outs[i]) for i in hbm_out]
    args = [
        pltpu.with_memory_space_constraint(a, pltpu.HBM) if i in hbm_in else a
        for i, a in enumerate(args)
    ]
    first, last = len(args), len(args) + len(outs)

    def cuts(ref, count):
        if count == 1:
            return [ref]
        count, axis = count if isinstance(count, tuple) else (count, 0)
        size = ref.shape[axis] // count
        return [
            ref.at[(slice(None),) * axis + (pl.ds(size * piece, size),)] for piece in range(count)
        ]

    def number(count):
        return count[0] if isinstance(count, tuple) else count

    def run(*refs):
        given, results = list(refs[:first]), list(refs[first:last])
        rest = refs[last:]
        staged = rest[len(scratch) : len(scratch) + len(stage_in) + len(stage_out)]
        sems = rest[-1] if staged else None
        arrivals, departures, at = {}, {}, 0
        for slot, (index, count) in enumerate(hbm_in.items()):
            stage, source = staged[slot], given[index]
            for piece, pair in enumerate(zip(cuts(source, count), cuts(stage, count))):
                copy = pltpu.make_async_copy(*pair, sems.at[at])
                if piece < 2 or not staged_in:
                    copy.start()
                arrivals[index, piece] = copy
                at += 1
            given[index] = stage
        for slot, (index, count) in enumerate(hbm_out.items()):
            stage = staged[len(stage_in) + slot]
            for piece, pair in enumerate(zip(cuts(stage, count), cuts(results[index], count))):
                departures[index, piece] = pltpu.make_async_copy(*pair, sems.at[at])
                at += 1
            results[index] = stage

        def ready(index, piece=0):
            arrivals[index, piece].wait()

        def more():
            for (index, piece), copy in arrivals.items():
                if piece >= 2:
                    copy.start()

        ready.more = more

        def leave(index, piece=0):
            departures[index, piece].start()

        if lazy:
            kernel(ready, leave, *given, *results, *rest[: len(scratch)])
        else:
            for copy in arrivals.values():
                copy.wait()
            kernel(*given, *results, *rest[: len(scratch)])
            for copy in departures.values():
                copy.start()
        for copy in departures.values():
            copy.wait()

    def space(index, smem, hbm):
        return SMEM if index in smem else ANY if index in hbm or index in any_in else VMEM

    extra = stage_in + stage_out
    if extra:
        count = sum(number(n) for n in (*hbm_in.values(), *hbm_out.values()))
        extra.append(pltpu.SemaphoreType.DMA((count,)))
    hbm = pl.BlockSpec(memory_space=pltpu.HBM)
    return pl.pallas_call(
        run,
        out_shape=shapes,
        in_specs=[space(i, smem_in, hbm_in) for i in range(len(args))],
        out_specs=[
            hbm if i in hbm_out or i in raw_out else SMEM if i in smem_out else VMEM for i in range(len(outs))
        ],
        scratch_shapes=[
            pltpu.VMEM(shape, F32)
            if isinstance(shape, tuple)
            else pltpu.SemaphoreType.DMA((shape,) if shape else ())
            for shape in scratch
        ]
        + extra,
        name=name or kernel.__name__,
        compiler_params=pltpu.CompilerParams(vmem_limit_bytes=room * 2**20),
        cost_estimate=pl.CostEstimate(
            flops=flops, bytes_accessed=0 if cheap else moved, transcendentals=0
        ),
    )(*args)


def along_y(value, s):
    return lax.ppermute(value, "pat", [(i, (i + 2 * s) % 8) for i in range(8)])


def partner(value):
    return lax.ppermute(value, "pat", [(i, i ^ 1) for i in range(8)])


def up(value):
    return lax.ppermute(value, "tile", [(i, (i + 1) % 16) for i in range(16)])


def down(value):
    return lax.ppermute(value, "tile", [((i + 1) % 16, i) for i in range(16)])


def spread(value, axes, count):
    return lax.all_to_all(jnp.broadcast_to(value[None], (count,) + value.shape), axes, 0, 0)


def one_hot():
    order = np.concatenate([np.arange(0, N, 2), np.arange(1, N, 2)])
    across = np.zeros((N, N), np.float32)
    across[order, np.arange(N)] = 1.0
    return np.stack([across, across.T]).astype(ml_dtypes.bfloat16)


def body(intensity, positions, object_init, probe_init):
    tile = lax.axis_index("tile")
    pat = lax.axis_index("pat")
    y, c = pat // 2, pat % 2
    top = tile * N - H
    where = jnp.stack([y, c, tile, top]).astype(jnp.int32)
    top_rows, low_rows = edges(where, pltpu.with_memory_space_constraint(object_init, pltpu.HBM))
    from_above, from_below = up(low_rows), down(top_rows)
    (news,) = call(announce_kernel, (((8, 128), jnp.int32),), (positions,), (0,), room=1)
    near = lax.all_to_all(news, "pat", 0, 0)
    table = jnp.asarray(real_tables())
    field = pltpu.with_memory_space_constraint(object_init, pltpu.HBM)
    measured, base = call(
        prepare_kernel,
        ((2, H, N), (2, N, N)),
        (where, positions, intensity[0], jnp.asarray(one_hot()), field),
        (0, 1),
        ((2, N, 384), None),
        any_in=(4,),
        room=8,
    )
    own_side, far_side = call(
        side_kernel,
        ((H, 1024), (H, 1024)),
        (where, near, base, from_above, from_below),
        (0, 1),
        any_in=(2,),
        room=4,
    )
    far_side = partner(far_side)

    probe = probe_init
    sent = (16, 9, 8, N)
    pieces = (4, 2, 32, N)
    scratch = ((4, 2, N, N), (2, H, N), (2, 2, N + 8, H))
    outs = (sent, sent, pieces, pieces, (N, N), (8, 8, N))
    messages, bands = [], []

    for iteration in range(ITERS):
        if iteration == 0:
            patch, keep, send, mine, other, power, near_rows = call(
                lambda *refs: patterns_kernel(True, *refs),
                ((2, N, N),) + outs,
                (
                    where,
                    positions,
                    base,
                    own_side,
                    far_side,
                    probe,
                    measured,
                    table,
                ),
                (0, 1),
                scratch,
                hbm_in={5: 4},
                lazy=True,
                flops=6 * 10**9,
                room=28,
                name="patterns",
            )
        else:
            patch, probe, keep, send, mine, other, power, near_rows = call(
                lambda *refs: patterns_kernel(False, *refs),
                ((2, N, N), (4, 2, N, N)) + outs,
                (
                    where,
                    positions,
                    messages[-1],
                    patch,
                    probe,
                    measured,
                    table,
                    dirp,
                    dmine,
                    doth,
                    *bands[0][1:],
                ),
                (0, 1),
                scratch,
                hbm_in={3: 1, 7: 1, 6: 1, 4: 4, 5: 1},
                staged_in=True,
                lazy=True,
                hbm_out={0: 1, 1: 4},
                any_in=(10, 11, 12),
                flops=6 * 10**9,
                room=30,
                name="patterns",
            )
        chip, b0, b1, b2, b3 = call(
            pack_kernel,
            (sent,) + ((2, 2, 32, N),) * 4,
            (keep, partner(send), mine, partner(other)),
            (),
            hbm_out={0: 4},
            lazy=True,
        )
        came = [b0, along_y(b1, 1), along_y(b2, 2), along_y(b3, 3)]
        (illum,) = call(
            illum_kernel,
            ((64, 1024),),
            (where, near, power),
            (0, 1),
            ((2, N + 8, H), (72, 1152)),
        )
        low, high, token = call(
            place_kernel,
            ((3, 32, 1024), (3, 32, 1024), (1, 1)),
            (where, near, illum, *came),
            (0, 1),
            ((2, 72, 1152),),
            smem_out=(2,),
        )
        above, below = up(high), down(low)
        shares = lax.all_to_all(chip, "tile", 0, 0)
        share, token = call(
            sum_kernel, ((9, 8, N), (1, 1)), (token, shares), (0,), smem_out=(1,)
        )
        probe_dir, df = call(
            share_kernel,
            ((16, 10, 8, N), (1, 2)),
            (share, *[along_y(share, s) for s in range(1, 4)], above, below, near_rows),
            (),
            ((10, 8, N), 16),
            smem_out=(1,),
            raw_out=(0,),
            any_in=(4, 5),
        )
        gathered = lax.all_to_all(probe_dir, "tile", 0, 0)
        band, ae, r0, r1, r2, r3 = call(
            direction_kernel,
            ((2, 32, 1024), (1, 2)) + ((2, 2, 32, N),) * 4,
            (where, near, df, low, high, above, below),
            (0, 1, 2),
            ((2, 72, 1152),),
            smem_out=(1,),
            cheap=True,
        )
        bands.append([band] + [along_y(band, s) for s in range(1, 4)])
        back = [r0] + [along_y(r, s) for s, r in ((1, r1), (2, r2), (3, r3))]
        (oth,) = call(stack_kernel, ((4, 2, 32, N),), back, (), room=4, cheap=True)
        last = iteration == ITERS - 1
        halves_out = ((2, H, N), (2, H, N))
        *dirps, kept, sent_mixed = call(
            last_patch_kernel if last else patch_kernel,
            halves_out if last else ((2, N, N),) + halves_out,
            (where, near, *back, partner(oth), patch),
            (0, 1),
            ((2, 2, N + 8, H),) + (((2, N, N),) if last else ()),
            cheap=True,
        )
        dirp = dirps[0] if dirps else None
        message, dmine = call(
            message_kernel,
            ((128, 128), (8, H, N)),
            (where, gathered, kept, partner(sent_mixed), ae, df),
            (0, 4, 5),
            hbm_out=(0,),
        )
        doth = partner(dmine)
        messages.append(lax.all_to_all(message, BOTH, 0, 0))
    (change,) = call(
        combine_kernel,
        ((4, 2, 32, 1024),),
        (*messages, *bands[0], *bands[1]),
        (),
        hbm_in={index: 1 for index in range(2, 10)},
        lazy=True,
    )
    change_far = partner(change)
    (probe_out,) = call(
        probe_kernel,
        (probe_init.shape,),
        (where, messages[1], probe, dmine, doth),
        (0,),
        hbm_in={2: 4},
        hbm_out={0: 4},
        lazy=True,
        flops=10**9,
    )
    (object_out,) = call(
        object_kernel,
        (object_init.shape,),
        (where, object_init, change, change_far),
        (0,),
        ((2, 8, N + 8, H),),
        hbm_in={1: (4, 1)},
        hbm_out={0: (4, 1)},
        lazy=True,
        room=16,
    )
    return object_out, probe_out


def solution(mesh):
    placed = (P(("pat", "tile"), None, None), P(("pat", "tile"), None), P(None, "tile", None), P())
    return jax.shard_map(
        body, mesh=mesh, in_specs=placed, out_specs=(P(None, "tile", None), P()), check_vma=False
    )
```
